32 devices in a mesh: groups: 2 (over x), wide: 16 (over z, y, core).
Axes of the slice: x: 2, y: 2, z: 4, core: 2. Of those that a mesh axis runs over, the one named last changes fastest.
Arguments:
- charges: bfloat16 [16, 131072], P(None, ('groups', 'wide')), parts along dimension 1, may hold values from -6 to 6
- cell_offset: float32 [3, 131072], P(None, ('groups', 'wide')), parts along dimension 1, may hold values from 0 to 1
- base_cell: int32 [3, 131072], P(None, ('groups', 'wide')), parts along dimension 1, may hold values from 0 to 127, as said below
- counts: int32 [512], P(('groups', 'wide')), parts along dimension 0, may hold values from 128 to 256, as said below
- widths: float32 [16], replicated, may hold values from 0.75 to 2
Outputs:
- atom_potential: float32 [16, 131072], P(None, ('groups', 'wide')), parts along dimension 1
- forces: float32 [3, 131072], P(None, ('groups', 'wide')), parts along dimension 1
The draws below stay inside these ranges and needn't reach their ends.
There are 2 independent parts, one for each index of `groups`. The reference program is written for one: setup_inputs(seed, part) draws one part's arguments, and reference() takes and returns one part's arrays. A program takes and returns all parts, laid end to end along the dimension named above; an argument that names none is the same for every part. Nothing has to cross between parts.
Inputs may be any that keep to these rules, and one draw needn't show every extreme that they name: For slot s on index i of wide (s // 4096 = i) in block b = (s // 256) mod 16: base_cell[0, s] lies in [i * 8, (i + 1) * 8), base_cell[1, s] in [b * 8, (b + 1) * 8), base_cell[2, s] in [0, 128). `counts`: each index of wide has a block whose 256 slots are all live.
All inputs are finite; a program needn't handle non-finite values.
Results may differ from the reference program's by a relative error of at most 0.002.
The reference program's roundings to bfloat16 on the way count: a program that leaves them out, or rounds other values in their place, can miss the bound.
Values may be sent and summed in bfloat16 or wider, within the bound.
No kernel may reach another device: no remote copies, remote signals or barrier semaphores. Data moves between devices by JAX's collectives and lax.ppermute only.
A program may use at most 128 MiB of HBM per device.

```python
import math
import jax
import jax.numpy as jnp
from jax import lax

CH = 16
MESH_X = 128
MESH_Y = 128
MESH_Z = 128
ORDER = 6
BLOCK_ROWS = 8
CAP = 256
PLANES = 8
NBLK = 16
SLOTS = 65536
N_WIDE = 16


def draw_base_cell(key, part):
    key = jax.random.fold_in(key, 11)
    slot_ids = jnp.arange(SLOTS, dtype=jnp.int32)
    device = slot_ids // (NBLK * CAP)
    block_id = slot_ids // CAP % NBLK
    subkeys = jax.random.split(key, 3)
    x_plane = device * PLANES + jax.random.randint(subkeys[0], (SLOTS,), 0, PLANES, dtype=jnp.int32)
    y_row = block_id * BLOCK_ROWS + jax.random.randint(subkeys[1], (SLOTS,), 0, BLOCK_ROWS, dtype=jnp.int32)
    z_cell = jax.random.randint(subkeys[2], (SLOTS,), 0, MESH_Z, dtype=jnp.int32)
    return jnp.stack([x_plane, y_row, z_cell]).astype(jnp.int32)


def draw_counts(key, part):
    key = jax.random.fold_in(key, 23)
    key_fill, key_full = jax.random.split(key)
    total = N_WIDE * NBLK
    filled = jax.random.randint(key_fill, (total,), CAP // 2, CAP + 1, dtype=jnp.int32)
    chosen = jax.random.randint(key_full, (N_WIDE,), 0, NBLK, dtype=jnp.int32)
    block_ids = jnp.arange(total, dtype=jnp.int32)
    full_block = block_ids % NBLK == jnp.repeat(chosen, NBLK)
    return jnp.where(full_block, CAP, filled).astype(jnp.int32)


def level_of(key, shape, shards, low, largest):
    level = 1.0
    for axis_at, shards_of in shards:
        draws = jax.random.uniform(jax.random.fold_in(jax.random.fold_in(key, 6), axis_at), (shards_of,), jnp.float32, low / len(shards), largest / len(shards))
        level = level * jnp.repeat(jnp.exp(draws), shape[axis_at] // shards_of).reshape((-1,) + (1,) * (len(shape) - 1 - axis_at))
    return level


def centred(own_key, shape, deviation, reach, shards=(), kind=jnp.bfloat16):
    result = jax.random.normal(own_key, shape, jnp.float32) * deviation
    if len(shards) > 0:
        result = level_of(own_key, shape, shards, -0.22, 0.18) * result
    return jnp.clip(result, min=-reach, max=reach).astype(kind)


def setup_inputs(seed: int = 0, part: int = 0) -> dict:
    seeds = jax.random.split(jax.random.key(seed), 6)
    part_splits = jax.random.split(jax.random.fold_in(seeds[5], part), 6)
    return {
        "charges": centred(part_splits[0], (CH, SLOTS), 1.0, 6.0, ((1, 16),)),
        "cell_offset": jnp.clip(1.0 * jax.random.uniform(part_splits[1], (3, SLOTS), jnp.float32) ** level_of(part_splits[1], (3, SLOTS), ((1, 16),), -0.2, 0.2), 0.0, 1.0),
        "base_cell": draw_base_cell(jax.random.fold_in(jax.random.fold_in(seeds[5], part), 71), part),
        "counts": draw_counts(jax.random.fold_in(jax.random.fold_in(seeds[5], part), 71), part),
        "widths": jnp.clip(jnp.exp(jax.random.uniform(seeds[4], (CH,), jnp.float32, math.log(0.75), math.log(2.0))), 0.75, 2.0),
    }


highest = lax.Precision.HIGHEST


def spline_table(offset, order_count):
    weights = [1.0 - offset, offset]
    slopes = [-jnp.ones_like(offset), jnp.ones_like(offset)]
    for degree in range(3, order_count + 1):
        if degree == order_count:
            slopes = [-weights[0]] + [weights[position - 1] - weights[position] for position in range(1, degree - 1)] + [weights[degree - 2]]
        factor = 1.0 / (degree - 1)
        updated = [None] * degree
        updated[degree - 1] = factor * offset * weights[degree - 2]
        for position in range(1, degree - 1):
            updated[degree - position - 1] = factor * ((offset + position) * weights[degree - position - 2] + (degree - position - offset) * weights[degree - position - 1])
        updated[0] = factor * (1.0 - offset) * weights[0]
        weights = updated
    return jnp.stack(weights), jnp.stack(slopes)


def stencil_rows(weights, slopes, relative, extent, period):
    shifts = jnp.arange(weights.shape[0], dtype=jnp.int32)[None, :, None]
    targets = (relative[:, None, :] + shifts) % period
    points = jnp.arange(extent, dtype=jnp.int32)[None, :, None, None]
    matches = points == targets[:, None]
    plain_rows = jnp.sum(jnp.where(matches, jnp.moveaxis(weights, 0, 1)[:, None], 0.0), axis=2)
    slope_rows = jnp.sum(jnp.where(matches, jnp.moveaxis(slopes, 0, 1)[:, None], 0.0), axis=2)
    return plain_rows, slope_rows


def folded(points, length):
    values = jnp.where(points * 2 > length, points - length, points)
    return values.astype(jnp.float32) / length


def moduli(points, length):
    base_weights, base_slopes = spline_table(jnp.zeros((1,), jnp.float32), ORDER)
    shifts = jnp.arange(ORDER, dtype=jnp.int32)
    phases = (points[:, None] * shifts[None, :]) % length
    angles = phases.astype(jnp.float32) * (2.0 * math.pi / length)
    real_sum = jnp.sum(base_weights[:, 0][None, :] * jnp.cos(angles), axis=1)
    imag_sum = jnp.sum(base_weights[:, 0][None, :] * jnp.sin(angles), axis=1)
    return real_sum * real_sum + imag_sum * imag_sum


def kernel_table(widths, x_freq, y_freq, z_freq, x_mod, y_mod, z_mod):
    total = x_freq[:, None, None, None] ** 2 + y_freq[None, :, None, None] ** 2 + z_freq[None, None, None, :] ** 2
    positive = total > 0
    safe = jnp.where(positive, total, 1.0)
    beta = widths[None, None, :, None]
    divisor = x_mod[:, None, None, None] * y_mod[None, :, None, None] * z_mod[None, None, None, :]
    return jnp.where(positive, 2.0 * jnp.exp(-(math.pi ** 2) * total / (beta * beta)) / (math.pi * safe * divisor), 0.0)


def combine_blocks(block_grid, block_rows, border):
    owned = block_grid[:, :, :block_rows]
    overflow = jnp.roll(block_grid[:, :, block_rows:], 1, axis=0)
    owned = owned.at[:, :, :border].add(overflow)
    moved = jnp.moveaxis(owned, 0, 1)
    return moved.reshape((moved.shape[0], moved.shape[1] * moved.shape[2]) + moved.shape[3:])


def contract(data, x_weights, y_weights):
    return jnp.einsum('pycs,ps,ys->cs', data, x_weights, y_weights, precision=highest)


def widen(values):
    return lax.optimization_barrier(values).astype(jnp.float32)


def reference(charges, cell_offset, base_cell, counts, widths):
    planes = MESH_X // N_WIDE
    border = ORDER - 1
    extent = planes + border
    y_extent = BLOCK_ROWS + border
    channels = charges.shape[0]
    charge_dev = jnp.moveaxis(charges.reshape(channels, N_WIDE, NBLK, CAP), 1, 0)
    offset_dev = jnp.moveaxis(cell_offset.reshape(3, N_WIDE, NBLK, CAP), 1, 0)
    base_dev = jnp.moveaxis(base_cell.reshape(3, N_WIDE, NBLK, CAP), 1, 0)
    count_dev = counts.reshape(N_WIDE, NBLK)
    devices = jnp.arange(N_WIDE, dtype=jnp.int32)

    def prepare(device, charge_one, offset_one, base_one, count_one):
        live_mask = jnp.arange(CAP, dtype=jnp.int32)[None, :] < count_one[:, None]
        charge_blocks = jnp.where(live_mask[:, None, :], jnp.moveaxis(charge_one, 0, 1), jnp.zeros((), jnp.bfloat16))
        x_weights, x_slopes = spline_table(offset_one[0], ORDER)
        y_weights, y_slopes = spline_table(offset_one[1], ORDER)
        z_weights, z_slopes = spline_table(offset_one[2], ORDER)
        row_start = jnp.arange(NBLK, dtype=jnp.int32)[:, None] * BLOCK_ROWS
        x_rows, x_drows = stencil_rows(x_weights, x_slopes, base_one[0] - device * planes, extent, extent)
        y_rows, y_drows = stencil_rows(y_weights, y_slopes, base_one[1] - row_start, y_extent, y_extent)
        z_plain, z_slope = stencil_rows(z_weights, z_slopes, base_one[2], MESH_Z, MESH_Z)
        z_table = jnp.stack([z_plain, z_slope], axis=2).astype(jnp.bfloat16)
        return live_mask, charge_blocks, x_rows, x_drows, y_rows, y_drows, z_table

    def spread_block(inputs):
        x_block, y_block, charge_block, table_block = inputs
        products = (x_block[:, None, None, :] * y_block[None, :, None, :] * charge_block.astype(jnp.float32)[None, None]).astype(jnp.bfloat16)
        spread = jnp.dot(widen(products).reshape(-1, CAP), widen(table_block[:, 0]).T, precision=highest)
        return spread.reshape(extent, y_extent, channels, MESH_Z)

    def spread_device(grid, inputs):
        device, charge_one, offset_one, base_one, count_one = inputs
        live_mask, charge_blocks, x_rows, x_drows, y_rows, y_drows, z_table = prepare(device, charge_one, offset_one, base_one, count_one)
        block_grid = lax.map(spread_block, (x_rows, y_rows, charge_blocks, z_table))
        grid_ext = combine_blocks(block_grid, BLOCK_ROWS, border)
        plane_index = (device * planes + jnp.arange(extent, dtype=jnp.int32)) % MESH_X
        return grid.at[plane_index].add(grid_ext), None

    start_grid = jnp.zeros((MESH_X, MESH_Y, channels, MESH_Z), jnp.float32)
    mesh, unused = lax.scan(spread_device, start_grid, (devices, charge_dev, offset_dev, base_dev, count_dev))
    spectrum = jnp.fft.fftn(mesh, axes=(0, 1, 3))
    x_points = jnp.arange(MESH_X, dtype=jnp.int32)
    y_points = jnp.arange(MESH_Y, dtype=jnp.int32)
    z_points = jnp.arange(MESH_Z, dtype=jnp.int32)
    kernel = kernel_table(widths, folded(x_points, MESH_X), folded(y_points, MESH_Y), folded(z_points, MESH_Z), moduli(x_points, MESH_X), moduli(y_points, MESH_Y), moduli(z_points, MESH_Z))
    field = jnp.real(jnp.fft.ifftn(spectrum * kernel, axes=(0, 1, 3)))
    potential_grid = field.astype(jnp.bfloat16)

    def gather_block(inputs):
        window, x_block, x_dblock, y_block, y_dblock, table_block, charge_block, live_block = inputs
        values = jnp.dot(widen(window).reshape(-1, MESH_Z), widen(table_block).reshape(MESH_Z, -1), precision=highest)
        values = values.reshape(extent, y_extent, channels, 2, CAP)
        direct = values[:, :, :, 0]
        sloped = values[:, :, :, 1]
        potential = jnp.where(live_block[None], contract(direct, x_block, y_block), 0.0)
        gradient = jnp.stack([contract(direct, x_dblock, y_block), contract(direct, x_block, y_dblock), contract(sloped, x_block, y_block)])
        forces = -jnp.sum(gradient * charge_block.astype(jnp.float32)[None], axis=1)
        return potential, forces

    def gather_device(inputs):
        device, charge_one, offset_one, base_one, count_one = inputs
        live_mask, charge_blocks, x_rows, x_drows, y_rows, y_drows, z_table = prepare(device, charge_one, offset_one, base_one, count_one)
        plane_index = (device * planes + jnp.arange(extent, dtype=jnp.int32)) % MESH_X
        potential_ext = potential_grid[plane_index]
        blocked = potential_ext.reshape(extent, NBLK, BLOCK_ROWS, channels, MESH_Z)
        following = jnp.roll(blocked[:, :, :border], -1, axis=1)
        windows = jnp.moveaxis(jnp.concatenate([blocked, following], axis=2), 1, 0)
        return lax.map(gather_block, (windows, x_rows, x_drows, y_rows, y_drows, z_table, charge_blocks, live_mask))

    potentials, forces = lax.map(gather_device, (devices, charge_dev, offset_dev, base_dev, count_dev))
    atom_potential = jnp.transpose(potentials, (2, 0, 1, 3)).reshape(channels, N_WIDE * NBLK * CAP)
    atom_forces = jnp.transpose(forces, (2, 0, 1, 3)).reshape(3, N_WIDE * NBLK * CAP)
    return atom_potential, atom_forces
```

```python
import functools
import math

import jax
import jax.numpy as jnp
import numpy as np
from jax import lax
from jax.experimental import pallas as pl
from jax.experimental.pallas import tpu as pltpu
from jax.sharding import PartitionSpec as P

MESH_X = 128
MESH_Y = 128
MESH_Z = 128
ORDER = 6


highest = lax.Precision.HIGHEST


def shifted(block, axis, distance):
    devices = range(lax.axis_size(axis))
    route = [((i - distance) % len(devices), i) for i in devices]
    return lax.ppermute(block, axis, route)


def spline_lists(offset, order_count):
    weights = [1.0 - offset, offset]
    slopes = [-jnp.ones_like(offset), jnp.ones_like(offset)]
    for degree in range(3, order_count + 1):
        if degree == order_count:
            slopes = (
                [-weights[0]]
                + [weights[position - 1] - weights[position] for position in range(1, degree - 1)]
                + [weights[degree - 2]]
            )
        factor = 1.0 / (degree - 1)
        updated = [None] * degree
        updated[degree - 1] = factor * offset * weights[degree - 2]
        for position in range(1, degree - 1):
            updated[degree - position - 1] = factor * (
                (offset + position) * weights[degree - position - 2]
                + (degree - position - offset) * weights[degree - position - 1]
            )
        updated[0] = factor * (1.0 - offset) * weights[0]
        weights = updated
    return (weights, slopes)


def spline_table(offset, order_count):
    weights, slopes = spline_lists(offset, order_count)
    return (jnp.stack(weights), jnp.stack(slopes))


def stencil_rows(weights, slopes, relative, extent, period):
    shifts = jnp.arange(weights.shape[0], dtype=jnp.int32)[None, :, None]
    targets = (relative[:, None, :] + shifts) % period
    points = jnp.arange(extent, dtype=jnp.int32)[None, :, None, None]
    matches = points == targets[:, None]
    plain_rows = jnp.sum(jnp.where(matches, jnp.moveaxis(weights, 0, 1)[:, None], 0.0), axis=2)
    slope_rows = jnp.sum(jnp.where(matches, jnp.moveaxis(slopes, 0, 1)[:, None], 0.0), axis=2)
    return (plain_rows, slope_rows)


def folded(points, length):
    values = jnp.where(points * 2 > length, points - length, points)
    return values.astype(jnp.float32) / length


def moduli(points, length):
    base_weights, base_slopes = spline_table(jnp.zeros((1,), jnp.float32), ORDER)
    shifts = jnp.arange(ORDER, dtype=jnp.int32)
    phases = points[:, None] * shifts[None, :] % length
    angles = phases.astype(jnp.float32) * (2.0 * math.pi / length)
    real_sum = jnp.sum(base_weights[:, 0][None, :] * jnp.cos(angles), axis=1)
    imag_sum = jnp.sum(base_weights[:, 0][None, :] * jnp.sin(angles), axis=1)
    return real_sum * real_sum + imag_sum * imag_sum


def kernel_table(widths, x_freq, y_freq, z_freq, x_mod, y_mod, z_mod):
    total = (
        x_freq[:, None, None, None] ** 2
        + y_freq[None, :, None, None] ** 2
        + z_freq[None, None, None, :] ** 2
    )
    positive = total > 0
    safe = jnp.where(positive, total, 1.0)
    beta = widths[None, None, :, None]
    divisor = x_mod[:, None, None, None] * y_mod[None, :, None, None] * z_mod[None, None, None, :]
    return jnp.where(
        positive,
        2.0 * jnp.exp(-math.pi**2 * total / (beta * beta)) / (math.pi * safe * divisor),
        0.0,
    )


def dft_tables(length):
    points = jnp.arange(length, dtype=jnp.int32)
    phases = points[:, None] * points[None, :] % length
    angles = phases.astype(jnp.float32) * (2.0 * math.pi / length)
    return (jnp.cos(angles), jnp.sin(angles))


def combine_blocks(block_grid, block_rows, border):
    owned = block_grid[:, :, :block_rows]
    overflow = jnp.roll(block_grid[:, :, block_rows:], 1, axis=0)
    owned = owned.at[:, :, :border].add(overflow)
    moved = jnp.moveaxis(owned, 0, 1)
    return moved.reshape((moved.shape[0], moved.shape[1] * moved.shape[2]) + moved.shape[3:])


def contract(data, x_weights, y_weights):
    return jnp.einsum("pycs,ps,ys->cs", data, x_weights, y_weights, precision=highest)


def turn(real_part, imag_part, cosines, sines, orient, pattern):

    def project(data, table):
        return jnp.einsum(pattern, data, table, precision=highest)

    real_out = project(real_part, cosines) - orient * project(imag_part, sines)
    imag_out = project(imag_part, cosines) + orient * project(real_part, sines)
    return jnp.stack([real_out, imag_out])


def slab_shards(charges, cell_offset, base_cell, counts, widths):
    wide_size = lax.axis_size("wide")
    device = lax.axis_index("wide")
    channels, slot_count = charges.shape
    blocks = counts.shape[0]
    capacity = slot_count // blocks
    planes = MESH_X // wide_size
    border = ORDER - 1
    extent = planes + border
    block_rows = MESH_Y // blocks
    y_extent = block_rows + border
    rounds = (border + planes - 1) // planes
    y_local = MESH_Y // wide_size
    live_mask = jnp.arange(capacity, dtype=jnp.int32)[None, :] < counts[:, None]
    charge_blocks = jnp.where(
        live_mask[:, None, :],
        jnp.moveaxis(charges.reshape(channels, blocks, capacity), 0, 1),
        jnp.zeros((), jnp.bfloat16),
    )
    offsets = cell_offset.reshape(3, blocks, capacity)
    bases = base_cell.reshape(3, blocks, capacity)
    x_weights, x_slopes = spline_table(offsets[0], ORDER)
    y_weights, y_slopes = spline_table(offsets[1], ORDER)
    z_weights, z_slopes = spline_table(offsets[2], ORDER)
    row_start = jnp.arange(blocks, dtype=jnp.int32)[:, None] * block_rows
    x_rows, x_drows = stencil_rows(x_weights, x_slopes, bases[0] - device * planes, extent, extent)
    y_rows, y_drows = stencil_rows(y_weights, y_slopes, bases[1] - row_start, y_extent, y_extent)
    z_plain, z_slope = stencil_rows(z_weights, z_slopes, bases[2], MESH_Z, MESH_Z)
    z_table = jnp.stack([z_plain, z_slope], axis=2).astype(jnp.bfloat16)

    def spread_block(inputs):
        x_block, y_block, charge_block, table_block = inputs
        products = (
            x_block[:, None, None, :]
            * y_block[None, :, None, :]
            * charge_block.astype(jnp.float32)[None, None]
        ).astype(jnp.bfloat16)
        spread = jnp.einsum(
            "rs,zs->rz",
            products.reshape(-1, capacity),
            table_block[:, 0],
            preferred_element_type=jnp.float32,
        )
        return spread.reshape(extent, y_extent, channels, MESH_Z)

    block_grid = lax.map(spread_block, (x_rows, y_rows, charge_blocks, z_table))
    grid_ext = combine_blocks(block_grid, block_rows, border)
    z_cos, z_sin = dft_tables(MESH_Z)
    y_cos, y_sin = dft_tables(MESH_Y)
    x_cos, x_sin = dft_tables(MESH_X)
    x_points = jnp.arange(MESH_X, dtype=jnp.int32)
    y_points = device * y_local + jnp.arange(y_local, dtype=jnp.int32)
    z_points = jnp.arange(MESH_Z, dtype=jnp.int32)
    kernel = kernel_table(
        widths,
        folded(x_points, MESH_X),
        folded(y_points, MESH_Y),
        folded(z_points, MESH_Z),
        moduli(x_points, MESH_X),
        moduli(y_points, MESH_Y),
        moduli(z_points, MESH_Z),
    )
    kernel = kernel / float(MESH_X * MESH_Y * MESH_Z)
    owned = grid_ext[:planes]
    for hop_index in range(1, rounds + 1):
        outgoing = grid_ext[hop_index * planes : (hop_index + 1) * planes]
        outgoing = jnp.pad(outgoing, ((0, planes - outgoing.shape[0]), (0, 0), (0, 0), (0, 0)))
        owned = owned + shifted(outgoing, "wide", hop_index)
    real_z = jnp.dot(owned, z_cos, precision=highest)
    imag_z = -jnp.dot(owned, z_sin, precision=highest)
    columns = lax.all_to_all(
        turn(real_z, imag_z, y_cos, y_sin, -1.0, "pycz,yk->pkcz"),
        "wide",
        split_axis=2,
        concat_axis=1,
        tiled=True,
    )
    spectrum = turn(columns[0], columns[1], x_cos, x_sin, -1.0, "xycz,xk->kycz")
    filtered = turn(spectrum[0] * kernel, spectrum[1] * kernel, x_cos, x_sin, 1.0, "xycz,xk->kycz")
    returned = lax.all_to_all(filtered, "wide", split_axis=1, concat_axis=2, tiled=True)
    along_y = turn(returned[0], returned[1], y_cos, y_sin, 1.0, "pycz,yk->pkcz")
    potential_own = (
        jnp.dot(along_y[0], z_cos, precision=highest)
        - jnp.dot(along_y[1], z_sin, precision=highest)
    ).astype(jnp.bfloat16)
    pieces = [potential_own]
    for hop_index in range(1, rounds + 1):
        pieces.append(shifted(potential_own, "wide", -hop_index))
    potential_ext = jnp.concatenate(pieces, axis=0)[:extent]
    blocked = potential_ext.reshape(extent, blocks, block_rows, channels, MESH_Z)
    following = jnp.roll(blocked[:, :, :border], -1, axis=1)
    windows = jnp.moveaxis(jnp.concatenate([blocked, following], axis=2), 1, 0)

    def gather_block(inputs):
        window, x_block, x_dblock, y_block, y_dblock, table_block, charge_block, live_block = inputs
        values = jnp.dot(
            window.reshape(-1, MESH_Z),
            table_block.reshape(MESH_Z, -1),
            preferred_element_type=jnp.float32,
        )
        values = values.reshape(extent, y_extent, channels, 2, capacity)
        direct = values[:, :, :, 0]
        sloped = values[:, :, :, 1]
        potential = jnp.where(live_block[None], contract(direct, x_block, y_block), 0.0)
        gradient = jnp.stack(
            [
                contract(direct, x_dblock, y_block),
                contract(direct, x_block, y_dblock),
                contract(sloped, x_block, y_block),
            ]
        )
        forces = -jnp.sum(gradient * charge_block.astype(jnp.float32)[None], axis=1)
        return (potential, forces)

    potentials, forces = lax.map(
        gather_block, (windows, x_rows, x_drows, y_rows, y_drows, z_table, charge_blocks, live_mask)
    )
    atom_potential = jnp.moveaxis(potentials, 0, 1).reshape(channels, slot_count)
    atom_forces = jnp.moveaxis(forces, 0, 1).reshape(3, slot_count)
    return (atom_potential, atom_forces)


def cas_terms(length):
    points = np.arange(length)
    angles = (points[:, None] * points[None, :] % length) * (2.0 * math.pi / length)
    left = (np.cos(angles) + np.sin(angles)).astype(np.float32)
    terms = []
    for _ in range(3):
        term = left.astype(jnp.bfloat16)
        terms.append(term)
        left = left - term.astype(np.float32)
    return terms


def split(values):
    terms = []
    for _ in range(3):
        term = values.astype(jnp.bfloat16)
        terms.append(term)
        values = values - term.astype(jnp.float32)
    return terms


def dot32(a, b, contract_b=0):
    return lax.dot_general(a, b, (((1,), (contract_b,)), ((), ())), preferred_element_type=jnp.float32)


def cas_lanes(values, right_a, right_b):
    first, second, third = split(values)
    wide = dot32(jnp.concatenate([first, second], axis=1), right_a)
    rest = dot32(jnp.concatenate([first, third], axis=1), right_b)
    length = values.shape[1]
    return wide[:, :length] + (wide[:, length:] + rest)


def cas_rows(values, left_a, left_b):
    first, second, third = split(values)
    wide = dot32(left_a, jnp.concatenate([first, second], axis=0))
    rest = dot32(left_b, jnp.concatenate([first, third], axis=0))
    length = values.shape[0]
    return wide[:length] + (wide[length:] + rest)


def channel_kernel(
    geometry_ref, charge_ref, pair_ref, square_ref, gain_ref, y_square_ref,
    right_a_ref, right_b_ref, left_a_ref, left_b_ref, out_ref,
    grid_ref, turned_ref, spline_ref, place_ref,
):
    slabs, _, blocks, capacity = geometry_ref.shape
    planes = MESH_X // slabs
    rows = MESH_Y // blocks
    border = ORDER - 1
    frame = 16
    extent = planes + border
    far = MESH_X + border

    def prepare(slab, carry):
        packed = geometry_ref[slab, 3].astype(jnp.int32)
        span = pl.ds(pl.multiple_of(slab * blocks, blocks), blocks)
        place_ref[0, span, :] = packed & 7
        place_ref[1, span, :] = (packed >> 3) & 7
        place_ref[2, span, :] = (packed >> 6) & 7
        place_ref[3, span, :] = packed >> 9
        for dimension in range(3):
            weights, slopes = spline_lists(geometry_ref[slab, dimension], ORDER)
            for position in range(ORDER):
                spline_ref[dimension * 2 * ORDER + position, span, :] = weights[position]
                spline_ref[(dimension * 2 + 1) * ORDER + position, span, :] = slopes[position]
        return carry

    lax.fori_loop(0, slabs, prepare, 0)

    def clear(plane, carry):
        grid_ref[plane] = jnp.zeros(grid_ref.shape[1:], jnp.float32)
        return carry

    lax.fori_loop(0, far, clear, 0)
    points = lax.broadcasted_iota(jnp.int32, (frame, capacity), 0)

    def local_table(dimension, block, kinds):
        distance = points - place_ref[dimension, pl.ds(block, 1), :]
        matches = [distance == position for position in range(ORDER)]
        tables = []
        for kind in kinds:
            table = jnp.zeros((frame, capacity), jnp.float32)
            for position in range(ORDER):
                row = spline_ref[(dimension * 2 + kind) * ORDER + position, pl.ds(block, 1), :]
                table = jnp.where(matches[position], row, table)
            tables.append(table)
        return tables

    def z_tables(block, kinds):
        tables = local_table(2, block, kinds)
        tile = jnp.broadcast_to(place_ref[3, pl.ds(block, 1), :], (8, capacity))
        here = [tile == index for index in range(MESH_Z // 8)]
        results = []
        for table in tables:
            low, high = table[:8], table[8:]
            pieces = [
                jnp.where(here[index], low, jnp.where(here[index - 1], high, 0.0))
                for index in range(MESH_Z // 8)
            ]
            results.append(jnp.concatenate(pieces, axis=0).astype(jnp.bfloat16))
        return results

    def spread(slab, block):
        place = slab * blocks + block
        (x_table,) = local_table(0, place, (0,))
        (y_table,) = local_table(1, place, (0,))
        (z_table,) = z_tables(place, (0,))
        charge = charge_ref[slab, pl.ds(block, 1), :]
        products = jnp.concatenate(
            [
                ((x_table[index : index + 1] * y_table) * charge).astype(jnp.bfloat16)
                for index in range(extent)
            ],
            axis=0,
        )
        sums = dot32(products, z_table, 1)
        row_span = pl.ds(pl.multiple_of(block * rows, rows), frame)
        for index in range(extent):
            grid_ref[slab * planes + index, row_span, :] += sums[index * frame : (index + 1) * frame]

    def spread_step(step, carry):
        spread(step // blocks, step % blocks)
        return carry

    lax.fori_loop(0, slabs * blocks, spread_step, 0)

    for index in range(border):
        grid_ref[index] += grid_ref[MESH_X + index]

    right_a, right_b = right_a_ref[...], right_b_ref[...]
    left_a, left_b = left_a_ref[...], left_b_ref[...]

    def forward(step, carry):
        both = []
        for index in range(2):
            plane = 2 * step + index
            both.append(grid_ref[plane, 0:8, :] + grid_ref[plane, MESH_Y : MESH_Y + 8, :])
            both.append(grid_ref[plane, 8:MESH_Y, :])
        along_z = cas_lanes(jnp.concatenate(both, axis=0), right_a, right_b)
        along_y = cas_rows(
            jnp.concatenate([along_z[:MESH_Y], along_z[MESH_Y:]], axis=1), left_a, left_b
        )
        for index in range(2):
            turned_ref[pl.ds(2 * step + index, MESH_Y, stride=MESH_X), :] = along_y[
                :, index * MESH_Z : (index + 1) * MESH_Z
            ]
        return carry

    lax.fori_loop(0, MESH_X // 2, forward, 0)

    def filtering(step, carry):
        spans = [pl.ds(pl.multiple_of((2 * step + index) * MESH_X, MESH_X), MESH_X) for index in range(2)]
        lines = jnp.concatenate([turned_ref[span, :] for span in spans], axis=1)
        spectrum = cas_rows(lines, left_a, left_b)
        filters = []
        for index in range(2):
            total = square_ref[...] + y_square_ref[2 * step + index]
            positive = total > 0
            safe = jnp.where(positive, total, 1.0)
            filters.append(jnp.where(positive, pair_ref[...] * gain_ref[2 * step + index] / safe, 0.0))
        lines = cas_rows(spectrum * jnp.concatenate(filters, axis=1), left_a, left_b)
        for index, span in enumerate(spans):
            turned_ref[span, :] = lines[:, index * MESH_Z : (index + 1) * MESH_Z]
        return carry

    lax.fori_loop(0, MESH_Y // 2, filtering, 0)

    def backward(step, carry):
        both = jnp.concatenate(
            [turned_ref[pl.ds(2 * step + index, MESH_Y, stride=MESH_X), :] for index in range(2)], axis=1
        )
        along_y = cas_rows(both, left_a, left_b)
        field = cas_lanes(
            jnp.concatenate([along_y[:, :MESH_Z], along_y[:, MESH_Z:]], axis=0), right_a, right_b
        )
        rounded = field.astype(jnp.bfloat16).astype(jnp.float32)
        for index in range(2):
            grid_ref[2 * step + index, 0:MESH_Y, :] = rounded[index * MESH_Y : (index + 1) * MESH_Y]
            grid_ref[2 * step + index, MESH_Y : MESH_Y + 8, :] = rounded[index * MESH_Y : index * MESH_Y + 8]
        return carry

    lax.fori_loop(0, MESH_X // 2, backward, 0)

    for index in range(border):
        grid_ref[MESH_X + index] = grid_ref[index]

    def gather(slab, block):
        place = slab * blocks + block
        x_table, x_slope = local_table(0, place, (0, 1))
        y_table, y_slope = local_table(1, place, (0, 1))
        z_table, z_slope = z_tables(place, (0, 1))
        charge = charge_ref[slab, pl.ds(block, 1), :]
        row_span = pl.ds(pl.multiple_of(block * rows, rows), frame)
        window = jnp.concatenate(
            [grid_ref[slab * planes + index, row_span, :] for index in range(extent)], axis=0
        ).astype(jnp.bfloat16)
        near = dot32(window, z_table)
        near_z = dot32(window, z_slope)
        plain = jnp.zeros((frame, capacity), jnp.float32)
        sloped = jnp.zeros((frame, capacity), jnp.float32)
        plain_z = jnp.zeros((frame, capacity), jnp.float32)
        for index in range(extent):
            part = near[index * frame : (index + 1) * frame]
            plain += x_table[index : index + 1] * part
            sloped += x_slope[index : index + 1] * part
            plain_z += x_table[index : index + 1] * near_z[index * frame : (index + 1) * frame]
        row = pl.ds(block, 1)
        out_ref[slab, 0, row, :] = jnp.sum(y_table * plain, axis=0, keepdims=True)
        out_ref[slab, 1, row, :] = -charge * jnp.sum(y_table * sloped, axis=0, keepdims=True)
        out_ref[slab, 2, row, :] = -charge * jnp.sum(y_slope * plain, axis=0, keepdims=True)
        out_ref[slab, 3, row, :] = -charge * jnp.sum(y_table * plain_z, axis=0, keepdims=True)

    def gather_step(step, carry):
        gather(step // blocks, step % blocks)
        return carry

    lax.fori_loop(0, slabs * blocks, gather_step, 0)


def channel_shards(charges, cell_offset, base_cell, counts, widths):
    device = lax.axis_index("wide")
    channels, slot_count = charges.shape
    blocks = counts.shape[0]
    capacity = slot_count // blocks
    slabs = lax.axis_size("wide")
    planes = MESH_X // slabs
    block_rows = MESH_Y // blocks
    live_mask = jnp.arange(capacity, dtype=jnp.int32)[None, :] < counts[:, None]
    charge_blocks = jnp.where(
        live_mask[None], charges.reshape(channels, blocks, capacity), jnp.zeros((), jnp.bfloat16)
    )
    bases = base_cell.reshape(3, blocks, capacity)
    row_start = jnp.arange(blocks, dtype=jnp.int32)[:, None] * block_rows
    packed = (bases[0] - device * planes) + 8 * (bases[1] - row_start) + 64 * bases[2]
    geometry = jnp.concatenate(
        [cell_offset.reshape(3, blocks, capacity), packed.astype(jnp.float32)[None]], axis=0
    )
    geometry = lax.all_gather(geometry, "wide", axis=0, tiled=False)
    charge_blocks = lax.all_to_all(charge_blocks, "wide", split_axis=0, concat_axis=0, tiled=True)

    width = lax.dynamic_index_in_dim(widths, device, keepdims=False)
    points = np.arange(MESH_X)
    folded_points = np.where(points * 2 > MESH_X, points - MESH_X, points) / MESH_X
    squares = (folded_points**2).astype(np.float32)
    first = np.array([1.0, 26.0, 66.0, 26.0, 1.0, 0.0]) / 120.0
    angles = 2.0 * math.pi * points[:, None] * np.arange(ORDER)[None, :] / MESH_X
    inverse = (1.0 / ((np.cos(angles) @ first) ** 2 + (np.sin(angles) @ first) ** 2)).astype(np.float32)
    gains = jnp.exp(-(math.pi**2) * squares / (width * width)) * inverse
    scale = 2.0 / (math.pi * MESH_X * MESH_Y * MESH_Z)
    pairs = gains[:, None] * (gains * scale)[None, :]
    pair_squares = squares[:, None] + squares[None, :]
    one, two, three = cas_terms(MESH_X)
    right_a = np.concatenate([np.concatenate([one, two], axis=1)] * 2, axis=0)
    right_b = np.concatenate([three, one], axis=0)
    left_a = np.concatenate([np.concatenate([one, one], axis=1), np.concatenate([two, two], axis=1)], axis=0)
    left_b = np.concatenate([three, one], axis=1)

    whole = pl.BlockSpec(memory_space=pltpu.VMEM)
    scalars = pl.BlockSpec(memory_space=pltpu.SMEM)
    result = pl.pallas_call(
        channel_kernel,
        out_shape=jax.ShapeDtypeStruct((slabs, 4, blocks, capacity), jnp.float32),
        in_specs=[whole] * 4 + [scalars] * 2 + [whole] * 4,
        out_specs=whole,
        scratch_shapes=[
            pltpu.VMEM((MESH_X + ORDER - 1, MESH_Y + 8, MESH_Z), jnp.float32),
            pltpu.VMEM((MESH_X * MESH_Y, MESH_Z), jnp.float32),
            pltpu.VMEM((6 * ORDER, slabs * blocks, capacity), jnp.float32),
            pltpu.VMEM((4, slabs * blocks, capacity), jnp.int32),
        ],
        compiler_params=pltpu.CompilerParams(vmem_limit_bytes=52 * 1024 * 1024),
        name="channel",
    )(
        geometry, charge_blocks.astype(jnp.float32), pairs, jnp.asarray(pair_squares), gains,
        jnp.asarray(squares), jnp.asarray(right_a), jnp.asarray(right_b), jnp.asarray(left_a),
        jnp.asarray(left_b),
    )
    returned = lax.all_to_all(result, "wide", split_axis=0, concat_axis=0, tiled=True)
    atom_potential = jnp.where(live_mask[None], returned[:, 0], 0.0).reshape(channels, slot_count)
    forces = jnp.sum(returned[:, 1:], axis=0).reshape(3, slot_count)
    return (atom_potential, forces)


def shards(charges, cell_offset, base_cell, counts, widths):
    if lax.axis_size("wide") == charges.shape[0] and MESH_X == 8 * lax.axis_size("wide"):
        return channel_shards(charges, cell_offset, base_cell, counts, widths)
    return slab_shards(charges, cell_offset, base_cell, counts, widths)


def solution(mesh):
    in_specs = (
        P(None, ("groups", "wide")),
        P(None, ("groups", "wide")),
        P(None, ("groups", "wide")),
        P(("groups", "wide")),
        P(),
    )
    out_specs = (P(None, ("groups", "wide")), P(None, ("groups", "wide")))
    return jax.shard_map(shards, mesh=mesh, in_specs=in_specs, out_specs=out_specs, check_vma=False)
```

```python
import functools
import math

import jax
import jax.numpy as jnp
import numpy as np
from jax import lax
from jax.experimental import pallas as pl
from jax.experimental.pallas import tpu as pltpu
from jax.sharding import PartitionSpec as P

MESH_X = 128
MESH_Y = 128
MESH_Z = 128
ORDER = 6


highest = lax.Precision.HIGHEST


def shifted(block, axis, distance):
    devices = range(lax.axis_size(axis))
    route = [((i - distance) % len(devices), i) for i in devices]
    return lax.ppermute(block, axis, route)


def spline_lists(offset, order_count):
    weights = [1.0 - offset, offset]
    slopes = [-jnp.ones_like(offset), jnp.ones_like(offset)]
    for degree in range(3, order_count + 1):
        if degree == order_count:
            slopes = (
                [-weights[0]]
                + [weights[position - 1] - weights[position] for position in range(1, degree - 1)]
                + [weights[degree - 2]]
            )
        factor = 1.0 / (degree - 1)
        updated = [None] * degree
        updated[degree - 1] = factor * offset * weights[degree - 2]
        for position in range(1, degree - 1):
            updated[degree - position - 1] = factor * (
                (offset + position) * weights[degree - position - 2]
                + (degree - position - offset) * weights[degree - position - 1]
            )
        updated[0] = factor * (1.0 - offset) * weights[0]
        weights = updated
    return (weights, slopes)


def spline_table(offset, order_count):
    weights, slopes = spline_lists(offset, order_count)
    return (jnp.stack(weights), jnp.stack(slopes))


def stencil_rows(weights, slopes, relative, extent, period):
    shifts = jnp.arange(weights.shape[0], dtype=jnp.int32)[None, :, None]
    targets = (relative[:, None, :] + shifts) % period
    points = jnp.arange(extent, dtype=jnp.int32)[None, :, None, None]
    matches = points == targets[:, None]
    plain_rows = jnp.sum(jnp.where(matches, jnp.moveaxis(weights, 0, 1)[:, None], 0.0), axis=2)
    slope_rows = jnp.sum(jnp.where(matches, jnp.moveaxis(slopes, 0, 1)[:, None], 0.0), axis=2)
    return (plain_rows, slope_rows)


def folded(points, length):
    values = jnp.where(points * 2 > length, points - length, points)
    return values.astype(jnp.float32) / length


def moduli(points, length):
    base_weights, base_slopes = spline_table(jnp.zeros((1,), jnp.float32), ORDER)
    shifts = jnp.arange(ORDER, dtype=jnp.int32)
    phases = points[:, None] * shifts[None, :] % length
    angles = phases.astype(jnp.float32) * (2.0 * math.pi / length)
    real_sum = jnp.sum(base_weights[:, 0][None, :] * jnp.cos(angles), axis=1)
    imag_sum = jnp.sum(base_weights[:, 0][None, :] * jnp.sin(angles), axis=1)
    return real_sum * real_sum + imag_sum * imag_sum


def kernel_table(widths, x_freq, y_freq, z_freq, x_mod, y_mod, z_mod):
    total = (
        x_freq[:, None, None, None] ** 2
        + y_freq[None, :, None, None] ** 2
        + z_freq[None, None, None, :] ** 2
    )
    positive = total > 0
    safe = jnp.where(positive, total, 1.0)
    beta = widths[None, None, :, None]
    divisor = x_mod[:, None, None, None] * y_mod[None, :, None, None] * z_mod[None, None, None, :]
    return jnp.where(
        positive,
        2.0 * jnp.exp(-math.pi**2 * total / (beta * beta)) / (math.pi * safe * divisor),
        0.0,
    )


def dft_tables(length):
    points = jnp.arange(length, dtype=jnp.int32)
    phases = points[:, None] * points[None, :] % length
    angles = phases.astype(jnp.float32) * (2.0 * math.pi / length)
    return (jnp.cos(angles), jnp.sin(angles))


def combine_blocks(block_grid, block_rows, border):
    owned = block_grid[:, :, :block_rows]
    overflow = jnp.roll(block_grid[:, :, block_rows:], 1, axis=0)
    owned = owned.at[:, :, :border].add(overflow)
    moved = jnp.moveaxis(owned, 0, 1)
    return moved.reshape((moved.shape[0], moved.shape[1] * moved.shape[2]) + moved.shape[3:])


def contract(data, x_weights, y_weights):
    return jnp.einsum("pycs,ps,ys->cs", data, x_weights, y_weights, precision=highest)


def turn(real_part, imag_part, cosines, sines, orient, pattern):

    def project(data, table):
        return jnp.einsum(pattern, data, table, precision=highest)

    real_out = project(real_part, cosines) - orient * project(imag_part, sines)
    imag_out = project(imag_part, cosines) + orient * project(real_part, sines)
    return jnp.stack([real_out, imag_out])


def slab_shards(charges, cell_offset, base_cell, counts, widths):
    wide_size = lax.axis_size("wide")
    device = lax.axis_index("wide")
    channels, slot_count = charges.shape
    blocks = counts.shape[0]
    capacity = slot_count // blocks
    planes = MESH_X // wide_size
    border = ORDER - 1
    extent = planes + border
    block_rows = MESH_Y // blocks
    y_extent = block_rows + border
    rounds = (border + planes - 1) // planes
    y_local = MESH_Y // wide_size
    live_mask = jnp.arange(capacity, dtype=jnp.int32)[None, :] < counts[:, None]
    charge_blocks = jnp.where(
        live_mask[:, None, :],
        jnp.moveaxis(charges.reshape(channels, blocks, capacity), 0, 1),
        jnp.zeros((), jnp.bfloat16),
    )
    offsets = cell_offset.reshape(3, blocks, capacity)
    bases = base_cell.reshape(3, blocks, capacity)
    x_weights, x_slopes = spline_table(offsets[0], ORDER)
    y_weights, y_slopes = spline_table(offsets[1], ORDER)
    z_weights, z_slopes = spline_table(offsets[2], ORDER)
    row_start = jnp.arange(blocks, dtype=jnp.int32)[:, None] * block_rows
    x_rows, x_drows = stencil_rows(x_weights, x_slopes, bases[0] - device * planes, extent, extent)
    y_rows, y_drows = stencil_rows(y_weights, y_slopes, bases[1] - row_start, y_extent, y_extent)
    z_plain, z_slope = stencil_rows(z_weights, z_slopes, bases[2], MESH_Z, MESH_Z)
    z_table = jnp.stack([z_plain, z_slope], axis=2).astype(jnp.bfloat16)

    def spread_block(inputs):
        x_block, y_block, charge_block, table_block = inputs
        products = (
            x_block[:, None, None, :]
            * y_block[None, :, None, :]
            * charge_block.astype(jnp.float32)[None, None]
        ).astype(jnp.bfloat16)
        spread = jnp.einsum(
            "rs,zs->rz",
            products.reshape(-1, capacity),
            table_block[:, 0],
            preferred_element_type=jnp.float32,
        )
        return spread.reshape(extent, y_extent, channels, MESH_Z)

    block_grid = lax.map(spread_block, (x_rows, y_rows, charge_blocks, z_table))
    grid_ext = combine_blocks(block_grid, block_rows, border)
    z_cos, z_sin = dft_tables(MESH_Z)
    y_cos, y_sin = dft_tables(MESH_Y)
    x_cos, x_sin = dft_tables(MESH_X)
    x_points = jnp.arange(MESH_X, dtype=jnp.int32)
    y_points = device * y_local + jnp.arange(y_local, dtype=jnp.int32)
    z_points = jnp.arange(MESH_Z, dtype=jnp.int32)
    kernel = kernel_table(
        widths,
        folded(x_points, MESH_X),
        folded(y_points, MESH_Y),
        folded(z_points, MESH_Z),
        moduli(x_points, MESH_X),
        moduli(y_points, MESH_Y),
        moduli(z_points, MESH_Z),
    )
    kernel = kernel / float(MESH_X * MESH_Y * MESH_Z)
    owned = grid_ext[:planes]
    for hop_index in range(1, rounds + 1):
        outgoing = grid_ext[hop_index * planes : (hop_index + 1) * planes]
        outgoing = jnp.pad(outgoing, ((0, planes - outgoing.shape[0]), (0, 0), (0, 0), (0, 0)))
        owned = owned + shifted(outgoing, "wide", hop_index)
    real_z = jnp.dot(owned, z_cos, precision=highest)
    imag_z = -jnp.dot(owned, z_sin, precision=highest)
    columns = lax.all_to_all(
        turn(real_z, imag_z, y_cos, y_sin, -1.0, "pycz,yk->pkcz"),
        "wide",
        split_axis=2,
        concat_axis=1,
        tiled=True,
    )
    spectrum = turn(columns[0], columns[1], x_cos, x_sin, -1.0, "xycz,xk->kycz")
    filtered = turn(spectrum[0] * kernel, spectrum[1] * kernel, x_cos, x_sin, 1.0, "xycz,xk->kycz")
    returned = lax.all_to_all(filtered, "wide", split_axis=1, concat_axis=2, tiled=True)
    along_y = turn(returned[0], returned[1], y_cos, y_sin, 1.0, "pycz,yk->pkcz")
    potential_own = (
        jnp.dot(along_y[0], z_cos, precision=highest)
        - jnp.dot(along_y[1], z_sin, precision=highest)
    ).astype(jnp.bfloat16)
    pieces = [potential_own]
    for hop_index in range(1, rounds + 1):
        pieces.append(shifted(potential_own, "wide", -hop_index))
    potential_ext = jnp.concatenate(pieces, axis=0)[:extent]
    blocked = potential_ext.reshape(extent, blocks, block_rows, channels, MESH_Z)
    following = jnp.roll(blocked[:, :, :border], -1, axis=1)
    windows = jnp.moveaxis(jnp.concatenate([blocked, following], axis=2), 1, 0)

    def gather_block(inputs):
        window, x_block, x_dblock, y_block, y_dblock, table_block, charge_block, live_block = inputs
        values = jnp.dot(
            window.reshape(-1, MESH_Z),
            table_block.reshape(MESH_Z, -1),
            preferred_element_type=jnp.float32,
        )
        values = values.reshape(extent, y_extent, channels, 2, capacity)
        direct = values[:, :, :, 0]
        sloped = values[:, :, :, 1]
        potential = jnp.where(live_block[None], contract(direct, x_block, y_block), 0.0)
        gradient = jnp.stack(
            [
                contract(direct, x_dblock, y_block),
                contract(direct, x_block, y_dblock),
                contract(sloped, x_block, y_block),
            ]
        )
        forces = -jnp.sum(gradient * charge_block.astype(jnp.float32)[None], axis=1)
        return (potential, forces)

    potentials, forces = lax.map(
        gather_block, (windows, x_rows, x_drows, y_rows, y_drows, z_table, charge_blocks, live_mask)
    )
    atom_potential = jnp.moveaxis(potentials, 0, 1).reshape(channels, slot_count)
    atom_forces = jnp.moveaxis(forces, 0, 1).reshape(3, slot_count)
    return (atom_potential, atom_forces)


def cas_terms(length):
    points = np.arange(length)
    angles = (points[:, None] * points[None, :] % length) * (2.0 * math.pi / length)
    left = (np.cos(angles) + np.sin(angles)).astype(np.float32)
    terms = []
    for _ in range(2):
        term = left.astype(jnp.bfloat16)
        terms.append(term)
        left = left - term.astype(np.float32)
    return terms


def split(values):
    first = values.astype(jnp.bfloat16)
    return first, (values - first.astype(jnp.float32)).astype(jnp.bfloat16)


def dot32(a, b, contract_b=0):
    return lax.dot_general(a, b, (((1,), (contract_b,)), ((), ())), preferred_element_type=jnp.float32)


def cas_lanes(values, right):
    sums = dot32(jnp.concatenate(split(values), axis=1), right)
    length = values.shape[1]
    return sums[:, :length] + sums[:, length:]


def cas_rows(values, left):
    first, second = split(values)
    return dot32(left, jnp.concatenate([first, second, first], axis=0))


def channel_kernel(
    geometry_ref, charge_ref, pair_ref, square_ref, gain_ref, y_square_ref,
    right_ref, left_ref, out_ref,
    grid_ref, turned_ref, window_ref, spline_ref, place_ref,
):
    slabs, _, blocks, capacity = geometry_ref.shape
    planes = MESH_X // slabs
    rows = MESH_Y // blocks
    border = ORDER - 1
    frame = 16
    extent = planes + border
    far = MESH_X + border

    def prepare(slab, carry):
        packed = geometry_ref[slab, 3].astype(jnp.int32)
        span = pl.ds(pl.multiple_of(slab * blocks, blocks), blocks)
        place_ref[0, span, :] = packed & 7
        place_ref[1, span, :] = (packed >> 3) & 7
        place_ref[2, span, :] = (packed >> 6) & 7
        place_ref[3, span, :] = packed >> 9
        for dimension in range(3):
            weights, slopes = spline_lists(geometry_ref[slab, dimension], ORDER)
            for kind, values in enumerate((weights, slopes)):
                for position in range(8):
                    value = values[position] if position < ORDER else jnp.zeros_like(values[0])
                    for half in range(capacity // 128):
                        spline_ref[
                            2 * dimension + kind, half, pl.ds(slab * blocks * 8 + position, blocks, stride=8), :
                        ] = value[:, half * 128 : (half + 1) * 128]
        return carry

    lax.fori_loop(0, slabs, prepare, 0)

    def clear(plane, carry):
        grid_ref[plane] = jnp.zeros(grid_ref.shape[1:], jnp.float32)
        return carry

    lax.fori_loop(0, far, clear, 0)
    points = lax.broadcasted_iota(jnp.int32, (8, capacity), 0)

    def row_of(dimension, block):
        return jnp.broadcast_to(place_ref[dimension, pl.ds(block, 1), :], (8, capacity))

    def cyclic_tables(dimension, block, kinds):
        base = row_of(dimension, block)
        index = (points - base) & 7
        span = pl.ds(pl.multiple_of(block * 8, 8), 8)
        tables = []
        for kind in kinds:
            values = jnp.concatenate(
                [spline_ref[2 * dimension + kind, half, span, :] for half in range(capacity // 128)], axis=1
            )
            tables.append(jnp.take_along_axis(values, index, axis=0, mode="promise_in_bounds"))
        return base, points >= base, tables

    def z_tables(block, kinds):
        unused, own, tables = cyclic_tables(2, block, kinds)
        tile = row_of(3, block)
        tile = jnp.where(own, tile, (tile + 1) & (MESH_Z // 8 - 1)).astype(jnp.float32)
        tile = jnp.concatenate([tile, tile - 1.0], axis=0).astype(jnp.bfloat16)
        here = [tile == jnp.bfloat16(2 * index) for index in range(MESH_Z // 16)]
        results = []
        for table in tables:
            twice = jnp.concatenate([table, table], axis=0).astype(jnp.bfloat16)
            results.append(
                jnp.concatenate([jnp.where(mask, twice, jnp.zeros_like(twice)) for mask in here], axis=0)
            )
        return results

    def spread(slab, block):
        place = slab * blocks + block
        x_base, unused, (x_table,) = cyclic_tables(0, place, (0,))
        unused, y_own, (y_table,) = cyclic_tables(1, place, (0,))
        (z_table,) = z_tables(place, (0,))
        charge = jnp.broadcast_to(charge_ref[slab, pl.ds(block, 1), :], (8, capacity))
        x_place = jnp.concatenate([x_base, x_base], axis=0).astype(jnp.float32).astype(jnp.bfloat16)
        low, high = [], []
        for index in range(planes):
            product = (x_table[index : index + 1] * y_table) * charge
            pair = jnp.concatenate(
                [jnp.where(y_own, product, 0.0), jnp.where(y_own, 0.0, product)], axis=0
            ).astype(jnp.bfloat16)
            if index < border:
                own = x_place <= jnp.bfloat16(index)
                low.append(jnp.where(own, pair, jnp.zeros_like(pair)))
                high.append(jnp.where(own, jnp.zeros_like(pair), pair))
            else:
                low.append(pair)
        sums = dot32(jnp.concatenate(low + high, axis=0), z_table, 1)
        row_span = pl.ds(pl.multiple_of(block * rows, rows), frame)
        for index in range(extent):
            grid_ref[slab * planes + index, row_span, :] += sums[index * frame : (index + 1) * frame]

    def spread_step(step, carry):
        spread(step // blocks, step % blocks)
        return carry

    lax.fori_loop(0, slabs * blocks, spread_step, 0, unroll=16)

    for index in range(border):
        grid_ref[index] += grid_ref[MESH_X + index]

    right, left = right_ref[...], left_ref[...]

    def forward(step, carry):
        both = []
        for index in range(2):
            plane = 2 * step + index
            both.append(grid_ref[plane, 0:8, :] + grid_ref[plane, MESH_Y : MESH_Y + 8, :])
            both.append(grid_ref[plane, 8:MESH_Y, :])
        along_z = cas_lanes(jnp.concatenate(both, axis=0), right)
        along_y = cas_rows(
            jnp.concatenate([along_z[:MESH_Y], along_z[MESH_Y:]], axis=1), left
        )
        for index in range(2):
            turned_ref[pl.ds(2 * step + index, MESH_Y, stride=MESH_X), :] = along_y[
                :, index * MESH_Z : (index + 1) * MESH_Z
            ]
        return carry

    lax.fori_loop(0, MESH_X // 2, forward, 0, unroll=16)

    def filtering(step, carry):
        spans = [pl.ds(pl.multiple_of((2 * step + index) * MESH_X, MESH_X), MESH_X) for index in range(2)]
        lines = jnp.concatenate([turned_ref[span, :] for span in spans], axis=1)
        spectrum = cas_rows(lines, left)
        filters = []
        for index in range(2):
            total = square_ref[...] + y_square_ref[2 * step + index]
            positive = total > 0
            safe = jnp.where(positive, total, 1.0)
            filters.append(jnp.where(positive, pair_ref[...] * gain_ref[2 * step + index] / safe, 0.0))
        lines = cas_rows(spectrum * jnp.concatenate(filters, axis=1), left)
        for index, span in enumerate(spans):
            turned_ref[span, :] = lines[:, index * MESH_Z : (index + 1) * MESH_Z]
        return carry

    lax.fori_loop(0, MESH_Y // 2, filtering, 0, unroll=16)

    def backward(step, carry):
        both = jnp.concatenate(
            [turned_ref[pl.ds(2 * step + index, MESH_Y, stride=MESH_X), :] for index in range(2)], axis=1
        )
        along_y = cas_rows(both, left)
        field = cas_lanes(
            jnp.concatenate([along_y[:, :MESH_Z], along_y[:, MESH_Z:]], axis=0), right
        )
        for index in range(2):
            plane = field[index * MESH_Y : (index + 1) * MESH_Y]
            plane = jnp.concatenate([plane, plane[:8]], axis=0)
            for block in range(blocks):
                window_ref[2 * step + index, block] = plane[block * rows : block * rows + frame].astype(jnp.bfloat16)
        return carry

    lax.fori_loop(0, MESH_X // 2, backward, 0, unroll=16)

    for index in range(border):
        window_ref[MESH_X + index] = window_ref[index]

    def gather(slab, block):
        place = slab * blocks + block
        x_base, unused, (x_table, x_slope) = cyclic_tables(0, place, (0, 1))
        unused, y_own, (y_table, y_slope) = cyclic_tables(1, place, (0, 1))
        z_table, z_slope = z_tables(place, (0, 1))
        charge = charge_ref[slab, pl.ds(block, 1), :]
        window = jnp.concatenate(
            [window_ref[slab * planes + index, block] for index in range(extent)], axis=0
        )

        def chosen(near, index, own):
            def rows_of(plane):
                return jnp.where(
                    y_own, near[plane * frame : plane * frame + 8], near[plane * frame + 8 : plane * frame + 16]
                )

            if index < border:
                return jnp.where(own, rows_of(index), rows_of(planes + index))
            return rows_of(index)

        near = dot32(window, z_table)
        near_z = dot32(window, z_slope)
        plain = sloped = plain_z = 0.0
        for index in range(planes):
            own = x_base <= index
            part = chosen(near, index, own)
            plain += x_table[index : index + 1] * part
            sloped += x_slope[index : index + 1] * part
            plain_z += x_table[index : index + 1] * chosen(near_z, index, own)
        row = pl.ds(block, 1)
        out_ref[slab, 0, row, :] = jnp.sum(y_table * plain, axis=0, keepdims=True)
        out_ref[slab, 1, row, :] = -charge * jnp.sum(y_table * sloped, axis=0, keepdims=True)
        out_ref[slab, 2, row, :] = -charge * jnp.sum(y_slope * plain, axis=0, keepdims=True)
        out_ref[slab, 3, row, :] = -charge * jnp.sum(y_table * plain_z, axis=0, keepdims=True)

    def gather_step(step, carry):
        gather(step // blocks, step % blocks)
        return carry

    lax.fori_loop(0, slabs * blocks, gather_step, 0, unroll=16)


def channel_shards(charges, cell_offset, base_cell, counts, widths):
    device = lax.axis_index("wide")
    channels, slot_count = charges.shape
    blocks = counts.shape[0]
    capacity = slot_count // blocks
    slabs = lax.axis_size("wide")
    planes = MESH_X // slabs
    block_rows = MESH_Y // blocks
    live_mask = jnp.arange(capacity, dtype=jnp.int32)[None, :] < counts[:, None]
    charge_blocks = jnp.where(
        live_mask[None], charges.reshape(channels, blocks, capacity), jnp.zeros((), jnp.bfloat16)
    )
    bases = base_cell.reshape(3, blocks, capacity)
    row_start = jnp.arange(blocks, dtype=jnp.int32)[:, None] * block_rows
    packed = (bases[0] - device * planes) + 8 * (bases[1] - row_start) + 64 * bases[2]
    geometry = jnp.concatenate(
        [cell_offset.reshape(3, blocks, capacity), packed.astype(jnp.float32)[None]], axis=0
    )
    geometry = lax.all_gather(geometry, "wide", axis=0, tiled=False)
    charge_blocks = lax.all_to_all(charge_blocks, "wide", split_axis=0, concat_axis=0, tiled=True)

    width = lax.dynamic_index_in_dim(widths, device, keepdims=False)
    points = np.arange(MESH_X)
    folded_points = np.where(points * 2 > MESH_X, points - MESH_X, points) / MESH_X
    squares = (folded_points**2).astype(np.float32)
    first = np.array([1.0, 26.0, 66.0, 26.0, 1.0, 0.0]) / 120.0
    angles = 2.0 * math.pi * points[:, None] * np.arange(ORDER)[None, :] / MESH_X
    inverse = (1.0 / ((np.cos(angles) @ first) ** 2 + (np.sin(angles) @ first) ** 2)).astype(np.float32)
    gains = jnp.exp(-(math.pi**2) * squares / (width * width)) * inverse
    scale = 2.0 / (math.pi * MESH_X * MESH_Y * MESH_Z)
    pairs = gains[:, None] * (gains * scale)[None, :]
    pair_squares = squares[:, None] + squares[None, :]
    one, two = cas_terms(MESH_X)
    right = np.concatenate([np.concatenate([one, two], axis=1)] * 2, axis=0)
    left = np.concatenate([one, one, two], axis=1)

    whole = pl.BlockSpec(memory_space=pltpu.VMEM)
    scalars = pl.BlockSpec(memory_space=pltpu.SMEM)
    result = pl.pallas_call(
        channel_kernel,
        out_shape=jax.ShapeDtypeStruct((slabs, 4, blocks, capacity), jnp.float32),
        in_specs=[whole] * 4 + [scalars] * 2 + [whole] * 2,
        out_specs=whole,
        scratch_shapes=[
            pltpu.VMEM((MESH_X + ORDER - 1, MESH_Y + 8, MESH_Z), jnp.float32),
            pltpu.VMEM((MESH_X * MESH_Y, MESH_Z), jnp.float32),
            pltpu.VMEM((MESH_X + ORDER - 1, blocks, 16, MESH_Z), jnp.bfloat16),
            pltpu.VMEM((6, capacity // 128, slabs * blocks * 8, 128), jnp.float32),
            pltpu.VMEM((4, slabs * blocks, capacity), jnp.int32),
        ],
        compiler_params=pltpu.CompilerParams(vmem_limit_bytes=52 * 1024 * 1024),
        name="channel",
    )(
        geometry, charge_blocks.astype(jnp.float32), pairs, jnp.asarray(pair_squares), gains,
        jnp.asarray(squares), jnp.asarray(right), jnp.asarray(left),
    )
    returned = lax.all_to_all(result, "wide", split_axis=0, concat_axis=0, tiled=True)
    atom_potential = jnp.where(live_mask[None], returned[:, 0], 0.0).reshape(channels, slot_count)
    forces = jnp.sum(returned[:, 1:], axis=0).reshape(3, slot_count)
    return (atom_potential, forces)


def shards(charges, cell_offset, base_cell, counts, widths):
    if lax.axis_size("wide") == charges.shape[0] and MESH_X == 8 * lax.axis_size("wide"):
        return channel_shards(charges, cell_offset, base_cell, counts, widths)
    return slab_shards(charges, cell_offset, base_cell, counts, widths)


def solution(mesh):
    in_specs = (
        P(None, ("groups", "wide")),
        P(None, ("groups", "wide")),
        P(None, ("groups", "wide")),
        P(("groups", "wide")),
        P(),
    )
    out_specs = (P(None, ("groups", "wide")), P(None, ("groups", "wide")))
    return jax.shard_map(shards, mesh=mesh, in_specs=in_specs, out_specs=out_specs, check_vma=False)
```

```python
import functools
import math

import jax
import jax.numpy as jnp
import numpy as np
from jax import lax
from jax.experimental import pallas as pl
from jax.experimental.pallas import tpu as pltpu
from jax.sharding import PartitionSpec as P

MESH_X = 128
MESH_Y = 128
MESH_Z = 128
ORDER = 6


highest = lax.Precision.HIGHEST


def shifted(block, axis, distance):
    devices = range(lax.axis_size(axis))
    route = [((i - distance) % len(devices), i) for i in devices]
    return lax.ppermute(block, axis, route)


def spline_lists(offset, order_count):
    weights = [1.0 - offset, offset]
    slopes = [-jnp.ones_like(offset), jnp.ones_like(offset)]
    for degree in range(3, order_count + 1):
        if degree == order_count:
            slopes = (
                [-weights[0]]
                + [weights[position - 1] - weights[position] for position in range(1, degree - 1)]
                + [weights[degree - 2]]
            )
        factor = 1.0 / (degree - 1)
        updated = [None] * degree
        updated[degree - 1] = factor * offset * weights[degree - 2]
        for position in range(1, degree - 1):
            updated[degree - position - 1] = factor * (
                (offset + position) * weights[degree - position - 2]
                + (degree - position - offset) * weights[degree - position - 1]
            )
        updated[0] = factor * (1.0 - offset) * weights[0]
        weights = updated
    return (weights, slopes)


def spline_table(offset, order_count):
    weights, slopes = spline_lists(offset, order_count)
    return (jnp.stack(weights), jnp.stack(slopes))


def stencil_rows(weights, slopes, relative, extent, period):
    shifts = jnp.arange(weights.shape[0], dtype=jnp.int32)[None, :, None]
    targets = (relative[:, None, :] + shifts) % period
    points = jnp.arange(extent, dtype=jnp.int32)[None, :, None, None]
    matches = points == targets[:, None]
    plain_rows = jnp.sum(jnp.where(matches, jnp.moveaxis(weights, 0, 1)[:, None], 0.0), axis=2)
    slope_rows = jnp.sum(jnp.where(matches, jnp.moveaxis(slopes, 0, 1)[:, None], 0.0), axis=2)
    return (plain_rows, slope_rows)


def folded(points, length):
    values = jnp.where(points * 2 > length, points - length, points)
    return values.astype(jnp.float32) / length


def moduli(points, length):
    base_weights, base_slopes = spline_table(jnp.zeros((1,), jnp.float32), ORDER)
    shifts = jnp.arange(ORDER, dtype=jnp.int32)
    phases = points[:, None] * shifts[None, :] % length
    angles = phases.astype(jnp.float32) * (2.0 * math.pi / length)
    real_sum = jnp.sum(base_weights[:, 0][None, :] * jnp.cos(angles), axis=1)
    imag_sum = jnp.sum(base_weights[:, 0][None, :] * jnp.sin(angles), axis=1)
    return real_sum * real_sum + imag_sum * imag_sum


def kernel_table(widths, x_freq, y_freq, z_freq, x_mod, y_mod, z_mod):
    total = (
        x_freq[:, None, None, None] ** 2
        + y_freq[None, :, None, None] ** 2
        + z_freq[None, None, None, :] ** 2
    )
    positive = total > 0
    safe = jnp.where(positive, total, 1.0)
    beta = widths[None, None, :, None]
    divisor = x_mod[:, None, None, None] * y_mod[None, :, None, None] * z_mod[None, None, None, :]
    return jnp.where(
        positive,
        2.0 * jnp.exp(-math.pi**2 * total / (beta * beta)) / (math.pi * safe * divisor),
        0.0,
    )


def dft_tables(length):
    points = jnp.arange(length, dtype=jnp.int32)
    phases = points[:, None] * points[None, :] % length
    angles = phases.astype(jnp.float32) * (2.0 * math.pi / length)
    return (jnp.cos(angles), jnp.sin(angles))


def combine_blocks(block_grid, block_rows, border):
    owned = block_grid[:, :, :block_rows]
    overflow = jnp.roll(block_grid[:, :, block_rows:], 1, axis=0)
    owned = owned.at[:, :, :border].add(overflow)
    moved = jnp.moveaxis(owned, 0, 1)
    return moved.reshape((moved.shape[0], moved.shape[1] * moved.shape[2]) + moved.shape[3:])


def contract(data, x_weights, y_weights):
    return jnp.einsum("pycs,ps,ys->cs", data, x_weights, y_weights, precision=highest)


def turn(real_part, imag_part, cosines, sines, orient, pattern):

    def project(data, table):
        return jnp.einsum(pattern, data, table, precision=highest)

    real_out = project(real_part, cosines) - orient * project(imag_part, sines)
    imag_out = project(imag_part, cosines) + orient * project(real_part, sines)
    return jnp.stack([real_out, imag_out])


def slab_shards(charges, cell_offset, base_cell, counts, widths):
    wide_size = lax.axis_size("wide")
    device = lax.axis_index("wide")
    channels, slot_count = charges.shape
    blocks = counts.shape[0]
    capacity = slot_count // blocks
    planes = MESH_X // wide_size
    border = ORDER - 1
    extent = planes + border
    block_rows = MESH_Y // blocks
    y_extent = block_rows + border
    rounds = (border + planes - 1) // planes
    y_local = MESH_Y // wide_size
    live_mask = jnp.arange(capacity, dtype=jnp.int32)[None, :] < counts[:, None]
    charge_blocks = jnp.where(
        live_mask[:, None, :],
        jnp.moveaxis(charges.reshape(channels, blocks, capacity), 0, 1),
        jnp.zeros((), jnp.bfloat16),
    )
    offsets = cell_offset.reshape(3, blocks, capacity)
    bases = base_cell.reshape(3, blocks, capacity)
    x_weights, x_slopes = spline_table(offsets[0], ORDER)
    y_weights, y_slopes = spline_table(offsets[1], ORDER)
    z_weights, z_slopes = spline_table(offsets[2], ORDER)
    row_start = jnp.arange(blocks, dtype=jnp.int32)[:, None] * block_rows
    x_rows, x_drows = stencil_rows(x_weights, x_slopes, bases[0] - device * planes, extent, extent)
    y_rows, y_drows = stencil_rows(y_weights, y_slopes, bases[1] - row_start, y_extent, y_extent)
    z_plain, z_slope = stencil_rows(z_weights, z_slopes, bases[2], MESH_Z, MESH_Z)
    z_table = jnp.stack([z_plain, z_slope], axis=2).astype(jnp.bfloat16)

    def spread_block(inputs):
        x_block, y_block, charge_block, table_block = inputs
        products = (
            x_block[:, None, None, :]
            * y_block[None, :, None, :]
            * charge_block.astype(jnp.float32)[None, None]
        ).astype(jnp.bfloat16)
        spread = jnp.einsum(
            "rs,zs->rz",
            products.reshape(-1, capacity),
            table_block[:, 0],
            preferred_element_type=jnp.float32,
        )
        return spread.reshape(extent, y_extent, channels, MESH_Z)

    block_grid = lax.map(spread_block, (x_rows, y_rows, charge_blocks, z_table))
    grid_ext = combine_blocks(block_grid, block_rows, border)
    z_cos, z_sin = dft_tables(MESH_Z)
    y_cos, y_sin = dft_tables(MESH_Y)
    x_cos, x_sin = dft_tables(MESH_X)
    x_points = jnp.arange(MESH_X, dtype=jnp.int32)
    y_points = device * y_local + jnp.arange(y_local, dtype=jnp.int32)
    z_points = jnp.arange(MESH_Z, dtype=jnp.int32)
    kernel = kernel_table(
        widths,
        folded(x_points, MESH_X),
        folded(y_points, MESH_Y),
        folded(z_points, MESH_Z),
        moduli(x_points, MESH_X),
        moduli(y_points, MESH_Y),
        moduli(z_points, MESH_Z),
    )
    kernel = kernel / float(MESH_X * MESH_Y * MESH_Z)
    owned = grid_ext[:planes]
    for hop_index in range(1, rounds + 1):
        outgoing = grid_ext[hop_index * planes : (hop_index + 1) * planes]
        outgoing = jnp.pad(outgoing, ((0, planes - outgoing.shape[0]), (0, 0), (0, 0), (0, 0)))
        owned = owned + shifted(outgoing, "wide", hop_index)
    real_z = jnp.dot(owned, z_cos, precision=highest)
    imag_z = -jnp.dot(owned, z_sin, precision=highest)
    columns = lax.all_to_all(
        turn(real_z, imag_z, y_cos, y_sin, -1.0, "pycz,yk->pkcz"),
        "wide",
        split_axis=2,
        concat_axis=1,
        tiled=True,
    )
    spectrum = turn(columns[0], columns[1], x_cos, x_sin, -1.0, "xycz,xk->kycz")
    filtered = turn(spectrum[0] * kernel, spectrum[1] * kernel, x_cos, x_sin, 1.0, "xycz,xk->kycz")
    returned = lax.all_to_all(filtered, "wide", split_axis=1, concat_axis=2, tiled=True)
    along_y = turn(returned[0], returned[1], y_cos, y_sin, 1.0, "pycz,yk->pkcz")
    potential_own = (
        jnp.dot(along_y[0], z_cos, precision=highest)
        - jnp.dot(along_y[1], z_sin, precision=highest)
    ).astype(jnp.bfloat16)
    pieces = [potential_own]
    for hop_index in range(1, rounds + 1):
        pieces.append(shifted(potential_own, "wide", -hop_index))
    potential_ext = jnp.concatenate(pieces, axis=0)[:extent]
    blocked = potential_ext.reshape(extent, blocks, block_rows, channels, MESH_Z)
    following = jnp.roll(blocked[:, :, :border], -1, axis=1)
    windows = jnp.moveaxis(jnp.concatenate([blocked, following], axis=2), 1, 0)

    def gather_block(inputs):
        window, x_block, x_dblock, y_block, y_dblock, table_block, charge_block, live_block = inputs
        values = jnp.dot(
            window.reshape(-1, MESH_Z),
            table_block.reshape(MESH_Z, -1),
            preferred_element_type=jnp.float32,
        )
        values = values.reshape(extent, y_extent, channels, 2, capacity)
        direct = values[:, :, :, 0]
        sloped = values[:, :, :, 1]
        potential = jnp.where(live_block[None], contract(direct, x_block, y_block), 0.0)
        gradient = jnp.stack(
            [
                contract(direct, x_dblock, y_block),
                contract(direct, x_block, y_dblock),
                contract(sloped, x_block, y_block),
            ]
        )
        forces = -jnp.sum(gradient * charge_block.astype(jnp.float32)[None], axis=1)
        return (potential, forces)

    potentials, forces = lax.map(
        gather_block, (windows, x_rows, x_drows, y_rows, y_drows, z_table, charge_blocks, live_mask)
    )
    atom_potential = jnp.moveaxis(potentials, 0, 1).reshape(channels, slot_count)
    atom_forces = jnp.moveaxis(forces, 0, 1).reshape(3, slot_count)
    return (atom_potential, atom_forces)


def cas_terms(length):
    points = np.arange(length)
    angles = (points[:, None] * points[None, :] % length) * (2.0 * math.pi / length)
    left = (np.cos(angles) + np.sin(angles)).astype(np.float32)
    terms = []
    for _ in range(2):
        term = left.astype(jnp.bfloat16)
        terms.append(term)
        left = left - term.astype(np.float32)
    return terms


def split(values):
    first = values.astype(jnp.bfloat16)
    return first, (values - first.astype(jnp.float32)).astype(jnp.bfloat16)


def dot32(a, b, contract_b=0):
    return lax.dot_general(a, b, (((1,), (contract_b,)), ((), ())), preferred_element_type=jnp.float32)


def cas_lanes(values, right):
    sums = dot32(jnp.concatenate(split(values), axis=1), right)
    length = values.shape[1]
    return sums[:, :length] + sums[:, length:]


def cas_rows(values, left):
    first, second = split(values)
    return dot32(left, jnp.concatenate([first, second, first], axis=0))


def channel_kernel(
    offset_ref, base_ref, charge_ref, pair_ref, square_ref, order_ref, gain_ref, y_square_ref,
    right_ref, left_ref, out_ref,
    grid_ref, turned_ref, window_ref, spline_ref, place_ref,
):
    slabs, _, blocks, capacity = offset_ref.shape
    planes = MESH_X // slabs
    rows = MESH_Y // blocks
    border = ORDER - 1
    frame = 16
    extent = planes + border
    far = MESH_X + border

    def prepare(slab, carry):
        span = pl.ds(pl.multiple_of(slab * blocks, blocks), blocks)
        z_base = base_ref[slab, 2].astype(jnp.float32).astype(jnp.int32)
        for dimension in range(2):
            place_ref[dimension, span, :] = base_ref[slab, dimension].astype(jnp.float32).astype(jnp.int32)
        place_ref[2, span, :] = z_base & 7
        place_ref[3, span, :] = z_base >> 3
        for dimension in range(3):
            weights, slopes = spline_lists(offset_ref[slab, dimension], ORDER)
            for kind, values in enumerate((weights, slopes)):
                for position in range(8):
                    value = values[position] if position < ORDER else jnp.zeros_like(values[0])
                    for half in range(capacity // 128):
                        spline_ref[
                            2 * dimension + kind, half, pl.ds(slab * blocks * 8 + position, blocks, stride=8), :
                        ] = value[:, half * 128 : (half + 1) * 128]
        return carry

    lax.fori_loop(0, slabs, prepare, 0)

    def clear(plane, carry):
        grid_ref[plane] = jnp.zeros(grid_ref.shape[1:], jnp.float32)
        return carry

    lax.fori_loop(0, far, clear, 0)
    points = lax.broadcasted_iota(jnp.int32, (8, capacity), 0)

    def row_of(dimension, block):
        return jnp.broadcast_to(place_ref[dimension, pl.ds(block, 1), :], (8, capacity))

    def cyclic_tables(dimension, block, kinds):
        base = row_of(dimension, block)
        index = (points - base) & 7
        span = pl.ds(pl.multiple_of(block * 8, 8), 8)
        tables = []
        for kind in kinds:
            values = jnp.concatenate(
                [spline_ref[2 * dimension + kind, half, span, :] for half in range(capacity // 128)], axis=1
            )
            tables.append(jnp.take_along_axis(values, index, axis=0, mode="promise_in_bounds"))
        return base, points >= base, tables

    def z_tables(block, kinds):
        unused, own, tables = cyclic_tables(2, block, kinds)
        tile = row_of(3, block)
        tile = jnp.where(own, tile, (tile + 1) & (MESH_Z // 8 - 1)).astype(jnp.float32)
        tile = jnp.concatenate([tile, tile - 1.0], axis=0).astype(jnp.bfloat16)
        here = [tile == jnp.bfloat16(2 * index) for index in range(MESH_Z // 16)]
        results = []
        for table in tables:
            twice = jnp.concatenate([table, table], axis=0).astype(jnp.bfloat16)
            results.append(
                jnp.concatenate([jnp.where(mask, twice, jnp.zeros_like(twice)) for mask in here], axis=0)
            )
        return results

    def spread(turn_index, block):
        place = turn_index * blocks + block
        slab = order_ref[turn_index]
        x_base, unused, (x_table,) = cyclic_tables(0, place, (0,))
        unused, y_own, (y_table,) = cyclic_tables(1, place, (0,))
        (z_table,) = z_tables(place, (0,))
        charge = jnp.broadcast_to(charge_ref[turn_index, pl.ds(block, 1), :], (8, capacity))
        x_place = jnp.concatenate([x_base, x_base], axis=0).astype(jnp.float32).astype(jnp.bfloat16)
        low, high = [], []
        for index in range(planes):
            product = (x_table[index : index + 1] * y_table) * charge
            pair = jnp.concatenate(
                [jnp.where(y_own, product, 0.0), jnp.where(y_own, 0.0, product)], axis=0
            ).astype(jnp.bfloat16)
            if index < border:
                own = x_place <= jnp.bfloat16(index)
                low.append(jnp.where(own, pair, jnp.zeros_like(pair)))
                high.append(jnp.where(own, jnp.zeros_like(pair), pair))
            else:
                low.append(pair)
        sums = dot32(jnp.concatenate(low + high, axis=0), z_table, 1)
        row_span = pl.ds(pl.multiple_of(block * rows, rows), frame)
        for index in range(extent):
            grid_ref[slab * planes + index, row_span, :] += sums[index * frame : (index + 1) * frame]

    def spread_step(step, carry):
        spread(step // blocks, step % blocks)
        return carry

    lax.fori_loop(0, slabs * blocks, spread_step, 0, unroll=16)

    for index in range(border):
        grid_ref[index] += grid_ref[MESH_X + index]

    right, left = right_ref[...], left_ref[...]

    def forward(step, carry):
        both = []
        for index in range(2):
            plane = 2 * step + index
            both.append(grid_ref[plane, 0:8, :] + grid_ref[plane, MESH_Y : MESH_Y + 8, :])
            both.append(grid_ref[plane, 8:MESH_Y, :])
        along_z = cas_lanes(jnp.concatenate(both, axis=0), right)
        along_y = cas_rows(
            jnp.concatenate([along_z[:MESH_Y], along_z[MESH_Y:]], axis=1), left
        )
        for index in range(2):
            turned_ref[pl.ds(2 * step + index, MESH_Y, stride=MESH_X), :] = along_y[
                :, index * MESH_Z : (index + 1) * MESH_Z
            ]
        return carry

    lax.fori_loop(0, MESH_X // 2, forward, 0, unroll=16)

    def filtering(step, carry):
        spans = [pl.ds(pl.multiple_of((2 * step + index) * MESH_X, MESH_X), MESH_X) for index in range(2)]
        lines = jnp.concatenate([turned_ref[span, :] for span in spans], axis=1)
        spectrum = cas_rows(lines, left)
        filters = []
        for index in range(2):
            total = square_ref[...] + y_square_ref[2 * step + index]
            positive = total > 0
            safe = jnp.where(positive, total, 1.0)
            filters.append(jnp.where(positive, pair_ref[...] * gain_ref[2 * step + index] / safe, 0.0))
        lines = cas_rows(spectrum * jnp.concatenate(filters, axis=1), left)
        for index, span in enumerate(spans):
            turned_ref[span, :] = lines[:, index * MESH_Z : (index + 1) * MESH_Z]
        return carry

    lax.fori_loop(0, MESH_Y // 2, filtering, 0, unroll=16)

    def backward(step, carry):
        both = jnp.concatenate(
            [turned_ref[pl.ds(2 * step + index, MESH_Y, stride=MESH_X), :] for index in range(2)], axis=1
        )
        along_y = cas_rows(both, left)
        field = cas_lanes(
            jnp.concatenate([along_y[:, :MESH_Z], along_y[:, MESH_Z:]], axis=0), right
        )
        for index in range(2):
            plane = field[index * MESH_Y : (index + 1) * MESH_Y]
            plane = jnp.concatenate([plane, plane[:8]], axis=0)
            for block in range(blocks):
                window_ref[2 * step + index, block] = plane[block * rows : block * rows + frame].astype(jnp.bfloat16)
        return carry

    lax.fori_loop(0, MESH_X // 2, backward, 0, unroll=16)

    for index in range(border):
        window_ref[MESH_X + index] = window_ref[index]

    def gather(turn_index, block):
        place = turn_index * blocks + block
        slab = order_ref[turn_index]
        x_base, unused, (x_table, x_slope) = cyclic_tables(0, place, (0, 1))
        unused, y_own, (y_table, y_slope) = cyclic_tables(1, place, (0, 1))
        z_table, z_slope = z_tables(place, (0, 1))
        charge = charge_ref[turn_index, pl.ds(block, 1), :]
        window = jnp.concatenate(
            [window_ref[slab * planes + index, block] for index in range(extent)], axis=0
        )

        def chosen(near, index, own):
            def rows_of(plane):
                return jnp.where(
                    y_own, near[plane * frame : plane * frame + 8], near[plane * frame + 8 : plane * frame + 16]
                )

            if index < border:
                return jnp.where(own, rows_of(index), rows_of(planes + index))
            return rows_of(index)

        near = dot32(window, z_table)
        near_z = dot32(window, z_slope)
        plain = sloped = plain_z = 0.0
        for index in range(planes):
            own = x_base <= index
            part = chosen(near, index, own)
            plain += x_table[index : index + 1] * part
            sloped += x_slope[index : index + 1] * part
            plain_z += x_table[index : index + 1] * chosen(near_z, index, own)
        row = pl.ds(block, 1)
        out_ref[slab, 0, row, :] = jnp.sum(y_table * plain, axis=0, keepdims=True)
        out_ref[slab, 1, row, :] = -charge * jnp.sum(y_table * sloped, axis=0, keepdims=True)
        out_ref[slab, 2, row, :] = -charge * jnp.sum(y_slope * plain, axis=0, keepdims=True)
        out_ref[slab, 3, row, :] = -charge * jnp.sum(y_table * plain_z, axis=0, keepdims=True)

    def gather_step(step, carry):
        gather(step // blocks, step % blocks)
        return carry

    lax.fori_loop(0, slabs * blocks, gather_step, 0, unroll=16)


def channel_shards(charges, cell_offset, base_cell, counts, widths):
    device = lax.axis_index("wide")
    channels, slot_count = charges.shape
    blocks = counts.shape[0]
    capacity = slot_count // blocks
    slabs = lax.axis_size("wide")
    planes = MESH_X // slabs
    block_rows = MESH_Y // blocks
    live_mask = jnp.arange(capacity, dtype=jnp.int32)[None, :] < counts[:, None]
    charge_blocks = jnp.where(
        live_mask[None], charges.reshape(channels, blocks, capacity), jnp.zeros((), jnp.bfloat16)
    )
    bases = base_cell.reshape(3, blocks, capacity)
    row_start = jnp.arange(blocks, dtype=jnp.int32)[:, None] * block_rows
    cells = jnp.stack([bases[0] - device * planes, bases[1] - row_start, bases[2]]).astype(jnp.bfloat16)
    offsets = cell_offset.reshape(1, 3, blocks, capacity)
    cells = cells[None]
    parts = charge_blocks[None]
    order = jnp.zeros((1,), jnp.int32)
    distance = slabs // 2
    while distance > 0:
        route = [(index, index ^ distance) for index in range(slabs)]
        upper = (device & distance) > 0
        first, second = parts[:, :distance], parts[:, distance:]
        kept, sent = jnp.where(upper, second, first), jnp.where(upper, first, second)
        offsets = jnp.concatenate([offsets, lax.ppermute(offsets, "wide", route)], axis=0)
        count = cells.shape[0]
        bundle = jnp.concatenate([cells.reshape((-1,) + cells.shape[2:]), sent.reshape((-1,) + sent.shape[2:])], axis=0)
        bundle = lax.ppermute(bundle, "wide", route)
        cells = jnp.concatenate([cells, bundle[: 3 * count].reshape(cells.shape)], axis=0)
        parts = jnp.concatenate([kept, bundle[3 * count :].reshape(kept.shape)], axis=0)
        order = jnp.concatenate([order, order ^ distance])
        distance //= 2
    charge_blocks = parts[:, 0]
    order = order ^ device

    width = lax.dynamic_index_in_dim(widths, device, keepdims=False)
    points = np.arange(MESH_X)
    folded_points = np.where(points * 2 > MESH_X, points - MESH_X, points) / MESH_X
    squares = (folded_points**2).astype(np.float32)
    first = np.array([1.0, 26.0, 66.0, 26.0, 1.0, 0.0]) / 120.0
    angles = 2.0 * math.pi * points[:, None] * np.arange(ORDER)[None, :] / MESH_X
    inverse = (1.0 / ((np.cos(angles) @ first) ** 2 + (np.sin(angles) @ first) ** 2)).astype(np.float32)
    gains = jnp.exp(-(math.pi**2) * squares / (width * width)) * inverse
    scale = 2.0 / (math.pi * MESH_X * MESH_Y * MESH_Z)
    pairs = gains[:, None] * (gains * scale)[None, :]
    pair_squares = squares[:, None] + squares[None, :]
    one, two = cas_terms(MESH_X)
    right = np.concatenate([np.concatenate([one, two], axis=1)] * 2, axis=0)
    left = np.concatenate([one, one, two], axis=1)

    whole = pl.BlockSpec(memory_space=pltpu.VMEM)
    scalars = pl.BlockSpec(memory_space=pltpu.SMEM)
    result = pl.pallas_call(
        channel_kernel,
        out_shape=jax.ShapeDtypeStruct((slabs, 4, blocks, capacity), jnp.float32),
        in_specs=[whole] * 5 + [scalars] * 3 + [whole] * 2,
        out_specs=whole,
        scratch_shapes=[
            pltpu.VMEM((MESH_X + ORDER - 1, MESH_Y + 8, MESH_Z), jnp.float32),
            pltpu.VMEM((MESH_X * MESH_Y, MESH_Z), jnp.float32),
            pltpu.VMEM((MESH_X + ORDER - 1, blocks, 16, MESH_Z), jnp.bfloat16),
            pltpu.VMEM((6, capacity // 128, slabs * blocks * 8, 128), jnp.float32),
            pltpu.VMEM((4, slabs * blocks, capacity), jnp.int32),
        ],
        compiler_params=pltpu.CompilerParams(vmem_limit_bytes=52 * 1024 * 1024),
        name="channel",
    )(
        offsets, cells, charge_blocks.astype(jnp.float32), pairs, jnp.asarray(pair_squares), order, gains,
        jnp.asarray(squares), jnp.asarray(right), jnp.asarray(left),
    )
    returned = lax.all_to_all(result, "wide", split_axis=0, concat_axis=0, tiled=True)
    atom_potential = jnp.where(live_mask[None], returned[:, 0], 0.0).reshape(channels, slot_count)
    forces = jnp.sum(returned[:, 1:], axis=0).reshape(3, slot_count)
    return (atom_potential, forces)


def shards(charges, cell_offset, base_cell, counts, widths):
    if lax.axis_size("wide") == charges.shape[0] and MESH_X == 8 * lax.axis_size("wide"):
        return channel_shards(charges, cell_offset, base_cell, counts, widths)
    return slab_shards(charges, cell_offset, base_cell, counts, widths)


def solution(mesh):
    in_specs = (
        P(None, ("groups", "wide")),
        P(None, ("groups", "wide")),
        P(None, ("groups", "wide")),
        P(("groups", "wide")),
        P(),
    )
    out_specs = (P(None, ("groups", "wide")), P(None, ("groups", "wide")))
    return jax.shard_map(shards, mesh=mesh, in_specs=in_specs, out_specs=out_specs, check_vma=False)
```

```python
import functools
import math

import jax
import jax.numpy as jnp
import numpy as np
from jax import lax
from jax.experimental import pallas as pl
from jax.experimental.pallas import tpu as pltpu
from jax.sharding import PartitionSpec as P

MESH_X = 128
MESH_Y = 128
MESH_Z = 128
ORDER = 6


highest = lax.Precision.HIGHEST


def shifted(block, axis, distance):
    devices = range(lax.axis_size(axis))
    route = [((i - distance) % len(devices), i) for i in devices]
    return lax.ppermute(block, axis, route)


def spline_lists(offset, order_count):
    weights = [1.0 - offset, offset]
    slopes = [-jnp.ones_like(offset), jnp.ones_like(offset)]
    for degree in range(3, order_count + 1):
        if degree == order_count:
            slopes = (
                [-weights[0]]
                + [weights[position - 1] - weights[position] for position in range(1, degree - 1)]
                + [weights[degree - 2]]
            )
        factor = 1.0 / (degree - 1)
        updated = [None] * degree
        updated[degree - 1] = factor * offset * weights[degree - 2]
        for position in range(1, degree - 1):
            updated[degree - position - 1] = factor * (
                (offset + position) * weights[degree - position - 2]
                + (degree - position - offset) * weights[degree - position - 1]
            )
        updated[0] = factor * (1.0 - offset) * weights[0]
        weights = updated
    return (weights, slopes)


def spline_table(offset, order_count):
    weights, slopes = spline_lists(offset, order_count)
    return (jnp.stack(weights), jnp.stack(slopes))


def stencil_rows(weights, slopes, relative, extent, period):
    shifts = jnp.arange(weights.shape[0], dtype=jnp.int32)[None, :, None]
    targets = (relative[:, None, :] + shifts) % period
    points = jnp.arange(extent, dtype=jnp.int32)[None, :, None, None]
    matches = points == targets[:, None]
    plain_rows = jnp.sum(jnp.where(matches, jnp.moveaxis(weights, 0, 1)[:, None], 0.0), axis=2)
    slope_rows = jnp.sum(jnp.where(matches, jnp.moveaxis(slopes, 0, 1)[:, None], 0.0), axis=2)
    return (plain_rows, slope_rows)


def folded(points, length):
    values = jnp.where(points * 2 > length, points - length, points)
    return values.astype(jnp.float32) / length


def moduli(points, length):
    base_weights, base_slopes = spline_table(jnp.zeros((1,), jnp.float32), ORDER)
    shifts = jnp.arange(ORDER, dtype=jnp.int32)
    phases = points[:, None] * shifts[None, :] % length
    angles = phases.astype(jnp.float32) * (2.0 * math.pi / length)
    real_sum = jnp.sum(base_weights[:, 0][None, :] * jnp.cos(angles), axis=1)
    imag_sum = jnp.sum(base_weights[:, 0][None, :] * jnp.sin(angles), axis=1)
    return real_sum * real_sum + imag_sum * imag_sum


def kernel_table(widths, x_freq, y_freq, z_freq, x_mod, y_mod, z_mod):
    total = (
        x_freq[:, None, None, None] ** 2
        + y_freq[None, :, None, None] ** 2
        + z_freq[None, None, None, :] ** 2
    )
    positive = total > 0
    safe = jnp.where(positive, total, 1.0)
    beta = widths[None, None, :, None]
    divisor = x_mod[:, None, None, None] * y_mod[None, :, None, None] * z_mod[None, None, None, :]
    return jnp.where(
        positive,
        2.0 * jnp.exp(-math.pi**2 * total / (beta * beta)) / (math.pi * safe * divisor),
        0.0,
    )


def dft_tables(length):
    points = jnp.arange(length, dtype=jnp.int32)
    phases = points[:, None] * points[None, :] % length
    angles = phases.astype(jnp.float32) * (2.0 * math.pi / length)
    return (jnp.cos(angles), jnp.sin(angles))


def combine_blocks(block_grid, block_rows, border):
    owned = block_grid[:, :, :block_rows]
    overflow = jnp.roll(block_grid[:, :, block_rows:], 1, axis=0)
    owned = owned.at[:, :, :border].add(overflow)
    moved = jnp.moveaxis(owned, 0, 1)
    return moved.reshape((moved.shape[0], moved.shape[1] * moved.shape[2]) + moved.shape[3:])


def contract(data, x_weights, y_weights):
    return jnp.einsum("pycs,ps,ys->cs", data, x_weights, y_weights, precision=highest)


def turn(real_part, imag_part, cosines, sines, orient, pattern):

    def project(data, table):
        return jnp.einsum(pattern, data, table, precision=highest)

    real_out = project(real_part, cosines) - orient * project(imag_part, sines)
    imag_out = project(imag_part, cosines) + orient * project(real_part, sines)
    return jnp.stack([real_out, imag_out])


def slab_shards(charges, cell_offset, base_cell, counts, widths):
    wide_size = lax.axis_size("wide")
    device = lax.axis_index("wide")
    channels, slot_count = charges.shape
    blocks = counts.shape[0]
    capacity = slot_count // blocks
    planes = MESH_X // wide_size
    border = ORDER - 1
    extent = planes + border
    block_rows = MESH_Y // blocks
    y_extent = block_rows + border
    rounds = (border + planes - 1) // planes
    y_local = MESH_Y // wide_size
    live_mask = jnp.arange(capacity, dtype=jnp.int32)[None, :] < counts[:, None]
    charge_blocks = jnp.where(
        live_mask[:, None, :],
        jnp.moveaxis(charges.reshape(channels, blocks, capacity), 0, 1),
        jnp.zeros((), jnp.bfloat16),
    )
    offsets = cell_offset.reshape(3, blocks, capacity)
    bases = base_cell.reshape(3, blocks, capacity)
    x_weights, x_slopes = spline_table(offsets[0], ORDER)
    y_weights, y_slopes = spline_table(offsets[1], ORDER)
    z_weights, z_slopes = spline_table(offsets[2], ORDER)
    row_start = jnp.arange(blocks, dtype=jnp.int32)[:, None] * block_rows
    x_rows, x_drows = stencil_rows(x_weights, x_slopes, bases[0] - device * planes, extent, extent)
    y_rows, y_drows = stencil_rows(y_weights, y_slopes, bases[1] - row_start, y_extent, y_extent)
    z_plain, z_slope = stencil_rows(z_weights, z_slopes, bases[2], MESH_Z, MESH_Z)
    z_table = jnp.stack([z_plain, z_slope], axis=2).astype(jnp.bfloat16)

    def spread_block(inputs):
        x_block, y_block, charge_block, table_block = inputs
        products = (
            x_block[:, None, None, :]
            * y_block[None, :, None, :]
            * charge_block.astype(jnp.float32)[None, None]
        ).astype(jnp.bfloat16)
        spread = jnp.einsum(
            "rs,zs->rz",
            products.reshape(-1, capacity),
            table_block[:, 0],
            preferred_element_type=jnp.float32,
        )
        return spread.reshape(extent, y_extent, channels, MESH_Z)

    block_grid = lax.map(spread_block, (x_rows, y_rows, charge_blocks, z_table))
    grid_ext = combine_blocks(block_grid, block_rows, border)
    z_cos, z_sin = dft_tables(MESH_Z)
    y_cos, y_sin = dft_tables(MESH_Y)
    x_cos, x_sin = dft_tables(MESH_X)
    x_points = jnp.arange(MESH_X, dtype=jnp.int32)
    y_points = device * y_local + jnp.arange(y_local, dtype=jnp.int32)
    z_points = jnp.arange(MESH_Z, dtype=jnp.int32)
    kernel = kernel_table(
        widths,
        folded(x_points, MESH_X),
        folded(y_points, MESH_Y),
        folded(z_points, MESH_Z),
        moduli(x_points, MESH_X),
        moduli(y_points, MESH_Y),
        moduli(z_points, MESH_Z),
    )
    kernel = kernel / float(MESH_X * MESH_Y * MESH_Z)
    owned = grid_ext[:planes]
    for hop_index in range(1, rounds + 1):
        outgoing = grid_ext[hop_index * planes : (hop_index + 1) * planes]
        outgoing = jnp.pad(outgoing, ((0, planes - outgoing.shape[0]), (0, 0), (0, 0), (0, 0)))
        owned = owned + shifted(outgoing, "wide", hop_index)
    real_z = jnp.dot(owned, z_cos, precision=highest)
    imag_z = -jnp.dot(owned, z_sin, precision=highest)
    columns = lax.all_to_all(
        turn(real_z, imag_z, y_cos, y_sin, -1.0, "pycz,yk->pkcz"),
        "wide",
        split_axis=2,
        concat_axis=1,
        tiled=True,
    )
    spectrum = turn(columns[0], columns[1], x_cos, x_sin, -1.0, "xycz,xk->kycz")
    filtered = turn(spectrum[0] * kernel, spectrum[1] * kernel, x_cos, x_sin, 1.0, "xycz,xk->kycz")
    returned = lax.all_to_all(filtered, "wide", split_axis=1, concat_axis=2, tiled=True)
    along_y = turn(returned[0], returned[1], y_cos, y_sin, 1.0, "pycz,yk->pkcz")
    potential_own = (
        jnp.dot(along_y[0], z_cos, precision=highest)
        - jnp.dot(along_y[1], z_sin, precision=highest)
    ).astype(jnp.bfloat16)
    pieces = [potential_own]
    for hop_index in range(1, rounds + 1):
        pieces.append(shifted(potential_own, "wide", -hop_index))
    potential_ext = jnp.concatenate(pieces, axis=0)[:extent]
    blocked = potential_ext.reshape(extent, blocks, block_rows, channels, MESH_Z)
    following = jnp.roll(blocked[:, :, :border], -1, axis=1)
    windows = jnp.moveaxis(jnp.concatenate([blocked, following], axis=2), 1, 0)

    def gather_block(inputs):
        window, x_block, x_dblock, y_block, y_dblock, table_block, charge_block, live_block = inputs
        values = jnp.dot(
            window.reshape(-1, MESH_Z),
            table_block.reshape(MESH_Z, -1),
            preferred_element_type=jnp.float32,
        )
        values = values.reshape(extent, y_extent, channels, 2, capacity)
        direct = values[:, :, :, 0]
        sloped = values[:, :, :, 1]
        potential = jnp.where(live_block[None], contract(direct, x_block, y_block), 0.0)
        gradient = jnp.stack(
            [
                contract(direct, x_dblock, y_block),
                contract(direct, x_block, y_dblock),
                contract(sloped, x_block, y_block),
            ]
        )
        forces = -jnp.sum(gradient * charge_block.astype(jnp.float32)[None], axis=1)
        return (potential, forces)

    potentials, forces = lax.map(
        gather_block, (windows, x_rows, x_drows, y_rows, y_drows, z_table, charge_blocks, live_mask)
    )
    atom_potential = jnp.moveaxis(potentials, 0, 1).reshape(channels, slot_count)
    atom_forces = jnp.moveaxis(forces, 0, 1).reshape(3, slot_count)
    return (atom_potential, atom_forces)


def cas_terms(length):
    points = np.arange(length)
    angles = (points[:, None] * points[None, :] % length) * (2.0 * math.pi / length)
    left = (np.cos(angles) + np.sin(angles)).astype(np.float32)
    terms = []
    for _ in range(2):
        term = left.astype(jnp.bfloat16)
        terms.append(term)
        left = left - term.astype(np.float32)
    return terms


def split(values):
    first = values.astype(jnp.bfloat16)
    return first, (values - first.astype(jnp.float32)).astype(jnp.bfloat16)


def dot32(a, b, contract_b=0):
    return lax.dot_general(a, b, (((1,), (contract_b,)), ((), ())), preferred_element_type=jnp.float32)


def cas_lanes(values, right):
    sums = dot32(jnp.concatenate(split(values), axis=1), right)
    length = values.shape[1]
    return sums[:, :length] + sums[:, length:]


def cas_rows(values, left):
    first, second = split(values)
    return dot32(left, jnp.concatenate([first, second, first], axis=0))


def level_of(largest):
    logarithm = jnp.log(jnp.maximum(largest, 1e-36)) * (1.0 / math.log(2.0))
    level = jnp.floor(logarithm + 1e-3).astype(jnp.int32) + 1 - 15 + 126
    return jnp.clip(level, 0, 250)


def power_of_two(level, sign):
    value = jnp.full(level.shape, 2.0 ** (-126 * sign), jnp.float32)
    for bit in range(7):
        value = value * jnp.where((level >> bit) & 1 > 0, 2.0 ** (sign * 2**bit), 1.0)
    return value * jnp.where((level >> 7) & 1 > 0, 2.0 ** (sign * 64), 1.0) * jnp.where((level >> 7) & 1 > 0, 2.0 ** (sign * 64), 1.0)


def channel_kernel(
    offset_ref, base_ref, charge_ref, far_offset_ref, far_ref, inverse_hbm, order_ref, widths_ref,
    right_hbm, left_hbm, out_ref,
    grid_ref, turned_ref, window_ref, spline_ref, place_ref, pair_ref, gain_ref, value_ref, charged_ref,
    inverse_ref, right_ref, left_ref, inverse_done, right_done, left_done,
):
    near, _, blocks, capacity = offset_ref.shape
    slabs = 2 * near
    planes = MESH_X // slabs
    rows = MESH_Y // blocks
    border = ORDER - 1
    frame = 16
    extent = planes + border
    far = MESH_X + border

    loads = [
        pltpu.make_async_copy(inverse_hbm, inverse_ref, inverse_done),
        pltpu.make_async_copy(right_hbm, right_ref, right_done),
        pltpu.make_async_copy(left_hbm, left_ref, left_done),
    ]
    for load in loads:
        load.start()

    def prepare(slab, offset_at, base_at, charge):
        span = pl.ds(pl.multiple_of(slab * blocks, blocks), blocks)
        charged_ref[slab] = charge.astype(jnp.float32)
        bases = [base_at(dimension).astype(jnp.float32).astype(jnp.int32) for dimension in range(3)]
        place_ref[0, span, :] = bases[0] & 7
        place_ref[1, span, :] = bases[1] & 7
        place_ref[2, span, :] = bases[2] & 7
        place_ref[3, span, :] = bases[2] >> 3
        for dimension in range(3):
            weights, slopes = spline_lists(offset_at(dimension), ORDER)
            for kind, values in enumerate((weights, slopes)):
                for position in range(8):
                    value = values[position] if position < ORDER else jnp.zeros_like(values[0])
                    for half in range(capacity // 128):
                        spline_ref[
                            2 * dimension + kind, half, pl.ds(slab * blocks * 8 + position, blocks, stride=8), :
                        ] = value[:, half * 128 : (half + 1) * 128]

    def prepare_both(index, carry):
        prepare(
            index,
            lambda dimension: offset_ref[index, dimension],
            lambda dimension: base_ref[index, dimension],
            charge_ref[index],
        )
        prepare(
            near + index,
            lambda dimension: far_offset_ref[index, dimension],
            lambda dimension: far_ref[3 * index + dimension],
            far_ref[3 * near + index],
        )
        return carry

    lax.fori_loop(0, near, prepare_both, 0)

    def clear(plane, carry):
        grid_ref[plane] = jnp.zeros(grid_ref.shape[1:], jnp.float32)
        return carry

    lax.fori_loop(0, far, clear, 0)
    points = lax.broadcasted_iota(jnp.int32, (8, capacity), 0)

    def row_of(dimension, block):
        return jnp.broadcast_to(place_ref[dimension, pl.ds(block, 1), :], (8, capacity))

    def cyclic_tables(dimension, block, kinds):
        base = row_of(dimension, block)
        index = (points - base) & 7
        span = pl.ds(pl.multiple_of(block * 8, 8), 8)
        tables = []
        for kind in kinds:
            values = jnp.concatenate(
                [spline_ref[2 * dimension + kind, half, span, :] for half in range(capacity // 128)], axis=1
            )
            tables.append(jnp.take_along_axis(values, index, axis=0, mode="promise_in_bounds"))
        return base, points >= base, tables

    def z_tables(block, kinds):
        unused, own, tables = cyclic_tables(2, block, kinds)
        tile = row_of(3, block)
        tile = jnp.where(own, tile, (tile + 1) & (MESH_Z // 8 - 1)).astype(jnp.float32)
        tile = jnp.concatenate([tile, tile - 1.0], axis=0).astype(jnp.bfloat16)
        here = [tile == jnp.bfloat16(2 * index) for index in range(MESH_Z // 16)]
        results = []
        for table in tables:
            twice = jnp.concatenate([table, table], axis=0).astype(jnp.bfloat16)
            results.append(
                jnp.concatenate([jnp.where(mask, twice, jnp.zeros_like(twice)) for mask in here], axis=0)
            )
        return results

    def spread(turn_index, block):
        place = turn_index * blocks + block
        slab = order_ref[turn_index]
        x_base, unused, (x_table,) = cyclic_tables(0, place, (0,))
        unused, y_own, (y_table,) = cyclic_tables(1, place, (0,))
        (z_table,) = z_tables(place, (0,))
        charge = jnp.broadcast_to(charged_ref[turn_index, pl.ds(block, 1), :], (8, capacity))
        x_place = jnp.concatenate([x_base, x_base], axis=0).astype(jnp.float32).astype(jnp.bfloat16)
        low, high = [], []
        for index in range(planes):
            product = (x_table[index : index + 1] * y_table) * charge
            pair = jnp.concatenate(
                [jnp.where(y_own, product, 0.0), jnp.where(y_own, 0.0, product)], axis=0
            ).astype(jnp.bfloat16)
            if index < border:
                own = x_place <= jnp.bfloat16(index)
                low.append(jnp.where(own, pair, jnp.zeros_like(pair)))
                high.append(jnp.where(own, jnp.zeros_like(pair), pair))
            else:
                low.append(pair)
        sums = dot32(jnp.concatenate(low + high, axis=0), z_table, 1)
        row_span = pl.ds(pl.multiple_of(block * rows, rows), frame)
        for index in range(extent):
            grid_ref[slab * planes + index, row_span, :] += sums[index * frame : (index + 1) * frame]

    def spread_step(step, carry):
        spread(step // blocks, step % blocks)
        return carry

    lax.fori_loop(0, slabs * blocks, spread_step, 0, unroll=16)

    for index in range(border):
        grid_ref[index] += grid_ref[MESH_X + index]

    for load in loads:
        load.wait()
    right, left = right_ref[...], left_ref[...]
    width = widths_ref[order_ref[0]]

    def squares(dimension):
        index = lax.broadcasted_iota(jnp.int32, (MESH_X, MESH_Z), dimension)
        index = jnp.where(index * 2 > MESH_X, index - MESH_X, index).astype(jnp.float32) / MESH_X
        return index * index

    across, along = squares(0), squares(1)
    decay = -(math.pi**2) / (width * width)
    gain_ref[...] = jnp.exp(decay * across) * inverse_ref[0]
    scale = 2.0 / (math.pi * MESH_X * MESH_Y * MESH_Z)
    pair_ref[0] = gain_ref[...] * (jnp.exp(decay * along) * (inverse_ref[1] * scale))
    pair_ref[1] = across + along

    def forward(step, carry):
        both = []
        for index in range(2):
            plane = 2 * step + index
            both.append(grid_ref[plane, 0:8, :] + grid_ref[plane, MESH_Y : MESH_Y + 8, :])
            both.append(grid_ref[plane, 8:MESH_Y, :])
        along_z = cas_lanes(jnp.concatenate(both, axis=0), right)
        along_y = cas_rows(
            jnp.concatenate([along_z[:MESH_Y], along_z[MESH_Y:]], axis=1), left
        )
        for index in range(2):
            turned_ref[pl.ds(2 * step + index, MESH_Y, stride=MESH_X), :] = along_y[
                :, index * MESH_Z : (index + 1) * MESH_Z
            ]
        return carry

    lax.fori_loop(0, MESH_X // 2, forward, 0, unroll=16)

    def filtering(step, carry):
        spans = [pl.ds(pl.multiple_of((2 * step + index) * MESH_X, MESH_X), MESH_X) for index in range(2)]
        lines = jnp.concatenate([turned_ref[span, :] for span in spans], axis=1)
        spectrum = cas_rows(lines, left)
        filters = []
        for index in range(2):
            row = 2 * step + index
            frequency = jnp.where(row * 2 > MESH_Y, row - MESH_Y, row).astype(jnp.float32) / MESH_Y
            total = pair_ref[1] + frequency * frequency
            positive = total > 0
            safe = jnp.where(positive, total, 1.0)
            filters.append(jnp.where(positive, pair_ref[0] * gain_ref[pl.ds(row, 1), :] / safe, 0.0))
        lines = cas_rows(spectrum * jnp.concatenate(filters, axis=1), left)
        for index, span in enumerate(spans):
            turned_ref[span, :] = lines[:, index * MESH_Z : (index + 1) * MESH_Z]
        return carry

    lax.fori_loop(0, MESH_Y // 2, filtering, 0, unroll=16)

    def backward(step, carry):
        both = jnp.concatenate(
            [turned_ref[pl.ds(2 * step + index, MESH_Y, stride=MESH_X), :] for index in range(2)], axis=1
        )
        along_y = cas_rows(both, left)
        field = cas_lanes(
            jnp.concatenate([along_y[:, :MESH_Z], along_y[:, MESH_Z:]], axis=0), right
        )
        for index in range(2):
            plane = field[index * MESH_Y : (index + 1) * MESH_Y]
            plane = jnp.concatenate([plane, plane[:8]], axis=0)
            for block in range(blocks):
                window_ref[2 * step + index, block] = plane[block * rows : block * rows + frame].astype(jnp.bfloat16)
        return carry

    lax.fori_loop(0, MESH_X // 2, backward, 0, unroll=16)

    for index in range(border):
        window_ref[MESH_X + index] = window_ref[index]

    def gather(turn_index, block):
        place = turn_index * blocks + block
        slab = order_ref[turn_index]
        x_base, unused, (x_table, x_slope) = cyclic_tables(0, place, (0, 1))
        unused, y_own, (y_table, y_slope) = cyclic_tables(1, place, (0, 1))
        z_table, z_slope = z_tables(place, (0, 1))
        charge = charged_ref[turn_index, pl.ds(block, 1), :]
        window = jnp.concatenate(
            [window_ref[slab * planes + index, block] for index in range(extent)], axis=0
        )

        def chosen(near, index, own):
            def rows_of(plane):
                return jnp.where(
                    y_own, near[plane * frame : plane * frame + 8], near[plane * frame + 8 : plane * frame + 16]
                )

            if index < border:
                return jnp.where(own, rows_of(index), rows_of(planes + index))
            return rows_of(index)

        both = dot32(window, jnp.concatenate([z_table, z_slope], axis=1))
        near, near_z = both[:, :capacity], both[:, capacity:]
        plain = sloped = plain_z = 0.0
        for index in range(planes):
            own = x_base <= index
            part = chosen(near, index, own)
            plain += x_table[index : index + 1] * part
            sloped += x_slope[index : index + 1] * part
            plain_z += x_table[index : index + 1] * chosen(near_z, index, own)
        row = pl.ds(block, 1)
        value_ref[slab, 0, row, :] = jnp.sum(y_table * plain, axis=0, keepdims=True)
        value_ref[slab, 1, row, :] = -charge * jnp.sum(y_table * sloped, axis=0, keepdims=True)
        value_ref[slab, 2, row, :] = -charge * jnp.sum(y_slope * plain, axis=0, keepdims=True)
        value_ref[slab, 3, row, :] = -charge * jnp.sum(y_table * plain_z, axis=0, keepdims=True)

    def gather_step(step, carry):
        gather(step // blocks, step % blocks)
        return carry

    lax.fori_loop(0, slabs * blocks, gather_step, 0, unroll=16)
    halves = capacity // 128
    lines = lax.broadcasted_iota(jnp.int32, (4 * halves, 128), 0)
    shift = 1.5 * 2.0**23

    def encode(slab, carry):
        pieces = [
            value_ref[slab, kind, :, half * 128 : (half + 1) * 128] for kind in range(4) for half in range(halves)
        ]
        largest = jnp.zeros((4 * halves, 128), jnp.float32)
        for line, piece in enumerate(pieces):
            largest = jnp.where(lines == line, jnp.max(jnp.abs(piece), axis=0, keepdims=True), largest)
        level = level_of(largest)
        inverse_scale = power_of_two(level, -1)
        for line, piece in enumerate(pieces):
            codes = (piece * inverse_scale[line : line + 1] + shift) - shift
            out_ref[slab, pl.ds(line * blocks, blocks), :] = codes.astype(jnp.int32).astype(jnp.int16)
        rest = jnp.zeros((blocks - 4 * halves, 128), jnp.int32)
        out_ref[slab, pl.ds(4 * halves * blocks, blocks), :] = jnp.concatenate([level, rest], axis=0).astype(jnp.int16)
        return carry

    lax.fori_loop(0, slabs, encode, 0, unroll=8)


def channel_shards(charges, cell_offset, base_cell, counts, widths):
    device = lax.axis_index("wide")
    channels, slot_count = charges.shape
    blocks = counts.shape[0]
    capacity = slot_count // blocks
    slabs = lax.axis_size("wide")
    live_mask = jnp.arange(capacity, dtype=jnp.int32)[None, :] < counts[:, None]
    charge_blocks = jnp.where(
        live_mask[None], charges.reshape(channels, blocks, capacity), jnp.zeros((), jnp.bfloat16)
    )
    cells = base_cell.astype(jnp.bfloat16).reshape(1, 3, blocks, capacity)
    offsets = cell_offset.reshape(1, 3, blocks, capacity)
    parts = charge_blocks[None]
    order = jnp.zeros((1,), jnp.int32)
    distance = slabs // 2
    while distance > 0:
        route = [(index, index ^ distance) for index in range(slabs)]
        upper = (device & distance) > 0
        first, second = parts[:, :distance], parts[:, distance:]
        kept, sent = jnp.where(upper, second, first), jnp.where(upper, first, second)
        count = cells.shape[0]
        bundle = jnp.concatenate([cells.reshape((-1,) + cells.shape[2:]), sent.reshape((-1,) + sent.shape[2:])], axis=0)
        arrived = lax.ppermute(offsets, "wide", route)
        bundle = lax.ppermute(bundle, "wide", route)
        order = jnp.concatenate([order, order ^ distance])
        if distance > 1:
            offsets = jnp.concatenate([offsets, arrived], axis=0)
            cells = jnp.concatenate([cells, bundle[: 3 * count].reshape(cells.shape)], axis=0)
            parts = jnp.concatenate([kept, bundle[3 * count :].reshape(kept.shape)], axis=0)
        distance //= 2
    order = order ^ device

    points = np.arange(MESH_X)
    first = np.array([1.0, 26.0, 66.0, 26.0, 1.0, 0.0]) / 120.0
    angles = 2.0 * math.pi * points[:, None] * np.arange(ORDER)[None, :] / MESH_X
    inverse = (1.0 / ((np.cos(angles) @ first) ** 2 + (np.sin(angles) @ first) ** 2)).astype(np.float32)
    inverse = np.stack([np.repeat(inverse[:, None], MESH_Z, axis=1), np.repeat(inverse[None], MESH_X, axis=0)])
    one, two = cas_terms(MESH_X)
    right = np.concatenate([np.concatenate([one, two], axis=1)] * 2, axis=0)
    left = np.concatenate([one, one, two], axis=1)

    halves = capacity // 128
    whole = pl.BlockSpec(memory_space=pltpu.VMEM)
    away = pl.BlockSpec(memory_space=pltpu.HBM)
    scalars = pl.BlockSpec(memory_space=pltpu.SMEM)
    result = pl.pallas_call(
        channel_kernel,
        out_shape=jax.ShapeDtypeStruct((slabs, (4 * halves + 1) * blocks, 128), jnp.int16),
        in_specs=[whole] * 5 + [away] + [scalars] * 2 + [away] * 2,
        out_specs=whole,
        scratch_shapes=[
            pltpu.VMEM((MESH_X + ORDER - 1, MESH_Y + 8, MESH_Z), jnp.float32),
            pltpu.VMEM((MESH_X * MESH_Y, MESH_Z), jnp.float32),
            pltpu.VMEM((MESH_X + ORDER - 1, blocks, 16, MESH_Z), jnp.bfloat16),
            pltpu.VMEM((6, capacity // 128, slabs * blocks * 8, 128), jnp.float32),
            pltpu.VMEM((4, slabs * blocks, capacity), jnp.int32),
            pltpu.VMEM((2, MESH_X, MESH_Z), jnp.float32),
            pltpu.VMEM((MESH_Y, MESH_Z), jnp.float32),
            pltpu.VMEM((slabs, 4, blocks, capacity), jnp.float32),
            pltpu.VMEM((slabs, blocks, capacity), jnp.float32),
            pltpu.VMEM(inverse.shape, jnp.float32),
            pltpu.VMEM(right.shape, jnp.bfloat16),
            pltpu.VMEM(left.shape, jnp.bfloat16),
            pltpu.SemaphoreType.DMA,
            pltpu.SemaphoreType.DMA,
            pltpu.SemaphoreType.DMA,
        ],
        compiler_params=pltpu.CompilerParams(vmem_limit_bytes=52 * 1024 * 1024),
        name="channel",
    )(
        offsets, cells, kept[:, 0], arrived, bundle, jnp.asarray(inverse), order, widths,
        jnp.asarray(right), jnp.asarray(left),
    )
    returned = lax.all_to_all(result, "wide", split_axis=0, concat_axis=0, tiled=True)
    codes = returned[:, : 4 * halves * blocks].reshape(channels, 4, halves, blocks, 128)
    levels = returned[:, 4 * halves * blocks : 4 * halves * blocks + 4 * halves].astype(jnp.int32)
    scales = power_of_two(levels, 1).reshape(channels, 4, halves, 1, 128)
    values = codes.astype(jnp.float32) * scales
    potential = jnp.moveaxis(values[:, 0], 1, 2).reshape(channels, blocks, capacity)
    atom_potential = jnp.where(live_mask[None], potential, 0.0).reshape(channels, slot_count)
    forces = jnp.moveaxis(jnp.sum(values[:, 1:], axis=0), 1, 2).reshape(3, slot_count)
    return (atom_potential, forces)


def shards(charges, cell_offset, base_cell, counts, widths):
    if lax.axis_size("wide") == charges.shape[0] and MESH_X == 8 * lax.axis_size("wide"):
        return channel_shards(charges, cell_offset, base_cell, counts, widths)
    return slab_shards(charges, cell_offset, base_cell, counts, widths)


def solution(mesh):
    in_specs = (
        P(None, ("groups", "wide")),
        P(None, ("groups", "wide")),
        P(None, ("groups", "wide")),
        P(("groups", "wide")),
        P(),
    )
    out_specs = (P(None, ("groups", "wide")), P(None, ("groups", "wide")))
    return jax.shard_map(shards, mesh=mesh, in_specs=in_specs, out_specs=out_specs, check_vma=False)
```

```python
import functools
import math

import jax
import jax.numpy as jnp
import numpy as np
from jax import lax
from jax.experimental import pallas as pl
from jax.experimental.pallas import tpu as pltpu
from jax.sharding import PartitionSpec as P

MESH_X = 128
MESH_Y = 128
MESH_Z = 128
ORDER = 6


highest = lax.Precision.HIGHEST


def shifted(block, axis, distance):
    devices = range(lax.axis_size(axis))
    route = [((i - distance) % len(devices), i) for i in devices]
    return lax.ppermute(block, axis, route)


def spline_lists(offset, order_count):
    weights = [1.0 - offset, offset]
    slopes = [-jnp.ones_like(offset), jnp.ones_like(offset)]
    for degree in range(3, order_count + 1):
        if degree == order_count:
            slopes = (
                [-weights[0]]
                + [weights[position - 1] - weights[position] for position in range(1, degree - 1)]
                + [weights[degree - 2]]
            )
        factor = 1.0 / (degree - 1)
        updated = [None] * degree
        updated[degree - 1] = factor * offset * weights[degree - 2]
        for position in range(1, degree - 1):
            updated[degree - position - 1] = factor * (
                (offset + position) * weights[degree - position - 2]
                + (degree - position - offset) * weights[degree - position - 1]
            )
        updated[0] = factor * (1.0 - offset) * weights[0]
        weights = updated
    return (weights, slopes)


def spline_table(offset, order_count):
    weights, slopes = spline_lists(offset, order_count)
    return (jnp.stack(weights), jnp.stack(slopes))


def stencil_rows(weights, slopes, relative, extent, period):
    shifts = jnp.arange(weights.shape[0], dtype=jnp.int32)[None, :, None]
    targets = (relative[:, None, :] + shifts) % period
    points = jnp.arange(extent, dtype=jnp.int32)[None, :, None, None]
    matches = points == targets[:, None]
    plain_rows = jnp.sum(jnp.where(matches, jnp.moveaxis(weights, 0, 1)[:, None], 0.0), axis=2)
    slope_rows = jnp.sum(jnp.where(matches, jnp.moveaxis(slopes, 0, 1)[:, None], 0.0), axis=2)
    return (plain_rows, slope_rows)


def folded(points, length):
    values = jnp.where(points * 2 > length, points - length, points)
    return values.astype(jnp.float32) / length


def moduli(points, length):
    base_weights, base_slopes = spline_table(jnp.zeros((1,), jnp.float32), ORDER)
    shifts = jnp.arange(ORDER, dtype=jnp.int32)
    phases = points[:, None] * shifts[None, :] % length
    angles = phases.astype(jnp.float32) * (2.0 * math.pi / length)
    real_sum = jnp.sum(base_weights[:, 0][None, :] * jnp.cos(angles), axis=1)
    imag_sum = jnp.sum(base_weights[:, 0][None, :] * jnp.sin(angles), axis=1)
    return real_sum * real_sum + imag_sum * imag_sum


def kernel_table(widths, x_freq, y_freq, z_freq, x_mod, y_mod, z_mod):
    total = (
        x_freq[:, None, None, None] ** 2
        + y_freq[None, :, None, None] ** 2
        + z_freq[None, None, None, :] ** 2
    )
    positive = total > 0
    safe = jnp.where(positive, total, 1.0)
    beta = widths[None, None, :, None]
    divisor = x_mod[:, None, None, None] * y_mod[None, :, None, None] * z_mod[None, None, None, :]
    return jnp.where(
        positive,
        2.0 * jnp.exp(-math.pi**2 * total / (beta * beta)) / (math.pi * safe * divisor),
        0.0,
    )


def dft_tables(length):
    points = jnp.arange(length, dtype=jnp.int32)
    phases = points[:, None] * points[None, :] % length
    angles = phases.astype(jnp.float32) * (2.0 * math.pi / length)
    return (jnp.cos(angles), jnp.sin(angles))


def combine_blocks(block_grid, block_rows, border):
    owned = block_grid[:, :, :block_rows]
    overflow = jnp.roll(block_grid[:, :, block_rows:], 1, axis=0)
    owned = owned.at[:, :, :border].add(overflow)
    moved = jnp.moveaxis(owned, 0, 1)
    return moved.reshape((moved.shape[0], moved.shape[1] * moved.shape[2]) + moved.shape[3:])


def contract(data, x_weights, y_weights):
    return jnp.einsum("pycs,ps,ys->cs", data, x_weights, y_weights, precision=highest)


def turn(real_part, imag_part, cosines, sines, orient, pattern):

    def project(data, table):
        return jnp.einsum(pattern, data, table, precision=highest)

    real_out = project(real_part, cosines) - orient * project(imag_part, sines)
    imag_out = project(imag_part, cosines) + orient * project(real_part, sines)
    return jnp.stack([real_out, imag_out])


def slab_shards(charges, cell_offset, base_cell, counts, widths):
    wide_size = lax.axis_size("wide")
    device = lax.axis_index("wide")
    channels, slot_count = charges.shape
    blocks = counts.shape[0]
    capacity = slot_count // blocks
    planes = MESH_X // wide_size
    border = ORDER - 1
    extent = planes + border
    block_rows = MESH_Y // blocks
    y_extent = block_rows + border
    rounds = (border + planes - 1) // planes
    y_local = MESH_Y // wide_size
    live_mask = jnp.arange(capacity, dtype=jnp.int32)[None, :] < counts[:, None]
    charge_blocks = jnp.where(
        live_mask[:, None, :],
        jnp.moveaxis(charges.reshape(channels, blocks, capacity), 0, 1),
        jnp.zeros((), jnp.bfloat16),
    )
    offsets = cell_offset.reshape(3, blocks, capacity)
    bases = base_cell.reshape(3, blocks, capacity)
    x_weights, x_slopes = spline_table(offsets[0], ORDER)
    y_weights, y_slopes = spline_table(offsets[1], ORDER)
    z_weights, z_slopes = spline_table(offsets[2], ORDER)
    row_start = jnp.arange(blocks, dtype=jnp.int32)[:, None] * block_rows
    x_rows, x_drows = stencil_rows(x_weights, x_slopes, bases[0] - device * planes, extent, extent)
    y_rows, y_drows = stencil_rows(y_weights, y_slopes, bases[1] - row_start, y_extent, y_extent)
    z_plain, z_slope = stencil_rows(z_weights, z_slopes, bases[2], MESH_Z, MESH_Z)
    z_table = jnp.stack([z_plain, z_slope], axis=2).astype(jnp.bfloat16)

    def spread_block(inputs):
        x_block, y_block, charge_block, table_block = inputs
        products = (
            x_block[:, None, None, :]
            * y_block[None, :, None, :]
            * charge_block.astype(jnp.float32)[None, None]
        ).astype(jnp.bfloat16)
        spread = jnp.einsum(
            "rs,zs->rz",
            products.reshape(-1, capacity),
            table_block[:, 0],
            preferred_element_type=jnp.float32,
        )
        return spread.reshape(extent, y_extent, channels, MESH_Z)

    block_grid = lax.map(spread_block, (x_rows, y_rows, charge_blocks, z_table))
    grid_ext = combine_blocks(block_grid, block_rows, border)
    z_cos, z_sin = dft_tables(MESH_Z)
    y_cos, y_sin = dft_tables(MESH_Y)
    x_cos, x_sin = dft_tables(MESH_X)
    x_points = jnp.arange(MESH_X, dtype=jnp.int32)
    y_points = device * y_local + jnp.arange(y_local, dtype=jnp.int32)
    z_points = jnp.arange(MESH_Z, dtype=jnp.int32)
    kernel = kernel_table(
        widths,
        folded(x_points, MESH_X),
        folded(y_points, MESH_Y),
        folded(z_points, MESH_Z),
        moduli(x_points, MESH_X),
        moduli(y_points, MESH_Y),
        moduli(z_points, MESH_Z),
    )
    kernel = kernel / float(MESH_X * MESH_Y * MESH_Z)
    owned = grid_ext[:planes]
    for hop_index in range(1, rounds + 1):
        outgoing = grid_ext[hop_index * planes : (hop_index + 1) * planes]
        outgoing = jnp.pad(outgoing, ((0, planes - outgoing.shape[0]), (0, 0), (0, 0), (0, 0)))
        owned = owned + shifted(outgoing, "wide", hop_index)
    real_z = jnp.dot(owned, z_cos, precision=highest)
    imag_z = -jnp.dot(owned, z_sin, precision=highest)
    columns = lax.all_to_all(
        turn(real_z, imag_z, y_cos, y_sin, -1.0, "pycz,yk->pkcz"),
        "wide",
        split_axis=2,
        concat_axis=1,
        tiled=True,
    )
    spectrum = turn(columns[0], columns[1], x_cos, x_sin, -1.0, "xycz,xk->kycz")
    filtered = turn(spectrum[0] * kernel, spectrum[1] * kernel, x_cos, x_sin, 1.0, "xycz,xk->kycz")
    returned = lax.all_to_all(filtered, "wide", split_axis=1, concat_axis=2, tiled=True)
    along_y = turn(returned[0], returned[1], y_cos, y_sin, 1.0, "pycz,yk->pkcz")
    potential_own = (
        jnp.dot(along_y[0], z_cos, precision=highest)
        - jnp.dot(along_y[1], z_sin, precision=highest)
    ).astype(jnp.bfloat16)
    pieces = [potential_own]
    for hop_index in range(1, rounds + 1):
        pieces.append(shifted(potential_own, "wide", -hop_index))
    potential_ext = jnp.concatenate(pieces, axis=0)[:extent]
    blocked = potential_ext.reshape(extent, blocks, block_rows, channels, MESH_Z)
    following = jnp.roll(blocked[:, :, :border], -1, axis=1)
    windows = jnp.moveaxis(jnp.concatenate([blocked, following], axis=2), 1, 0)

    def gather_block(inputs):
        window, x_block, x_dblock, y_block, y_dblock, table_block, charge_block, live_block = inputs
        values = jnp.dot(
            window.reshape(-1, MESH_Z),
            table_block.reshape(MESH_Z, -1),
            preferred_element_type=jnp.float32,
        )
        values = values.reshape(extent, y_extent, channels, 2, capacity)
        direct = values[:, :, :, 0]
        sloped = values[:, :, :, 1]
        potential = jnp.where(live_block[None], contract(direct, x_block, y_block), 0.0)
        gradient = jnp.stack(
            [
                contract(direct, x_dblock, y_block),
                contract(direct, x_block, y_dblock),
                contract(sloped, x_block, y_block),
            ]
        )
        forces = -jnp.sum(gradient * charge_block.astype(jnp.float32)[None], axis=1)
        return (potential, forces)

    potentials, forces = lax.map(
        gather_block, (windows, x_rows, x_drows, y_rows, y_drows, z_table, charge_blocks, live_mask)
    )
    atom_potential = jnp.moveaxis(potentials, 0, 1).reshape(channels, slot_count)
    atom_forces = jnp.moveaxis(forces, 0, 1).reshape(3, slot_count)
    return (atom_potential, atom_forces)


def cas_terms(length):
    points = np.arange(length)
    angles = (points[:, None] * points[None, :] % length) * (2.0 * math.pi / length)
    left = (np.cos(angles) + np.sin(angles)).astype(np.float32)
    terms = []
    for _ in range(2):
        term = left.astype(jnp.bfloat16)
        terms.append(term)
        left = left - term.astype(np.float32)
    return terms


def split(values):
    first = values.astype(jnp.bfloat16)
    return first, (values - first.astype(jnp.float32)).astype(jnp.bfloat16)


def dot32(a, b, contract_b=0):
    return lax.dot_general(a, b, (((1,), (contract_b,)), ((), ())), preferred_element_type=jnp.float32)


def cas_lanes(values, right):
    sums = dot32(jnp.concatenate(split(values), axis=1), right)
    length = values.shape[1]
    return sums[:, :length] + sums[:, length:]


def cas_rows(values, left):
    sums = dot32(left, jnp.concatenate(split(values), axis=0))
    length = values.shape[0]
    return sums[:length] + sums[length:]


def level_of(largest):
    logarithm = jnp.log(jnp.maximum(largest, 1e-36)) * (1.0 / math.log(2.0))
    level = jnp.floor(logarithm + 1e-3).astype(jnp.int32) + 1 - 15 + 126
    return jnp.clip(level, 0, 250)


def power_of_two(level, sign):
    value = jnp.full(level.shape, 2.0 ** (-126 * sign), jnp.float32)
    for bit in range(7):
        value = value * jnp.where((level >> bit) & 1 > 0, 2.0 ** (sign * 2**bit), 1.0)
    return value * jnp.where((level >> 7) & 1 > 0, 2.0 ** (sign * 64), 1.0) * jnp.where((level >> 7) & 1 > 0, 2.0 ** (sign * 64), 1.0)


def channel_kernel(
    offset_ref, base_ref, charge_ref, far_offset_ref, far_ref, inverse_hbm, order_ref, widths_ref,
    right_hbm, left_hbm, out_ref,
    grid_ref, turned_ref, window_ref, spline_ref, place_ref, pair_ref, gain_ref, value_ref, charged_ref,
    inverse_ref, right_ref, left_ref, inverse_done, right_done, left_done,
):
    near, _, blocks, capacity = offset_ref.shape
    slabs = 2 * near
    planes = MESH_X // slabs
    rows = MESH_Y // blocks
    border = ORDER - 1
    frame = 16
    extent = planes + border
    far = MESH_X + border

    loads = [
        pltpu.make_async_copy(inverse_hbm, inverse_ref, inverse_done),
        pltpu.make_async_copy(right_hbm, right_ref, right_done),
        pltpu.make_async_copy(left_hbm, left_ref, left_done),
    ]
    for load in loads:
        load.start()

    def prepare(slab, offset_at, base_at, charge):
        span = pl.ds(pl.multiple_of(slab * blocks, blocks), blocks)
        charged_ref[slab] = charge.astype(jnp.float32)
        bases = [base_at(dimension).astype(jnp.float32).astype(jnp.int32) for dimension in range(3)]
        place_ref[0, span, :] = bases[0] & 7
        place_ref[1, span, :] = bases[1] & 7
        place_ref[2, span, :] = bases[2] & 7
        place_ref[3, span, :] = bases[2] >> 3
        for dimension in range(3):
            weights, slopes = spline_lists(offset_at(dimension), ORDER)
            for kind, values in enumerate((weights, slopes)):
                for position in range(8):
                    value = values[position] if position < ORDER else jnp.zeros_like(values[0])
                    for half in range(capacity // 128):
                        spline_ref[
                            2 * dimension + kind, half, pl.ds(slab * blocks * 8 + position, blocks, stride=8), :
                        ] = value[:, half * 128 : (half + 1) * 128]

    def prepare_both(index, carry):
        prepare(
            index,
            lambda dimension: offset_ref[index, dimension],
            lambda dimension: base_ref[index, dimension],
            charge_ref[index],
        )
        prepare(
            near + index,
            lambda dimension: far_offset_ref[index, dimension],
            lambda dimension: far_ref[3 * index + dimension],
            far_ref[3 * near + index],
        )
        return carry

    lax.fori_loop(0, near, prepare_both, 0)

    def clear(plane, carry):
        grid_ref[plane] = jnp.zeros(grid_ref.shape[1:], jnp.float32)
        return carry

    lax.fori_loop(0, far, clear, 0)
    points = lax.broadcasted_iota(jnp.int32, (8, capacity), 0)

    def row_of(dimension, block):
        return jnp.broadcast_to(place_ref[dimension, pl.ds(block, 1), :], (8, capacity))

    def cyclic_tables(dimension, block, kinds):
        base = row_of(dimension, block)
        index = (points - base) & 7
        span = pl.ds(pl.multiple_of(block * 8, 8), 8)
        tables = []
        for kind in kinds:
            values = jnp.concatenate(
                [spline_ref[2 * dimension + kind, half, span, :] for half in range(capacity // 128)], axis=1
            )
            tables.append(jnp.take_along_axis(values, index, axis=0, mode="promise_in_bounds"))
        return base, points >= base, tables

    def z_tables(block, kinds):
        unused, own, tables = cyclic_tables(2, block, kinds)
        tile = row_of(3, block)
        tile = jnp.where(own, tile, (tile + 1) & (MESH_Z // 8 - 1)).astype(jnp.float32)
        tile = jnp.concatenate([tile, tile - 1.0], axis=0).astype(jnp.bfloat16)
        here = [tile == jnp.bfloat16(2 * index) for index in range(MESH_Z // 16)]
        results = []
        for table in tables:
            twice = jnp.concatenate([table, table], axis=0).astype(jnp.bfloat16)
            results.append(
                jnp.concatenate([jnp.where(mask, twice, jnp.zeros_like(twice)) for mask in here], axis=0)
            )
        return results

    def spread(turn_index, block):
        place = turn_index * blocks + block
        slab = order_ref[turn_index]
        x_base, unused, (x_table,) = cyclic_tables(0, place, (0,))
        unused, y_own, (y_table,) = cyclic_tables(1, place, (0,))
        (z_table,) = z_tables(place, (0,))
        charge = jnp.broadcast_to(charged_ref[turn_index, pl.ds(block, 1), :], (8, capacity))
        x_place = jnp.concatenate([x_base, x_base], axis=0).astype(jnp.float32).astype(jnp.bfloat16)
        low, high = [], []
        for index in range(planes):
            product = (x_table[index : index + 1] * y_table) * charge
            pair = jnp.concatenate(
                [jnp.where(y_own, product, 0.0), jnp.where(y_own, 0.0, product)], axis=0
            ).astype(jnp.bfloat16)
            if index < border:
                own = x_place <= jnp.bfloat16(index)
                low.append(jnp.where(own, pair, jnp.zeros_like(pair)))
                high.append(jnp.where(own, jnp.zeros_like(pair), pair))
            else:
                low.append(pair)
        sums = dot32(jnp.concatenate(low + high, axis=0), z_table, 1)
        row_span = pl.ds(pl.multiple_of(block * rows, rows), frame)
        for index in range(extent):
            grid_ref[slab * planes + index, row_span, :] += sums[index * frame : (index + 1) * frame]

    def spread_step(step, carry):
        spread(step // blocks, step % blocks)
        return carry

    lax.fori_loop(0, slabs * blocks, spread_step, 0, unroll=32)

    for index in range(border):
        grid_ref[index] += grid_ref[MESH_X + index]

    for load in loads:
        load.wait()
    right, left = right_ref[...], left_ref[...]
    width = widths_ref[order_ref[0]]

    def squares(dimension):
        index = lax.broadcasted_iota(jnp.int32, (MESH_X, MESH_Z), dimension)
        index = jnp.where(index * 2 > MESH_X, index - MESH_X, index).astype(jnp.float32) / MESH_X
        return index * index

    across, along = squares(0), squares(1)
    decay = -(math.pi**2) / (width * width)
    gain_ref[...] = jnp.exp(decay * across) * inverse_ref[0]
    scale = 2.0 / (math.pi * MESH_X * MESH_Y * MESH_Z)
    pair_ref[0] = gain_ref[...] * (jnp.exp(decay * along) * (inverse_ref[1] * scale))
    pair_ref[1] = across + along

    def forward(step, carry):
        both = []
        for index in range(2):
            plane = 2 * step + index
            both.append(grid_ref[plane, 0:8, :] + grid_ref[plane, MESH_Y : MESH_Y + 8, :])
            both.append(grid_ref[plane, 8:MESH_Y, :])
        along_z = cas_lanes(jnp.concatenate(both, axis=0), right)
        along_y = cas_rows(
            jnp.concatenate([along_z[:MESH_Y], along_z[MESH_Y:]], axis=1), left
        )
        for index in range(2):
            turned_ref[pl.ds(2 * step + index, MESH_Y, stride=MESH_X), :] = along_y[
                :, index * MESH_Z : (index + 1) * MESH_Z
            ]
        return carry

    lax.fori_loop(0, MESH_X // 2, forward, 0, unroll=32)

    def filtering(step, carry):
        spans = [pl.ds(pl.multiple_of((2 * step + index) * MESH_X, MESH_X), MESH_X) for index in range(2)]
        lines = jnp.concatenate([turned_ref[span, :] for span in spans], axis=1)
        spectrum = cas_rows(lines, left)
        filters = []
        for index in range(2):
            row = 2 * step + index
            frequency = jnp.where(row * 2 > MESH_Y, row - MESH_Y, row).astype(jnp.float32) / MESH_Y
            total = pair_ref[1] + frequency * frequency
            positive = total > 0
            safe = jnp.where(positive, total, 1.0)
            filters.append(jnp.where(positive, pair_ref[0] * gain_ref[pl.ds(row, 1), :] / safe, 0.0))
        lines = cas_rows(spectrum * jnp.concatenate(filters, axis=1), left)
        for index, span in enumerate(spans):
            turned_ref[span, :] = lines[:, index * MESH_Z : (index + 1) * MESH_Z]
        return carry

    lax.fori_loop(0, MESH_Y // 2, filtering, 0, unroll=32)

    def backward(step, carry):
        both = jnp.concatenate(
            [turned_ref[pl.ds(2 * step + index, MESH_Y, stride=MESH_X), :] for index in range(2)], axis=1
        )
        along_y = cas_rows(both, left)
        field = cas_lanes(
            jnp.concatenate([along_y[:, :MESH_Z], along_y[:, MESH_Z:]], axis=0), right
        )
        for index in range(2):
            plane = field[index * MESH_Y : (index + 1) * MESH_Y]
            plane = jnp.concatenate([plane, plane[:8]], axis=0)
            for block in range(blocks):
                window_ref[2 * step + index, block] = plane[block * rows : block * rows + frame].astype(jnp.bfloat16)
        return carry

    lax.fori_loop(0, MESH_X // 2, backward, 0, unroll=32)

    for index in range(border):
        window_ref[MESH_X + index] = window_ref[index]

    def gather(turn_index, block):
        place = turn_index * blocks + block
        slab = order_ref[turn_index]
        x_base, unused, (x_table, x_slope) = cyclic_tables(0, place, (0, 1))
        unused, y_own, (y_table, y_slope) = cyclic_tables(1, place, (0, 1))
        z_table, z_slope = z_tables(place, (0, 1))
        charge = charged_ref[turn_index, pl.ds(block, 1), :]
        window = jnp.concatenate(
            [window_ref[slab * planes + index, block] for index in range(extent)], axis=0
        )

        def chosen(near, index, own):
            def rows_of(plane):
                return jnp.where(
                    y_own, near[plane * frame : plane * frame + 8], near[plane * frame + 8 : plane * frame + 16]
                )

            if index < border:
                return jnp.where(own, rows_of(index), rows_of(planes + index))
            return rows_of(index)

        both = dot32(window, jnp.concatenate([z_table, z_slope], axis=1))
        near, near_z = both[:, :capacity], both[:, capacity:]
        plain = sloped = plain_z = 0.0
        for index in range(planes):
            own = x_base <= index
            part = chosen(near, index, own)
            plain += x_table[index : index + 1] * part
            sloped += x_slope[index : index + 1] * part
            plain_z += x_table[index : index + 1] * chosen(near_z, index, own)
        row = pl.ds(block, 1)
        value_ref[slab, 0, row, :] = jnp.sum(y_table * plain, axis=0, keepdims=True)
        value_ref[slab, 1, row, :] = -charge * jnp.sum(y_table * sloped, axis=0, keepdims=True)
        value_ref[slab, 2, row, :] = -charge * jnp.sum(y_slope * plain, axis=0, keepdims=True)
        value_ref[slab, 3, row, :] = -charge * jnp.sum(y_table * plain_z, axis=0, keepdims=True)

    def gather_step(step, carry):
        gather(step // blocks, step % blocks)
        return carry

    lax.fori_loop(0, slabs * blocks, gather_step, 0, unroll=32)
    halves = capacity // 128
    lines = lax.broadcasted_iota(jnp.int32, (4 * halves, 128), 0)
    shift = 1.5 * 2.0**23

    def encode(slab, carry):
        pieces = [
            value_ref[slab, kind, :, half * 128 : (half + 1) * 128] for kind in range(4) for half in range(halves)
        ]
        largest = jnp.zeros((4 * halves, 128), jnp.float32)
        for line, piece in enumerate(pieces):
            largest = jnp.where(lines == line, jnp.max(jnp.abs(piece), axis=0, keepdims=True), largest)
        level = level_of(largest)
        inverse_scale = power_of_two(level, -1)
        for line, piece in enumerate(pieces):
            codes = (piece * inverse_scale[line : line + 1] + shift) - shift
            out_ref[slab, pl.ds(line * blocks, blocks), :] = codes.astype(jnp.int32).astype(jnp.int16)
        rest = jnp.zeros((blocks - 4 * halves, 128), jnp.int32)
        out_ref[slab, pl.ds(4 * halves * blocks, blocks), :] = jnp.concatenate([level, rest], axis=0).astype(jnp.int16)
        return carry

    lax.fori_loop(0, slabs, encode, 0, unroll=8)


def channel_shards(charges, cell_offset, base_cell, counts, widths):
    device = lax.axis_index("wide")
    channels, slot_count = charges.shape
    blocks = counts.shape[0]
    capacity = slot_count // blocks
    slabs = lax.axis_size("wide")
    live_mask = jnp.arange(capacity, dtype=jnp.int32)[None, :] < counts[:, None]
    charge_blocks = jnp.where(
        live_mask[None], charges.reshape(channels, blocks, capacity), jnp.zeros((), jnp.bfloat16)
    )
    cells = base_cell.astype(jnp.bfloat16).reshape(1, 3, blocks, capacity)
    offsets = cell_offset.reshape(1, 3, blocks, capacity)
    parts = charge_blocks[None]
    order = jnp.zeros((1,), jnp.int32)
    distance = slabs // 2
    while distance > 0:
        route = [(index, index ^ distance) for index in range(slabs)]
        upper = (device & distance) > 0
        first, second = parts[:, :distance], parts[:, distance:]
        kept, sent = jnp.where(upper, second, first), jnp.where(upper, first, second)
        count = cells.shape[0]
        bundle = jnp.concatenate([cells.reshape((-1,) + cells.shape[2:]), sent.reshape((-1,) + sent.shape[2:])], axis=0)
        arrived = lax.ppermute(offsets, "wide", route)
        bundle = lax.ppermute(bundle, "wide", route)
        order = jnp.concatenate([order, order ^ distance])
        if distance > 1:
            offsets = jnp.concatenate([offsets, arrived], axis=0)
            cells = jnp.concatenate([cells, bundle[: 3 * count].reshape(cells.shape)], axis=0)
            parts = jnp.concatenate([kept, bundle[3 * count :].reshape(kept.shape)], axis=0)
        distance //= 2
    order = order ^ device

    points = np.arange(MESH_X)
    first = np.array([1.0, 26.0, 66.0, 26.0, 1.0, 0.0]) / 120.0
    angles = 2.0 * math.pi * points[:, None] * np.arange(ORDER)[None, :] / MESH_X
    inverse = (1.0 / ((np.cos(angles) @ first) ** 2 + (np.sin(angles) @ first) ** 2)).astype(np.float32)
    inverse = np.stack([np.repeat(inverse[:, None], MESH_Z, axis=1), np.repeat(inverse[None], MESH_X, axis=0)])
    one, two = cas_terms(MESH_X)
    right = np.concatenate([np.concatenate([one, two], axis=1)] * 2, axis=0)
    left = np.concatenate([np.concatenate([one, one], axis=1), np.concatenate([two, two], axis=1)], axis=0)

    halves = capacity // 128
    whole = pl.BlockSpec(memory_space=pltpu.VMEM)
    away = pl.BlockSpec(memory_space=pltpu.HBM)
    scalars = pl.BlockSpec(memory_space=pltpu.SMEM)
    result = pl.pallas_call(
        channel_kernel,
        out_shape=jax.ShapeDtypeStruct((slabs, (4 * halves + 1) * blocks, 128), jnp.int16),
        in_specs=[whole] * 5 + [away] + [scalars] * 2 + [away] * 2,
        out_specs=whole,
        scratch_shapes=[
            pltpu.VMEM((MESH_X + ORDER - 1, MESH_Y + 8, MESH_Z), jnp.float32),
            pltpu.VMEM((MESH_X * MESH_Y, MESH_Z), jnp.float32),
            pltpu.VMEM((MESH_X + ORDER - 1, blocks, 16, MESH_Z), jnp.bfloat16),
            pltpu.VMEM((6, capacity // 128, slabs * blocks * 8, 128), jnp.float32),
            pltpu.VMEM((4, slabs * blocks, capacity), jnp.int32),
            pltpu.VMEM((2, MESH_X, MESH_Z), jnp.float32),
            pltpu.VMEM((MESH_Y, MESH_Z), jnp.float32),
            pltpu.VMEM((slabs, 4, blocks, capacity), jnp.float32),
            pltpu.VMEM((slabs, blocks, capacity), jnp.float32),
            pltpu.VMEM(inverse.shape, jnp.float32),
            pltpu.VMEM(right.shape, jnp.bfloat16),
            pltpu.VMEM(left.shape, jnp.bfloat16),
            pltpu.SemaphoreType.DMA,
            pltpu.SemaphoreType.DMA,
            pltpu.SemaphoreType.DMA,
        ],
        compiler_params=pltpu.CompilerParams(vmem_limit_bytes=52 * 1024 * 1024),
        name="channel",
    )(
        offsets, cells, kept[:, 0], arrived, bundle, jnp.asarray(inverse), order, widths,
        jnp.asarray(right), jnp.asarray(left),
    )
    returned = lax.all_to_all(result, "wide", split_axis=0, concat_axis=0, tiled=True)
    codes = returned[:, : 4 * halves * blocks].reshape(channels, 4, halves, blocks, 128)
    levels = returned[:, 4 * halves * blocks : 4 * halves * blocks + 4 * halves].astype(jnp.int32)
    scales = power_of_two(levels, 1).reshape(channels, 4, halves, 1, 128)
    values = codes.astype(jnp.float32) * scales
    potential = jnp.moveaxis(values[:, 0], 1, 2).reshape(channels, blocks, capacity)
    atom_potential = jnp.where(live_mask[None], potential, 0.0).reshape(channels, slot_count)
    forces = jnp.moveaxis(jnp.sum(values[:, 1:], axis=0), 1, 2).reshape(3, slot_count)
    return (atom_potential, forces)


def shards(charges, cell_offset, base_cell, counts, widths):
    if lax.axis_size("wide") == charges.shape[0] and MESH_X == 8 * lax.axis_size("wide"):
        return channel_shards(charges, cell_offset, base_cell, counts, widths)
    return slab_shards(charges, cell_offset, base_cell, counts, widths)


def solution(mesh):
    in_specs = (
        P(None, ("groups", "wide")),
        P(None, ("groups", "wide")),
        P(None, ("groups", "wide")),
        P(("groups", "wide")),
        P(),
    )
    out_specs = (P(None, ("groups", "wide")), P(None, ("groups", "wide")))
    return jax.shard_map(shards, mesh=mesh, in_specs=in_specs, out_specs=out_specs, check_vma=False)
```

```python
import functools
import math

import jax
import jax.numpy as jnp
import numpy as np
from jax import lax
from jax.experimental import pallas as pl
from jax.experimental.pallas import tpu as pltpu
from jax.sharding import PartitionSpec as P

MESH_X = 128
MESH_Y = 128
MESH_Z = 128
ORDER = 6


highest = lax.Precision.HIGHEST


def shifted(block, axis, distance):
    devices = range(lax.axis_size(axis))
    route = [((i - distance) % len(devices), i) for i in devices]
    return lax.ppermute(block, axis, route)


def spline_lists(offset, order_count):
    weights = [1.0 - offset, offset]
    slopes = [-jnp.ones_like(offset), jnp.ones_like(offset)]
    for degree in range(3, order_count + 1):
        if degree == order_count:
            slopes = (
                [-weights[0]]
                + [weights[position - 1] - weights[position] for position in range(1, degree - 1)]
                + [weights[degree - 2]]
            )
        factor = 1.0 / (degree - 1)
        updated = [None] * degree
        updated[degree - 1] = factor * offset * weights[degree - 2]
        for position in range(1, degree - 1):
            updated[degree - position - 1] = factor * (
                (offset + position) * weights[degree - position - 2]
                + (degree - position - offset) * weights[degree - position - 1]
            )
        updated[0] = factor * (1.0 - offset) * weights[0]
        weights = updated
    return (weights, slopes)


def spline_table(offset, order_count):
    weights, slopes = spline_lists(offset, order_count)
    return (jnp.stack(weights), jnp.stack(slopes))


def stencil_rows(weights, slopes, relative, extent, period):
    shifts = jnp.arange(weights.shape[0], dtype=jnp.int32)[None, :, None]
    targets = (relative[:, None, :] + shifts) % period
    points = jnp.arange(extent, dtype=jnp.int32)[None, :, None, None]
    matches = points == targets[:, None]
    plain_rows = jnp.sum(jnp.where(matches, jnp.moveaxis(weights, 0, 1)[:, None], 0.0), axis=2)
    slope_rows = jnp.sum(jnp.where(matches, jnp.moveaxis(slopes, 0, 1)[:, None], 0.0), axis=2)
    return (plain_rows, slope_rows)


def folded(points, length):
    values = jnp.where(points * 2 > length, points - length, points)
    return values.astype(jnp.float32) / length


def moduli(points, length):
    base_weights, base_slopes = spline_table(jnp.zeros((1,), jnp.float32), ORDER)
    shifts = jnp.arange(ORDER, dtype=jnp.int32)
    phases = points[:, None] * shifts[None, :] % length
    angles = phases.astype(jnp.float32) * (2.0 * math.pi / length)
    real_sum = jnp.sum(base_weights[:, 0][None, :] * jnp.cos(angles), axis=1)
    imag_sum = jnp.sum(base_weights[:, 0][None, :] * jnp.sin(angles), axis=1)
    return real_sum * real_sum + imag_sum * imag_sum


def kernel_table(widths, x_freq, y_freq, z_freq, x_mod, y_mod, z_mod):
    total = (
        x_freq[:, None, None, None] ** 2
        + y_freq[None, :, None, None] ** 2
        + z_freq[None, None, None, :] ** 2
    )
    positive = total > 0
    safe = jnp.where(positive, total, 1.0)
    beta = widths[None, None, :, None]
    divisor = x_mod[:, None, None, None] * y_mod[None, :, None, None] * z_mod[None, None, None, :]
    return jnp.where(
        positive,
        2.0 * jnp.exp(-math.pi**2 * total / (beta * beta)) / (math.pi * safe * divisor),
        0.0,
    )


def dft_tables(length):
    points = jnp.arange(length, dtype=jnp.int32)
    phases = points[:, None] * points[None, :] % length
    angles = phases.astype(jnp.float32) * (2.0 * math.pi / length)
    return (jnp.cos(angles), jnp.sin(angles))


def combine_blocks(block_grid, block_rows, border):
    owned = block_grid[:, :, :block_rows]
    overflow = jnp.roll(block_grid[:, :, block_rows:], 1, axis=0)
    owned = owned.at[:, :, :border].add(overflow)
    moved = jnp.moveaxis(owned, 0, 1)
    return moved.reshape((moved.shape[0], moved.shape[1] * moved.shape[2]) + moved.shape[3:])


def contract(data, x_weights, y_weights):
    return jnp.einsum("pycs,ps,ys->cs", data, x_weights, y_weights, precision=highest)


def turn(real_part, imag_part, cosines, sines, orient, pattern):

    def project(data, table):
        return jnp.einsum(pattern, data, table, precision=highest)

    real_out = project(real_part, cosines) - orient * project(imag_part, sines)
    imag_out = project(imag_part, cosines) + orient * project(real_part, sines)
    return jnp.stack([real_out, imag_out])


def slab_shards(charges, cell_offset, base_cell, counts, widths):
    wide_size = lax.axis_size("wide")
    device = lax.axis_index("wide")
    channels, slot_count = charges.shape
    blocks = counts.shape[0]
    capacity = slot_count // blocks
    planes = MESH_X // wide_size
    border = ORDER - 1
    extent = planes + border
    block_rows = MESH_Y // blocks
    y_extent = block_rows + border
    rounds = (border + planes - 1) // planes
    y_local = MESH_Y // wide_size
    live_mask = jnp.arange(capacity, dtype=jnp.int32)[None, :] < counts[:, None]
    charge_blocks = jnp.where(
        live_mask[:, None, :],
        jnp.moveaxis(charges.reshape(channels, blocks, capacity), 0, 1),
        jnp.zeros((), jnp.bfloat16),
    )
    offsets = cell_offset.reshape(3, blocks, capacity)
    bases = base_cell.reshape(3, blocks, capacity)
    x_weights, x_slopes = spline_table(offsets[0], ORDER)
    y_weights, y_slopes = spline_table(offsets[1], ORDER)
    z_weights, z_slopes = spline_table(offsets[2], ORDER)
    row_start = jnp.arange(blocks, dtype=jnp.int32)[:, None] * block_rows
    x_rows, x_drows = stencil_rows(x_weights, x_slopes, bases[0] - device * planes, extent, extent)
    y_rows, y_drows = stencil_rows(y_weights, y_slopes, bases[1] - row_start, y_extent, y_extent)
    z_plain, z_slope = stencil_rows(z_weights, z_slopes, bases[2], MESH_Z, MESH_Z)
    z_table = jnp.stack([z_plain, z_slope], axis=2).astype(jnp.bfloat16)

    def spread_block(inputs):
        x_block, y_block, charge_block, table_block = inputs
        products = (
            x_block[:, None, None, :]
            * y_block[None, :, None, :]
            * charge_block.astype(jnp.float32)[None, None]
        ).astype(jnp.bfloat16)
        spread = jnp.einsum(
            "rs,zs->rz",
            products.reshape(-1, capacity),
            table_block[:, 0],
            preferred_element_type=jnp.float32,
        )
        return spread.reshape(extent, y_extent, channels, MESH_Z)

    block_grid = lax.map(spread_block, (x_rows, y_rows, charge_blocks, z_table))
    grid_ext = combine_blocks(block_grid, block_rows, border)
    z_cos, z_sin = dft_tables(MESH_Z)
    y_cos, y_sin = dft_tables(MESH_Y)
    x_cos, x_sin = dft_tables(MESH_X)
    x_points = jnp.arange(MESH_X, dtype=jnp.int32)
    y_points = device * y_local + jnp.arange(y_local, dtype=jnp.int32)
    z_points = jnp.arange(MESH_Z, dtype=jnp.int32)
    kernel = kernel_table(
        widths,
        folded(x_points, MESH_X),
        folded(y_points, MESH_Y),
        folded(z_points, MESH_Z),
        moduli(x_points, MESH_X),
        moduli(y_points, MESH_Y),
        moduli(z_points, MESH_Z),
    )
    kernel = kernel / float(MESH_X * MESH_Y * MESH_Z)
    owned = grid_ext[:planes]
    for hop_index in range(1, rounds + 1):
        outgoing = grid_ext[hop_index * planes : (hop_index + 1) * planes]
        outgoing = jnp.pad(outgoing, ((0, planes - outgoing.shape[0]), (0, 0), (0, 0), (0, 0)))
        owned = owned + shifted(outgoing, "wide", hop_index)
    real_z = jnp.dot(owned, z_cos, precision=highest)
    imag_z = -jnp.dot(owned, z_sin, precision=highest)
    columns = lax.all_to_all(
        turn(real_z, imag_z, y_cos, y_sin, -1.0, "pycz,yk->pkcz"),
        "wide",
        split_axis=2,
        concat_axis=1,
        tiled=True,
    )
    spectrum = turn(columns[0], columns[1], x_cos, x_sin, -1.0, "xycz,xk->kycz")
    filtered = turn(spectrum[0] * kernel, spectrum[1] * kernel, x_cos, x_sin, 1.0, "xycz,xk->kycz")
    returned = lax.all_to_all(filtered, "wide", split_axis=1, concat_axis=2, tiled=True)
    along_y = turn(returned[0], returned[1], y_cos, y_sin, 1.0, "pycz,yk->pkcz")
    potential_own = (
        jnp.dot(along_y[0], z_cos, precision=highest)
        - jnp.dot(along_y[1], z_sin, precision=highest)
    ).astype(jnp.bfloat16)
    pieces = [potential_own]
    for hop_index in range(1, rounds + 1):
        pieces.append(shifted(potential_own, "wide", -hop_index))
    potential_ext = jnp.concatenate(pieces, axis=0)[:extent]
    blocked = potential_ext.reshape(extent, blocks, block_rows, channels, MESH_Z)
    following = jnp.roll(blocked[:, :, :border], -1, axis=1)
    windows = jnp.moveaxis(jnp.concatenate([blocked, following], axis=2), 1, 0)

    def gather_block(inputs):
        window, x_block, x_dblock, y_block, y_dblock, table_block, charge_block, live_block = inputs
        values = jnp.dot(
            window.reshape(-1, MESH_Z),
            table_block.reshape(MESH_Z, -1),
            preferred_element_type=jnp.float32,
        )
        values = values.reshape(extent, y_extent, channels, 2, capacity)
        direct = values[:, :, :, 0]
        sloped = values[:, :, :, 1]
        potential = jnp.where(live_block[None], contract(direct, x_block, y_block), 0.0)
        gradient = jnp.stack(
            [
                contract(direct, x_dblock, y_block),
                contract(direct, x_block, y_dblock),
                contract(sloped, x_block, y_block),
            ]
        )
        forces = -jnp.sum(gradient * charge_block.astype(jnp.float32)[None], axis=1)
        return (potential, forces)

    potentials, forces = lax.map(
        gather_block, (windows, x_rows, x_drows, y_rows, y_drows, z_table, charge_blocks, live_mask)
    )
    atom_potential = jnp.moveaxis(potentials, 0, 1).reshape(channels, slot_count)
    atom_forces = jnp.moveaxis(forces, 0, 1).reshape(3, slot_count)
    return (atom_potential, atom_forces)


def cas_terms(length):
    points = np.arange(length)
    angles = (points[:, None] * points[None, :] % length) * (2.0 * math.pi / length)
    left = (np.cos(angles) + np.sin(angles)).astype(np.float32)
    terms = []
    for _ in range(2):
        term = left.astype(jnp.bfloat16)
        terms.append(term)
        left = left - term.astype(np.float32)
    return terms


def split(values):
    first = values.astype(jnp.bfloat16)
    return first, (values - first.astype(jnp.float32)).astype(jnp.bfloat16)


def dot32(a, b, contract_b=0):
    return lax.dot_general(a, b, (((1,), (contract_b,)), ((), ())), preferred_element_type=jnp.float32)


def cas_lanes(values, right):
    sums = dot32(jnp.concatenate(split(values), axis=1), right)
    length = values.shape[1]
    return sums[:, :length] + sums[:, length:]


def cas_rows(values, left):
    sums = dot32(left, jnp.concatenate(split(values), axis=0))
    length = values.shape[0]
    return sums[:length] + sums[length:]


def level_of(largest):
    logarithm = jnp.log(jnp.maximum(largest, 1e-36)) * (1.0 / math.log(2.0))
    level = jnp.floor(logarithm + 1e-3).astype(jnp.int32) + 1 - 15 + 126
    return jnp.clip(level, 0, 250)


def power_of_two(level, sign):
    value = jnp.full(level.shape, 2.0 ** (-126 * sign), jnp.float32)
    for bit in range(7):
        value = value * jnp.where((level >> bit) & 1 > 0, 2.0 ** (sign * 2**bit), 1.0)
    return value * jnp.where((level >> 7) & 1 > 0, 2.0 ** (sign * 64), 1.0) * jnp.where((level >> 7) & 1 > 0, 2.0 ** (sign * 64), 1.0)


def channel_kernel(
    offset_ref, base_ref, charge_ref, far_offset_ref, far_ref, inverse_hbm, order_ref, widths_ref,
    right_hbm, left_hbm, out_ref,
    grid_ref, turned_ref, window_ref, spline_ref, place_ref, pair_ref, gain_ref, value_ref, charged_ref,
    inverse_ref, right_ref, left_ref, inverse_done, right_done, left_done,
):
    near, _, blocks, capacity = offset_ref.shape
    slabs = 2 * near
    planes = MESH_X // slabs
    rows = MESH_Y // blocks
    border = ORDER - 1
    frame = 16
    extent = planes + border
    far = MESH_X + border

    loads = [
        pltpu.make_async_copy(inverse_hbm, inverse_ref, inverse_done),
        pltpu.make_async_copy(right_hbm, right_ref, right_done),
        pltpu.make_async_copy(left_hbm, left_ref, left_done),
    ]
    for load in loads:
        load.start()

    def prepare(slab, offset_at, base_at, charge):
        span = pl.ds(pl.multiple_of(slab * blocks, blocks), blocks)
        charged_ref[slab] = charge.astype(jnp.float32)
        bases = [base_at(dimension).astype(jnp.float32).astype(jnp.int32) for dimension in range(3)]
        place_ref[0, span, :] = bases[0] & 7
        place_ref[1, span, :] = bases[1] & 7
        place_ref[2, span, :] = bases[2] & 7
        place_ref[3, span, :] = bases[2] >> 3
        for dimension in range(3):
            weights, slopes = spline_lists(offset_at(dimension), ORDER)
            for kind, values in enumerate((weights, slopes)):
                for position in range(8):
                    value = values[position] if position < ORDER else jnp.zeros_like(values[0])
                    for half in range(capacity // 128):
                        spline_ref[
                            2 * dimension + kind, half, pl.ds(slab * blocks * 8 + position, blocks, stride=8), :
                        ] = value[:, half * 128 : (half + 1) * 128]

    def prepare_both(index, carry):
        prepare(
            index,
            lambda dimension: offset_ref[index, dimension],
            lambda dimension: base_ref[index, dimension],
            charge_ref[index],
        )
        prepare(
            near + index,
            lambda dimension: far_offset_ref[index, dimension],
            lambda dimension: far_ref[3 * index + dimension],
            far_ref[3 * near + index],
        )
        return carry

    lax.fori_loop(0, near, prepare_both, 0)

    def clear(plane, carry):
        grid_ref[plane] = jnp.zeros(grid_ref.shape[1:], jnp.float32)
        return carry

    lax.fori_loop(0, far, clear, 0)
    points = lax.broadcasted_iota(jnp.int32, (8, capacity), 0)

    def row_of(dimension, block):
        return jnp.broadcast_to(place_ref[dimension, pl.ds(block, 1), :], (8, capacity))

    def cyclic_tables(dimension, block, kinds):
        base = row_of(dimension, block)
        index = (points - base) & 7
        span = pl.ds(pl.multiple_of(block * 8, 8), 8)
        tables = []
        for kind in kinds:
            values = jnp.concatenate(
                [spline_ref[2 * dimension + kind, half, span, :] for half in range(capacity // 128)], axis=1
            )
            tables.append(jnp.take_along_axis(values, index, axis=0, mode="promise_in_bounds"))
        return base, points >= base, tables

    def z_tables(block, kinds):
        unused, own, tables = cyclic_tables(2, block, kinds)
        tile = row_of(3, block)
        tile = jnp.where(own, tile, (tile + 1) & (MESH_Z // 8 - 1)).astype(jnp.float32)
        tile = jnp.concatenate([tile, tile - 1.0], axis=0).astype(jnp.bfloat16)
        here = [tile == jnp.bfloat16(2 * index) for index in range(MESH_Z // 16)]
        results = []
        for table in tables:
            twice = jnp.concatenate([table, table], axis=0).astype(jnp.bfloat16)
            results.append(
                jnp.concatenate([jnp.where(mask, twice, jnp.zeros_like(twice)) for mask in here], axis=0)
            )
        return results

    def spread(turn_index, block):
        place = turn_index * blocks + block
        slab = order_ref[turn_index]
        x_base, unused, (x_table,) = cyclic_tables(0, place, (0,))
        unused, y_own, (y_table,) = cyclic_tables(1, place, (0,))
        (z_table,) = z_tables(place, (0,))
        charge = jnp.broadcast_to(charged_ref[turn_index, pl.ds(block, 1), :], (8, capacity))
        x_place = jnp.concatenate([x_base, x_base], axis=0).astype(jnp.float32).astype(jnp.bfloat16)
        low, high = [], []
        for index in range(planes):
            product = (x_table[index : index + 1] * y_table) * charge
            pair = jnp.concatenate(
                [jnp.where(y_own, product, 0.0), jnp.where(y_own, 0.0, product)], axis=0
            ).astype(jnp.bfloat16)
            if index < border:
                own = x_place <= jnp.bfloat16(index)
                low.append(jnp.where(own, pair, jnp.zeros_like(pair)))
                high.append(jnp.where(own, jnp.zeros_like(pair), pair))
            else:
                low.append(pair)
        sums = dot32(jnp.concatenate(low + high, axis=0), z_table, 1)
        row_span = pl.ds(pl.multiple_of(block * rows, rows), frame)
        for index in range(extent):
            grid_ref[slab * planes + index, row_span, :] += sums[index * frame : (index + 1) * frame]

    def spread_step(step, carry):
        spread(step // blocks, step % blocks)
        return carry

    lax.fori_loop(0, slabs * blocks, spread_step, 0, unroll=64)

    for index in range(border):
        grid_ref[index] += grid_ref[MESH_X + index]

    for load in loads:
        load.wait()
    right, left = right_ref[...], left_ref[...]
    width = widths_ref[order_ref[0]]

    def squares(dimension):
        index = lax.broadcasted_iota(jnp.int32, (MESH_X, MESH_Z), dimension)
        index = jnp.where(index * 2 > MESH_X, index - MESH_X, index).astype(jnp.float32) / MESH_X
        return index * index

    across, along = squares(0), squares(1)
    decay = -(math.pi**2) / (width * width)
    gain_ref[...] = jnp.exp(decay * across) * inverse_ref[0]
    scale = 2.0 / (math.pi * MESH_X * MESH_Y * MESH_Z)
    pair_ref[0] = gain_ref[...] * (jnp.exp(decay * along) * (inverse_ref[1] * scale))
    pair_ref[1] = across + along

    def forward(step, carry):
        both = []
        for index in range(2):
            plane = 2 * step + index
            both.append(grid_ref[plane, 0:8, :] + grid_ref[plane, MESH_Y : MESH_Y + 8, :])
            both.append(grid_ref[plane, 8:MESH_Y, :])
        along_z = cas_lanes(jnp.concatenate(both, axis=0), right)
        along_y = cas_rows(
            jnp.concatenate([along_z[:MESH_Y], along_z[MESH_Y:]], axis=1), left
        )
        for index in range(2):
            turned_ref[pl.ds(2 * step + index, MESH_Y, stride=MESH_X), :] = along_y[
                :, index * MESH_Z : (index + 1) * MESH_Z
            ]
        return carry

    lax.fori_loop(0, MESH_X // 2, forward, 0, unroll=64)

    def filtering(step, carry):
        spans = [pl.ds(pl.multiple_of((2 * step + index) * MESH_X, MESH_X), MESH_X) for index in range(2)]
        lines = jnp.concatenate([turned_ref[span, :] for span in spans], axis=1)
        spectrum = cas_rows(lines, left)
        filters = []
        for index in range(2):
            row = 2 * step + index
            frequency = jnp.where(row * 2 > MESH_Y, row - MESH_Y, row).astype(jnp.float32) / MESH_Y
            total = pair_ref[1] + frequency * frequency
            positive = total > 0
            safe = jnp.where(positive, total, 1.0)
            filters.append(jnp.where(positive, pair_ref[0] * gain_ref[pl.ds(row, 1), :] / safe, 0.0))
        lines = cas_rows(spectrum * jnp.concatenate(filters, axis=1), left)
        for index, span in enumerate(spans):
            turned_ref[span, :] = lines[:, index * MESH_Z : (index + 1) * MESH_Z]
        return carry

    lax.fori_loop(0, MESH_Y // 2, filtering, 0, unroll=64)

    def backward(step, carry):
        both = jnp.concatenate(
            [turned_ref[pl.ds(2 * step + index, MESH_Y, stride=MESH_X), :] for index in range(2)], axis=1
        )
        along_y = cas_rows(both, left)
        field = cas_lanes(
            jnp.concatenate([along_y[:, :MESH_Z], along_y[:, MESH_Z:]], axis=0), right
        )
        for index in range(2):
            plane = field[index * MESH_Y : (index + 1) * MESH_Y]
            plane = jnp.concatenate([plane, plane[:8]], axis=0)
            for block in range(blocks):
                window_ref[2 * step + index, block] = plane[block * rows : block * rows + frame].astype(jnp.bfloat16)
        return carry

    lax.fori_loop(0, MESH_X // 2, backward, 0, unroll=64)

    for index in range(border):
        window_ref[MESH_X + index] = window_ref[index]

    def gather(turn_index, block):
        place = turn_index * blocks + block
        slab = order_ref[turn_index]
        x_base, unused, (x_table, x_slope) = cyclic_tables(0, place, (0, 1))
        unused, y_own, (y_table, y_slope) = cyclic_tables(1, place, (0, 1))
        z_table, z_slope = z_tables(place, (0, 1))
        charge = charged_ref[turn_index, pl.ds(block, 1), :]
        window = jnp.concatenate(
            [window_ref[slab * planes + index, block] for index in range(extent)], axis=0
        )

        def chosen(near, index, own):
            def rows_of(plane):
                return jnp.where(
                    y_own, near[plane * frame : plane * frame + 8], near[plane * frame + 8 : plane * frame + 16]
                )

            if index < border:
                return jnp.where(own, rows_of(index), rows_of(planes + index))
            return rows_of(index)

        both = dot32(window, jnp.concatenate([z_table, z_slope], axis=1))
        near, near_z = both[:, :capacity], both[:, capacity:]
        plain = sloped = plain_z = 0.0
        for index in range(planes):
            own = x_base <= index
            part = chosen(near, index, own)
            plain += x_table[index : index + 1] * part
            sloped += x_slope[index : index + 1] * part
            plain_z += x_table[index : index + 1] * chosen(near_z, index, own)
        row = pl.ds(block, 1)
        value_ref[slab, 0, row, :] = jnp.sum(y_table * plain, axis=0, keepdims=True)
        value_ref[slab, 1, row, :] = -charge * jnp.sum(y_table * sloped, axis=0, keepdims=True)
        value_ref[slab, 2, row, :] = -charge * jnp.sum(y_slope * plain, axis=0, keepdims=True)
        value_ref[slab, 3, row, :] = -charge * jnp.sum(y_table * plain_z, axis=0, keepdims=True)

    def gather_step(step, carry):
        gather(step // blocks, step % blocks)
        return carry

    lax.fori_loop(0, slabs * blocks, gather_step, 0, unroll=64)
    halves = capacity // 128
    lines = lax.broadcasted_iota(jnp.int32, (4 * halves, 128), 0)
    shift = 1.5 * 2.0**23

    def encode(slab, carry):
        pieces = [
            value_ref[slab, kind, :, half * 128 : (half + 1) * 128] for kind in range(4) for half in range(halves)
        ]
        largest = jnp.zeros((4 * halves, 128), jnp.float32)
        for line, piece in enumerate(pieces):
            largest = jnp.where(lines == line, jnp.max(jnp.abs(piece), axis=0, keepdims=True), largest)
        level = level_of(largest)
        inverse_scale = power_of_two(level, -1)
        for line, piece in enumerate(pieces):
            codes = (piece * inverse_scale[line : line + 1] + shift) - shift
            out_ref[slab, pl.ds(line * blocks, blocks), :] = codes.astype(jnp.int32).astype(jnp.int16)
        rest = jnp.zeros((blocks - 4 * halves, 128), jnp.int32)
        out_ref[slab, pl.ds(4 * halves * blocks, blocks), :] = jnp.concatenate([level, rest], axis=0).astype(jnp.int16)
        return carry

    lax.fori_loop(0, slabs, encode, 0, unroll=8)


def channel_shards(charges, cell_offset, base_cell, counts, widths):
    device = lax.axis_index("wide")
    channels, slot_count = charges.shape
    blocks = counts.shape[0]
    capacity = slot_count // blocks
    slabs = lax.axis_size("wide")
    live_mask = jnp.arange(capacity, dtype=jnp.int32)[None, :] < counts[:, None]
    charge_blocks = jnp.where(
        live_mask[None], charges.reshape(channels, blocks, capacity), jnp.zeros((), jnp.bfloat16)
    )
    cells = base_cell.astype(jnp.bfloat16).reshape(1, 3, blocks, capacity)
    offsets = cell_offset.reshape(1, 3, blocks, capacity)
    parts = charge_blocks[None]
    order = jnp.zeros((1,), jnp.int32)
    distance = slabs // 2
    while distance > 0:
        route = [(index, index ^ distance) for index in range(slabs)]
        upper = (device & distance) > 0
        first, second = parts[:, :distance], parts[:, distance:]
        kept, sent = jnp.where(upper, second, first), jnp.where(upper, first, second)
        count = cells.shape[0]
        bundle = jnp.concatenate([cells.reshape((-1,) + cells.shape[2:]), sent.reshape((-1,) + sent.shape[2:])], axis=0)
        arrived = lax.ppermute(offsets, "wide", route)
        bundle = lax.ppermute(bundle, "wide", route)
        order = jnp.concatenate([order, order ^ distance])
        if distance > 1:
            offsets = jnp.concatenate([offsets, arrived], axis=0)
            cells = jnp.concatenate([cells, bundle[: 3 * count].reshape(cells.shape)], axis=0)
            parts = jnp.concatenate([kept, bundle[3 * count :].reshape(kept.shape)], axis=0)
        distance //= 2
    order = order ^ device

    points = np.arange(MESH_X)
    first = np.array([1.0, 26.0, 66.0, 26.0, 1.0, 0.0]) / 120.0
    angles = 2.0 * math.pi * points[:, None] * np.arange(ORDER)[None, :] / MESH_X
    inverse = (1.0 / ((np.cos(angles) @ first) ** 2 + (np.sin(angles) @ first) ** 2)).astype(np.float32)
    inverse = np.stack([np.repeat(inverse[:, None], MESH_Z, axis=1), np.repeat(inverse[None], MESH_X, axis=0)])
    one, two = cas_terms(MESH_X)
    right = np.concatenate([np.concatenate([one, two], axis=1)] * 2, axis=0)
    left = np.concatenate([np.concatenate([one, one], axis=1), np.concatenate([two, two], axis=1)], axis=0)

    halves = capacity // 128
    whole = pl.BlockSpec(memory_space=pltpu.VMEM)
    away = pl.BlockSpec(memory_space=pltpu.HBM)
    scalars = pl.BlockSpec(memory_space=pltpu.SMEM)
    result = pl.pallas_call(
        channel_kernel,
        out_shape=jax.ShapeDtypeStruct((slabs, (4 * halves + 1) * blocks, 128), jnp.int16),
        in_specs=[whole] * 5 + [away] + [scalars] * 2 + [away] * 2,
        out_specs=whole,
        scratch_shapes=[
            pltpu.VMEM((MESH_X + ORDER - 1, MESH_Y + 8, MESH_Z), jnp.float32),
            pltpu.VMEM((MESH_X * MESH_Y + MESH_X, MESH_Z), jnp.float32),
            pltpu.VMEM((MESH_X + ORDER - 1, blocks, 16, MESH_Z), jnp.bfloat16),
            pltpu.VMEM((6, capacity // 128, slabs * blocks * 8 + 8, 128), jnp.float32),
            pltpu.VMEM((4, slabs * blocks, capacity), jnp.int32),
            pltpu.VMEM((2, MESH_X, MESH_Z), jnp.float32),
            pltpu.VMEM((MESH_Y, MESH_Z), jnp.float32),
            pltpu.VMEM((slabs, 4, blocks, capacity), jnp.float32),
            pltpu.VMEM((slabs, blocks, capacity), jnp.float32),
            pltpu.VMEM(inverse.shape, jnp.float32),
            pltpu.VMEM(right.shape, jnp.bfloat16),
            pltpu.VMEM(left.shape, jnp.bfloat16),
            pltpu.SemaphoreType.DMA,
            pltpu.SemaphoreType.DMA,
            pltpu.SemaphoreType.DMA,
        ],
        compiler_params=pltpu.CompilerParams(vmem_limit_bytes=52 * 1024 * 1024),
        name="channel",
    )(
        offsets, cells, kept[:, 0], arrived, bundle, jnp.asarray(inverse), order, widths,
        jnp.asarray(right), jnp.asarray(left),
    )
    returned = lax.all_to_all(result, "wide", split_axis=0, concat_axis=0, tiled=True)
    codes = returned[:, : 4 * halves * blocks].reshape(channels, 4, halves, blocks, 128)
    levels = returned[:, 4 * halves * blocks : 4 * halves * blocks + 4 * halves].astype(jnp.int32)
    scales = power_of_two(levels, 1).reshape(channels, 4, halves, 1, 128)
    values = codes.astype(jnp.float32) * scales
    potential = jnp.moveaxis(values[:, 0], 1, 2).reshape(channels, blocks, capacity)
    atom_potential = jnp.where(live_mask[None], potential, 0.0).reshape(channels, slot_count)
    forces = jnp.moveaxis(jnp.sum(values[:, 1:], axis=0), 1, 2).reshape(3, slot_count)
    return (atom_potential, forces)


def shards(charges, cell_offset, base_cell, counts, widths):
    if lax.axis_size("wide") == charges.shape[0] and MESH_X == 8 * lax.axis_size("wide"):
        return channel_shards(charges, cell_offset, base_cell, counts, widths)
    return slab_shards(charges, cell_offset, base_cell, counts, widths)


def solution(mesh):
    in_specs = (
        P(None, ("groups", "wide")),
        P(None, ("groups", "wide")),
        P(None, ("groups", "wide")),
        P(("groups", "wide")),
        P(),
    )
    out_specs = (P(None, ("groups", "wide")), P(None, ("groups", "wide")))
    return jax.shard_map(shards, mesh=mesh, in_specs=in_specs, out_specs=out_specs, check_vma=False)
```

```python
import functools
import math

import jax
import jax.numpy as jnp
import numpy as np
from jax import lax
from jax.experimental import pallas as pl
from jax.experimental.pallas import tpu as pltpu
from jax.sharding import PartitionSpec as P

MESH_X = 128
MESH_Y = 128
MESH_Z = 128
ORDER = 6


highest = lax.Precision.HIGHEST


def shifted(block, axis, distance):
    devices = range(lax.axis_size(axis))
    route = [((i - distance) % len(devices), i) for i in devices]
    return lax.ppermute(block, axis, route)


def spline_lists(offset, order_count):
    weights = [1.0 - offset, offset]
    slopes = [-jnp.ones_like(offset), jnp.ones_like(offset)]
    for degree in range(3, order_count + 1):
        if degree == order_count:
            slopes = (
                [-weights[0]]
                + [weights[position - 1] - weights[position] for position in range(1, degree - 1)]
                + [weights[degree - 2]]
            )
        factor = 1.0 / (degree - 1)
        updated = [None] * degree
        updated[degree - 1] = factor * offset * weights[degree - 2]
        for position in range(1, degree - 1):
            updated[degree - position - 1] = factor * (
                (offset + position) * weights[degree - position - 2]
                + (degree - position - offset) * weights[degree - position - 1]
            )
        updated[0] = factor * (1.0 - offset) * weights[0]
        weights = updated
    return (weights, slopes)


def spline_table(offset, order_count):
    weights, slopes = spline_lists(offset, order_count)
    return (jnp.stack(weights), jnp.stack(slopes))


def stencil_rows(weights, slopes, relative, extent, period):
    shifts = jnp.arange(weights.shape[0], dtype=jnp.int32)[None, :, None]
    targets = (relative[:, None, :] + shifts) % period
    points = jnp.arange(extent, dtype=jnp.int32)[None, :, None, None]
    matches = points == targets[:, None]
    plain_rows = jnp.sum(jnp.where(matches, jnp.moveaxis(weights, 0, 1)[:, None], 0.0), axis=2)
    slope_rows = jnp.sum(jnp.where(matches, jnp.moveaxis(slopes, 0, 1)[:, None], 0.0), axis=2)
    return (plain_rows, slope_rows)


def folded(points, length):
    values = jnp.where(points * 2 > length, points - length, points)
    return values.astype(jnp.float32) / length


def moduli(points, length):
    base_weights, base_slopes = spline_table(jnp.zeros((1,), jnp.float32), ORDER)
    shifts = jnp.arange(ORDER, dtype=jnp.int32)
    phases = points[:, None] * shifts[None, :] % length
    angles = phases.astype(jnp.float32) * (2.0 * math.pi / length)
    real_sum = jnp.sum(base_weights[:, 0][None, :] * jnp.cos(angles), axis=1)
    imag_sum = jnp.sum(base_weights[:, 0][None, :] * jnp.sin(angles), axis=1)
    return real_sum * real_sum + imag_sum * imag_sum


def kernel_table(widths, x_freq, y_freq, z_freq, x_mod, y_mod, z_mod):
    total = (
        x_freq[:, None, None, None] ** 2
        + y_freq[None, :, None, None] ** 2
        + z_freq[None, None, None, :] ** 2
    )
    positive = total > 0
    safe = jnp.where(positive, total, 1.0)
    beta = widths[None, None, :, None]
    divisor = x_mod[:, None, None, None] * y_mod[None, :, None, None] * z_mod[None, None, None, :]
    return jnp.where(
        positive,
        2.0 * jnp.exp(-math.pi**2 * total / (beta * beta)) / (math.pi * safe * divisor),
        0.0,
    )


def dft_tables(length):
    points = jnp.arange(length, dtype=jnp.int32)
    phases = points[:, None] * points[None, :] % length
    angles = phases.astype(jnp.float32) * (2.0 * math.pi / length)
    return (jnp.cos(angles), jnp.sin(angles))


def combine_blocks(block_grid, block_rows, border):
    owned = block_grid[:, :, :block_rows]
    overflow = jnp.roll(block_grid[:, :, block_rows:], 1, axis=0)
    owned = owned.at[:, :, :border].add(overflow)
    moved = jnp.moveaxis(owned, 0, 1)
    return moved.reshape((moved.shape[0], moved.shape[1] * moved.shape[2]) + moved.shape[3:])


def contract(data, x_weights, y_weights):
    return jnp.einsum("pycs,ps,ys->cs", data, x_weights, y_weights, precision=highest)


def turn(real_part, imag_part, cosines, sines, orient, pattern):

    def project(data, table):
        return jnp.einsum(pattern, data, table, precision=highest)

    real_out = project(real_part, cosines) - orient * project(imag_part, sines)
    imag_out = project(imag_part, cosines) + orient * project(real_part, sines)
    return jnp.stack([real_out, imag_out])


def slab_shards(charges, cell_offset, base_cell, counts, widths):
    wide_size = lax.axis_size("wide")
    device = lax.axis_index("wide")
    channels, slot_count = charges.shape
    blocks = counts.shape[0]
    capacity = slot_count // blocks
    planes = MESH_X // wide_size
    border = ORDER - 1
    extent = planes + border
    block_rows = MESH_Y // blocks
    y_extent = block_rows + border
    rounds = (border + planes - 1) // planes
    y_local = MESH_Y // wide_size
    live_mask = jnp.arange(capacity, dtype=jnp.int32)[None, :] < counts[:, None]
    charge_blocks = jnp.where(
        live_mask[:, None, :],
        jnp.moveaxis(charges.reshape(channels, blocks, capacity), 0, 1),
        jnp.zeros((), jnp.bfloat16),
    )
    offsets = cell_offset.reshape(3, blocks, capacity)
    bases = base_cell.reshape(3, blocks, capacity)
    x_weights, x_slopes = spline_table(offsets[0], ORDER)
    y_weights, y_slopes = spline_table(offsets[1], ORDER)
    z_weights, z_slopes = spline_table(offsets[2], ORDER)
    row_start = jnp.arange(blocks, dtype=jnp.int32)[:, None] * block_rows
    x_rows, x_drows = stencil_rows(x_weights, x_slopes, bases[0] - device * planes, extent, extent)
    y_rows, y_drows = stencil_rows(y_weights, y_slopes, bases[1] - row_start, y_extent, y_extent)
    z_plain, z_slope = stencil_rows(z_weights, z_slopes, bases[2], MESH_Z, MESH_Z)
    z_table = jnp.stack([z_plain, z_slope], axis=2).astype(jnp.bfloat16)

    def spread_block(inputs):
        x_block, y_block, charge_block, table_block = inputs
        products = (
            x_block[:, None, None, :]
            * y_block[None, :, None, :]
            * charge_block.astype(jnp.float32)[None, None]
        ).astype(jnp.bfloat16)
        spread = jnp.einsum(
            "rs,zs->rz",
            products.reshape(-1, capacity),
            table_block[:, 0],
            preferred_element_type=jnp.float32,
        )
        return spread.reshape(extent, y_extent, channels, MESH_Z)

    block_grid = lax.map(spread_block, (x_rows, y_rows, charge_blocks, z_table))
    grid_ext = combine_blocks(block_grid, block_rows, border)
    z_cos, z_sin = dft_tables(MESH_Z)
    y_cos, y_sin = dft_tables(MESH_Y)
    x_cos, x_sin = dft_tables(MESH_X)
    x_points = jnp.arange(MESH_X, dtype=jnp.int32)
    y_points = device * y_local + jnp.arange(y_local, dtype=jnp.int32)
    z_points = jnp.arange(MESH_Z, dtype=jnp.int32)
    kernel = kernel_table(
        widths,
        folded(x_points, MESH_X),
        folded(y_points, MESH_Y),
        folded(z_points, MESH_Z),
        moduli(x_points, MESH_X),
        moduli(y_points, MESH_Y),
        moduli(z_points, MESH_Z),
    )
    kernel = kernel / float(MESH_X * MESH_Y * MESH_Z)
    owned = grid_ext[:planes]
    for hop_index in range(1, rounds + 1):
        outgoing = grid_ext[hop_index * planes : (hop_index + 1) * planes]
        outgoing = jnp.pad(outgoing, ((0, planes - outgoing.shape[0]), (0, 0), (0, 0), (0, 0)))
        owned = owned + shifted(outgoing, "wide", hop_index)
    real_z = jnp.dot(owned, z_cos, precision=highest)
    imag_z = -jnp.dot(owned, z_sin, precision=highest)
    columns = lax.all_to_all(
        turn(real_z, imag_z, y_cos, y_sin, -1.0, "pycz,yk->pkcz"),
        "wide",
        split_axis=2,
        concat_axis=1,
        tiled=True,
    )
    spectrum = turn(columns[0], columns[1], x_cos, x_sin, -1.0, "xycz,xk->kycz")
    filtered = turn(spectrum[0] * kernel, spectrum[1] * kernel, x_cos, x_sin, 1.0, "xycz,xk->kycz")
    returned = lax.all_to_all(filtered, "wide", split_axis=1, concat_axis=2, tiled=True)
    along_y = turn(returned[0], returned[1], y_cos, y_sin, 1.0, "pycz,yk->pkcz")
    potential_own = (
        jnp.dot(along_y[0], z_cos, precision=highest)
        - jnp.dot(along_y[1], z_sin, precision=highest)
    ).astype(jnp.bfloat16)
    pieces = [potential_own]
    for hop_index in range(1, rounds + 1):
        pieces.append(shifted(potential_own, "wide", -hop_index))
    potential_ext = jnp.concatenate(pieces, axis=0)[:extent]
    blocked = potential_ext.reshape(extent, blocks, block_rows, channels, MESH_Z)
    following = jnp.roll(blocked[:, :, :border], -1, axis=1)
    windows = jnp.moveaxis(jnp.concatenate([blocked, following], axis=2), 1, 0)

    def gather_block(inputs):
        window, x_block, x_dblock, y_block, y_dblock, table_block, charge_block, live_block = inputs
        values = jnp.dot(
            window.reshape(-1, MESH_Z),
            table_block.reshape(MESH_Z, -1),
            preferred_element_type=jnp.float32,
        )
        values = values.reshape(extent, y_extent, channels, 2, capacity)
        direct = values[:, :, :, 0]
        sloped = values[:, :, :, 1]
        potential = jnp.where(live_block[None], contract(direct, x_block, y_block), 0.0)
        gradient = jnp.stack(
            [
                contract(direct, x_dblock, y_block),
                contract(direct, x_block, y_dblock),
                contract(sloped, x_block, y_block),
            ]
        )
        forces = -jnp.sum(gradient * charge_block.astype(jnp.float32)[None], axis=1)
        return (potential, forces)

    potentials, forces = lax.map(
        gather_block, (windows, x_rows, x_drows, y_rows, y_drows, z_table, charge_blocks, live_mask)
    )
    atom_potential = jnp.moveaxis(potentials, 0, 1).reshape(channels, slot_count)
    atom_forces = jnp.moveaxis(forces, 0, 1).reshape(3, slot_count)
    return (atom_potential, atom_forces)


def cas_terms(length):
    points = np.arange(length)
    angles = (points[:, None] * points[None, :] % length) * (2.0 * math.pi / length)
    left = (np.cos(angles) + np.sin(angles)).astype(np.float32)
    terms = []
    for _ in range(2):
        term = left.astype(jnp.bfloat16)
        terms.append(term)
        left = left - term.astype(np.float32)
    return terms


def split(values):
    first = values.astype(jnp.bfloat16)
    return first, (values - first.astype(jnp.float32)).astype(jnp.bfloat16)


def dot32(a, b, contract_b=0):
    return lax.dot_general(a, b, (((1,), (contract_b,)), ((), ())), preferred_element_type=jnp.float32)


def cas_lanes(values, right):
    sums = dot32(jnp.concatenate(split(values), axis=1), right)
    length = values.shape[1]
    return sums[:, :length] + sums[:, length:]


def cas_rows(values, left):
    sums = dot32(left, jnp.concatenate(split(values), axis=0))
    length = values.shape[0]
    return sums[:length] + sums[length:]


def level_of(largest):
    logarithm = jnp.log(jnp.maximum(largest, 1e-36)) * (1.0 / math.log(2.0))
    level = jnp.floor(logarithm + 1e-3).astype(jnp.int32) + 1 - 15 + 126
    return jnp.clip(level, 0, 250)


def power_of_two(level, sign):
    value = jnp.full(level.shape, 2.0 ** (-126 * sign), jnp.float32)
    for bit in range(7):
        value = value * jnp.where((level >> bit) & 1 > 0, 2.0 ** (sign * 2**bit), 1.0)
    return value * jnp.where((level >> 7) & 1 > 0, 2.0 ** (sign * 64), 1.0) * jnp.where((level >> 7) & 1 > 0, 2.0 ** (sign * 64), 1.0)


def channel_kernel(
    offset_ref, base_ref, charge_ref, far_offset_ref, far_ref, inverse_hbm, order_ref, widths_ref,
    right_hbm, left_hbm, out_ref,
    grid_ref, turned_ref, window_ref, spline_ref, place_ref, pair_ref, gain_ref, value_ref, charged_ref,
    inverse_ref, right_ref, left_ref, inverse_done, right_done, left_done,
):
    near, _, blocks, capacity = offset_ref.shape
    slabs = 2 * near
    planes = MESH_X // slabs
    rows = MESH_Y // blocks
    border = ORDER - 1
    frame = 16
    extent = planes + border
    far = MESH_X + border

    loads = [
        pltpu.make_async_copy(inverse_hbm, inverse_ref, inverse_done),
        pltpu.make_async_copy(right_hbm, right_ref, right_done),
        pltpu.make_async_copy(left_hbm, left_ref, left_done),
    ]
    for load in loads:
        load.start()

    def prepare(slab, offset_at, base_at, charge):
        span = pl.ds(pl.multiple_of(slab * blocks, blocks), blocks)
        charged_ref[slab] = charge.astype(jnp.float32)
        bases = [base_at(dimension).astype(jnp.float32).astype(jnp.int32) for dimension in range(3)]
        place_ref[0, span, :] = bases[0] & 7
        place_ref[1, span, :] = bases[1] & 7
        place_ref[2, span, :] = bases[2] & 7
        place_ref[3, span, :] = bases[2] >> 3
        for dimension in range(3):
            weights, slopes = spline_lists(offset_at(dimension), ORDER)
            for kind, values in enumerate((weights, slopes)):
                for position in range(8):
                    value = values[position] if position < ORDER else jnp.zeros_like(values[0])
                    for half in range(capacity // 128):
                        spline_ref[
                            2 * dimension + kind, half, pl.ds(slab * blocks * 8 + position, blocks, stride=8), :
                        ] = value[:, half * 128 : (half + 1) * 128]

    def prepare_both(index, carry):
        prepare(
            index,
            lambda dimension: offset_ref[index, dimension],
            lambda dimension: base_ref[index, dimension],
            charge_ref[index],
        )
        prepare(
            near + index,
            lambda dimension: far_offset_ref[index, dimension],
            lambda dimension: far_ref[3 * index + dimension],
            far_ref[3 * near + index],
        )
        return carry

    lax.fori_loop(0, near, prepare_both, 0)

    def clear(plane, carry):
        grid_ref[plane] = jnp.zeros(grid_ref.shape[1:], jnp.float32)
        return carry

    lax.fori_loop(0, far, clear, 0)
    points = lax.broadcasted_iota(jnp.int32, (8, capacity), 0)

    def row_of(dimension, block):
        return jnp.broadcast_to(place_ref[dimension, pl.ds(block, 1), :], (8, capacity))

    def cyclic_tables(dimension, block, kinds):
        base = row_of(dimension, block)
        index = (points - base) & 7
        span = pl.ds(pl.multiple_of(block * 8, 8), 8)
        tables = []
        for kind in kinds:
            values = jnp.concatenate(
                [spline_ref[2 * dimension + kind, half, span, :] for half in range(capacity // 128)], axis=1
            )
            tables.append(jnp.take_along_axis(values, index, axis=0, mode="promise_in_bounds"))
        return base, points >= base, tables

    def z_tables(block, kinds):
        unused, own, tables = cyclic_tables(2, block, kinds)
        tile = row_of(3, block)
        tile = jnp.where(own, tile, (tile + 1) & (MESH_Z // 8 - 1)).astype(jnp.float32)
        tile = jnp.concatenate([tile, tile - 1.0], axis=0).astype(jnp.bfloat16)
        here = [tile == jnp.bfloat16(2 * index) for index in range(MESH_Z // 16)]
        results = []
        for table in tables:
            twice = jnp.concatenate([table, table], axis=0).astype(jnp.bfloat16)
            results.append(
                jnp.concatenate([jnp.where(mask, twice, jnp.zeros_like(twice)) for mask in here], axis=0)
            )
        return results

    def spread(turn_index, block):
        place = turn_index * blocks + block
        slab = order_ref[turn_index]
        x_base, unused, (x_table,) = cyclic_tables(0, place, (0,))
        unused, y_own, (y_table,) = cyclic_tables(1, place, (0,))
        (z_table,) = z_tables(place, (0,))
        charge = jnp.broadcast_to(charged_ref[turn_index, pl.ds(block, 1), :], (8, capacity))
        x_place = jnp.concatenate([x_base, x_base], axis=0).astype(jnp.float32).astype(jnp.bfloat16)
        low, high = [], []
        for index in range(planes):
            product = (x_table[index : index + 1] * y_table) * charge
            pair = jnp.concatenate(
                [jnp.where(y_own, product, 0.0), jnp.where(y_own, 0.0, product)], axis=0
            ).astype(jnp.bfloat16)
            if index < border:
                own = x_place <= jnp.bfloat16(index)
                low.append(jnp.where(own, pair, jnp.zeros_like(pair)))
                high.append(jnp.where(own, jnp.zeros_like(pair), pair))
            else:
                low.append(pair)
        sums = dot32(jnp.concatenate(low + high, axis=0), z_table, 1)
        row_span = pl.ds(pl.multiple_of(block * rows, rows), frame)
        for index in range(extent):
            grid_ref[slab * planes + index, row_span, :] += sums[index * frame : (index + 1) * frame]

    def spread_step(step, carry):
        spread(step // blocks, step % blocks)
        return carry

    lax.fori_loop(0, slabs * blocks, spread_step, 0, unroll=64)

    for index in range(border):
        grid_ref[index] += grid_ref[MESH_X + index]

    for load in loads:
        load.wait()
    right, left = right_ref[...], left_ref[...]
    width = widths_ref[order_ref[0]]

    def squares(dimension):
        index = lax.broadcasted_iota(jnp.int32, (MESH_X, MESH_Z), dimension)
        index = jnp.where(index * 2 > MESH_X, index - MESH_X, index).astype(jnp.float32) / MESH_X
        return index * index

    across, along = squares(0), squares(1)
    decay = -(math.pi**2) / (width * width)
    gain_ref[...] = jnp.exp(decay * across) * inverse_ref[0]
    scale = 2.0 / (math.pi * MESH_X * MESH_Y * MESH_Z)
    pair_ref[0] = gain_ref[...] * (jnp.exp(decay * along) * (inverse_ref[1] * scale))
    pair_ref[1] = across + along

    def forward(step, carry):
        both = []
        for index in range(2):
            plane = 2 * step + index
            both.append(grid_ref[plane, 0:8, :] + grid_ref[plane, MESH_Y : MESH_Y + 8, :])
            both.append(grid_ref[plane, 8:MESH_Y, :])
        along_z = cas_lanes(jnp.concatenate(both, axis=0), right)
        along_y = cas_rows(
            jnp.concatenate([along_z[:MESH_Y], along_z[MESH_Y:]], axis=1), left
        )
        for index in range(2):
            turned_ref[pl.ds(2 * step + index, MESH_Y, stride=MESH_X), :] = along_y[
                :, index * MESH_Z : (index + 1) * MESH_Z
            ]
        return carry

    lax.fori_loop(0, MESH_X // 2, forward, 0, unroll=64)

    def filtering(step, carry):
        spans = [pl.ds(pl.multiple_of((2 * step + index) * MESH_X, MESH_X), MESH_X) for index in range(2)]
        lines = jnp.concatenate([turned_ref[span, :] for span in spans], axis=1)
        spectrum = cas_rows(lines, left)
        filters = []
        for index in range(2):
            row = 2 * step + index
            frequency = jnp.where(row * 2 > MESH_Y, row - MESH_Y, row).astype(jnp.float32) / MESH_Y
            total = pair_ref[1] + frequency * frequency
            positive = total > 0
            safe = jnp.where(positive, total, 1.0)
            filters.append(jnp.where(positive, pair_ref[0] * gain_ref[pl.ds(row, 1), :] / safe, 0.0))
        lines = cas_rows(spectrum * jnp.concatenate(filters, axis=1), left)
        for index, span in enumerate(spans):
            turned_ref[span, :] = lines[:, index * MESH_Z : (index + 1) * MESH_Z]
        return carry

    lax.fori_loop(0, MESH_Y // 2, filtering, 0, unroll=64)

    def backward(step, carry):
        both = jnp.concatenate(
            [turned_ref[pl.ds(2 * step + index, MESH_Y, stride=MESH_X), :] for index in range(2)], axis=1
        )
        along_y = cas_rows(both, left)
        field = cas_lanes(
            jnp.concatenate([along_y[:, :MESH_Z], along_y[:, MESH_Z:]], axis=0), right
        )
        for index in range(2):
            plane = field[index * MESH_Y : (index + 1) * MESH_Y]
            plane = jnp.concatenate([plane, plane[:8]], axis=0)
            for block in range(blocks):
                window_ref[2 * step + index, block] = plane[block * rows : block * rows + frame].astype(jnp.bfloat16)
        return carry

    lax.fori_loop(0, MESH_X // 2, backward, 0, unroll=64)

    for index in range(border):
        window_ref[MESH_X + index] = window_ref[index]

    def gather(turn_index, block):
        place = turn_index * blocks + block
        slab = order_ref[turn_index]
        x_base, unused, (x_table, x_slope) = cyclic_tables(0, place, (0, 1))
        unused, y_own, (y_table, y_slope) = cyclic_tables(1, place, (0, 1))
        z_table, z_slope = z_tables(place, (0, 1))
        charge = charged_ref[turn_index, pl.ds(block, 1), :]
        window = jnp.concatenate(
            [window_ref[slab * planes + index, block] for index in range(extent)], axis=0
        )

        def chosen(near, index, own):
            def rows_of(plane):
                return jnp.where(
                    y_own, near[plane * frame : plane * frame + 8], near[plane * frame + 8 : plane * frame + 16]
                )

            if index < border:
                return jnp.where(own, rows_of(index), rows_of(planes + index))
            return rows_of(index)

        both = dot32(window, jnp.concatenate([z_table, z_slope], axis=1))
        near, near_z = both[:, :capacity], both[:, capacity:]
        plain = sloped = plain_z = 0.0
        for index in range(planes):
            own = x_base <= index
            part = chosen(near, index, own)
            plain += x_table[index : index + 1] * part
            sloped += x_slope[index : index + 1] * part
            plain_z += x_table[index : index + 1] * chosen(near_z, index, own)
        row = pl.ds(block, 1)
        value_ref[slab, 0, row, :] = jnp.sum(y_table * plain, axis=0, keepdims=True)
        value_ref[slab, 1, row, :] = -charge * jnp.sum(y_table * sloped, axis=0, keepdims=True)
        value_ref[slab, 2, row, :] = -charge * jnp.sum(y_slope * plain, axis=0, keepdims=True)
        value_ref[slab, 3, row, :] = -charge * jnp.sum(y_table * plain_z, axis=0, keepdims=True)

    def gather_step(step, carry):
        gather(step // blocks, step % blocks)
        return carry

    lax.fori_loop(0, slabs * blocks, gather_step, 0, unroll=64)
    halves = capacity // 128
    lines = lax.broadcasted_iota(jnp.int32, (4 * halves, 128), 0)
    shift = 1.5 * 2.0**23

    def encode(slab, carry):
        pieces = [
            value_ref[slab, kind, :, half * 128 : (half + 1) * 128] for kind in range(4) for half in range(halves)
        ]
        largest = jnp.zeros((4 * halves, 128), jnp.float32)
        for line, piece in enumerate(pieces):
            largest = jnp.where(lines == line, jnp.max(jnp.abs(piece), axis=0, keepdims=True), largest)
        level = level_of(largest)
        inverse_scale = power_of_two(level, -1)
        for line, piece in enumerate(pieces):
            codes = (piece * inverse_scale[line : line + 1] + shift) - shift
            out_ref[slab, pl.ds(line * blocks, blocks), :] = codes.astype(jnp.int32).astype(jnp.int16)
        rest = jnp.zeros((blocks - 4 * halves, 128), jnp.int32)
        out_ref[slab, pl.ds(4 * halves * blocks, blocks), :] = jnp.concatenate([level, rest], axis=0).astype(jnp.int16)
        return carry

    lax.fori_loop(0, slabs, encode, 0, unroll=8)


def channel_shards(charges, cell_offset, base_cell, counts, widths):
    device = lax.axis_index("wide")
    channels, slot_count = charges.shape
    blocks = counts.shape[0]
    capacity = slot_count // blocks
    slabs = lax.axis_size("wide")
    live_mask = jnp.arange(capacity, dtype=jnp.int32)[None, :] < counts[:, None]
    charge_blocks = jnp.where(
        live_mask[None], charges.reshape(channels, blocks, capacity), jnp.zeros((), jnp.bfloat16)
    )
    cells = base_cell.astype(jnp.bfloat16).reshape(1, 3, blocks, capacity)
    offsets = cell_offset.reshape(1, 3, blocks, capacity)
    parts = charge_blocks[None]
    order = jnp.zeros((1,), jnp.int32)
    distance = slabs // 2
    ahead = 2
    ahead_route = [(index, index ^ ahead) for index in range(slabs)]
    early_offsets = lax.ppermute(offsets, "wide", ahead_route)
    early_cells = lax.ppermute(cells, "wide", ahead_route)
    while distance > 0:
        route = [(index, index ^ distance) for index in range(slabs)]
        known = 1 if distance == ahead else 0
        upper = (device & distance) > 0
        first, second = parts[:, :distance], parts[:, distance:]
        kept, sent = jnp.where(upper, second, first), jnp.where(upper, first, second)
        count = cells.shape[0]
        bundle = jnp.concatenate([cells[known:].reshape((-1,) + cells.shape[2:]), sent.reshape((-1,) + sent.shape[2:])], axis=0)
        arrived = lax.ppermute(offsets[known:], "wide", route)
        bundle = lax.ppermute(bundle, "wide", route)
        order = jnp.concatenate([order, order ^ distance])
        if distance > 1:
            offsets = jnp.concatenate([offsets, early_offsets, arrived] if known else [offsets, arrived], axis=0)
            fresh = bundle[: 3 * (count - known)].reshape((-1,) + cells.shape[1:])
            cells = jnp.concatenate([cells, early_cells, fresh] if known else [cells, fresh], axis=0)
            parts = jnp.concatenate([kept, bundle[3 * (count - known) :].reshape(kept.shape)], axis=0)
        distance //= 2
    order = order ^ device

    points = np.arange(MESH_X)
    first = np.array([1.0, 26.0, 66.0, 26.0, 1.0, 0.0]) / 120.0
    angles = 2.0 * math.pi * points[:, None] * np.arange(ORDER)[None, :] / MESH_X
    inverse = (1.0 / ((np.cos(angles) @ first) ** 2 + (np.sin(angles) @ first) ** 2)).astype(np.float32)
    inverse = np.stack([np.repeat(inverse[:, None], MESH_Z, axis=1), np.repeat(inverse[None], MESH_X, axis=0)])
    one, two = cas_terms(MESH_X)
    right = np.concatenate([np.concatenate([one, two], axis=1)] * 2, axis=0)
    left = np.concatenate([np.concatenate([one, one], axis=1), np.concatenate([two, two], axis=1)], axis=0)

    halves = capacity // 128
    whole = pl.BlockSpec(memory_space=pltpu.VMEM)
    away = pl.BlockSpec(memory_space=pltpu.HBM)
    scalars = pl.BlockSpec(memory_space=pltpu.SMEM)
    result = pl.pallas_call(
        channel_kernel,
        out_shape=jax.ShapeDtypeStruct((slabs, (4 * halves + 1) * blocks, 128), jnp.int16),
        in_specs=[whole] * 5 + [away] + [scalars] * 2 + [away] * 2,
        out_specs=whole,
        scratch_shapes=[
            pltpu.VMEM((MESH_X + ORDER - 1, MESH_Y + 8, MESH_Z), jnp.float32),
            pltpu.VMEM((MESH_X * MESH_Y + MESH_X, MESH_Z), jnp.float32),
            pltpu.VMEM((MESH_X + ORDER - 1, blocks, 16, MESH_Z), jnp.bfloat16),
            pltpu.VMEM((6, capacity // 128, slabs * blocks * 8 + 8, 128), jnp.float32),
            pltpu.VMEM((4, slabs * blocks, capacity), jnp.int32),
            pltpu.VMEM((2, MESH_X, MESH_Z), jnp.float32),
            pltpu.VMEM((MESH_Y, MESH_Z), jnp.float32),
            pltpu.VMEM((slabs, 4, blocks, capacity), jnp.float32),
            pltpu.VMEM((slabs, blocks, capacity), jnp.float32),
            pltpu.VMEM(inverse.shape, jnp.float32),
            pltpu.VMEM(right.shape, jnp.bfloat16),
            pltpu.VMEM(left.shape, jnp.bfloat16),
            pltpu.SemaphoreType.DMA,
            pltpu.SemaphoreType.DMA,
            pltpu.SemaphoreType.DMA,
        ],
        compiler_params=pltpu.CompilerParams(vmem_limit_bytes=52 * 1024 * 1024),
        name="channel",
    )(
        offsets, cells, kept[:, 0], arrived, bundle, jnp.asarray(inverse), order, widths,
        jnp.asarray(right), jnp.asarray(left),
    )
    returned = lax.all_to_all(result, "wide", split_axis=0, concat_axis=0, tiled=True)
    codes = returned[:, : 4 * halves * blocks].reshape(channels, 4, halves, blocks, 128)
    levels = returned[:, 4 * halves * blocks : 4 * halves * blocks + 4 * halves].astype(jnp.int32)
    scales = power_of_two(levels, 1).reshape(channels, 4, halves, 1, 128)
    values = codes.astype(jnp.float32) * scales
    potential = jnp.moveaxis(values[:, 0], 1, 2).reshape(channels, blocks, capacity)
    atom_potential = jnp.where(live_mask[None], potential, 0.0).reshape(channels, slot_count)
    forces = jnp.moveaxis(jnp.sum(values[:, 1:], axis=0), 1, 2).reshape(3, slot_count)
    return (atom_potential, forces)


def shards(charges, cell_offset, base_cell, counts, widths):
    if lax.axis_size("wide") == charges.shape[0] and MESH_X == 8 * lax.axis_size("wide"):
        return channel_shards(charges, cell_offset, base_cell, counts, widths)
    return slab_shards(charges, cell_offset, base_cell, counts, widths)


def solution(mesh):
    in_specs = (
        P(None, ("groups", "wide")),
        P(None, ("groups", "wide")),
        P(None, ("groups", "wide")),
        P(("groups", "wide")),
        P(),
    )
    out_specs = (P(None, ("groups", "wide")), P(None, ("groups", "wide")))
    return jax.shard_map(shards, mesh=mesh, in_specs=in_specs, out_specs=out_specs, check_vma=False)
```

```python
import functools
import math

import jax
import jax.numpy as jnp
import numpy as np
from jax import lax
from jax.experimental import pallas as pl
from jax.experimental.pallas import tpu as pltpu
from jax.sharding import PartitionSpec as P

MESH_X = 128
MESH_Y = 128
MESH_Z = 128
ORDER = 6


highest = lax.Precision.HIGHEST


def shifted(block, axis, distance):
    devices = range(lax.axis_size(axis))
    route = [((i - distance) % len(devices), i) for i in devices]
    return lax.ppermute(block, axis, route)


def spline_lists(offset, order_count):
    weights = [1.0 - offset, offset]
    slopes = [-jnp.ones_like(offset), jnp.ones_like(offset)]
    for degree in range(3, order_count + 1):
        if degree == order_count:
            slopes = (
                [-weights[0]]
                + [weights[position - 1] - weights[position] for position in range(1, degree - 1)]
                + [weights[degree - 2]]
            )
        factor = 1.0 / (degree - 1)
        updated = [None] * degree
        updated[degree - 1] = factor * offset * weights[degree - 2]
        for position in range(1, degree - 1):
            updated[degree - position - 1] = factor * (
                (offset + position) * weights[degree - position - 2]
                + (degree - position - offset) * weights[degree - position - 1]
            )
        updated[0] = factor * (1.0 - offset) * weights[0]
        weights = updated
    return (weights, slopes)


def spline_table(offset, order_count):
    weights, slopes = spline_lists(offset, order_count)
    return (jnp.stack(weights), jnp.stack(slopes))


def stencil_rows(weights, slopes, relative, extent, period):
    shifts = jnp.arange(weights.shape[0], dtype=jnp.int32)[None, :, None]
    targets = (relative[:, None, :] + shifts) % period
    points = jnp.arange(extent, dtype=jnp.int32)[None, :, None, None]
    matches = points == targets[:, None]
    plain_rows = jnp.sum(jnp.where(matches, jnp.moveaxis(weights, 0, 1)[:, None], 0.0), axis=2)
    slope_rows = jnp.sum(jnp.where(matches, jnp.moveaxis(slopes, 0, 1)[:, None], 0.0), axis=2)
    return (plain_rows, slope_rows)


def folded(points, length):
    values = jnp.where(points * 2 > length, points - length, points)
    return values.astype(jnp.float32) / length


def moduli(points, length):
    base_weights, base_slopes = spline_table(jnp.zeros((1,), jnp.float32), ORDER)
    shifts = jnp.arange(ORDER, dtype=jnp.int32)
    phases = points[:, None] * shifts[None, :] % length
    angles = phases.astype(jnp.float32) * (2.0 * math.pi / length)
    real_sum = jnp.sum(base_weights[:, 0][None, :] * jnp.cos(angles), axis=1)
    imag_sum = jnp.sum(base_weights[:, 0][None, :] * jnp.sin(angles), axis=1)
    return real_sum * real_sum + imag_sum * imag_sum


def kernel_table(widths, x_freq, y_freq, z_freq, x_mod, y_mod, z_mod):
    total = (
        x_freq[:, None, None, None] ** 2
        + y_freq[None, :, None, None] ** 2
        + z_freq[None, None, None, :] ** 2
    )
    positive = total > 0
    safe = jnp.where(positive, total, 1.0)
    beta = widths[None, None, :, None]
    divisor = x_mod[:, None, None, None] * y_mod[None, :, None, None] * z_mod[None, None, None, :]
    return jnp.where(
        positive,
        2.0 * jnp.exp(-math.pi**2 * total / (beta * beta)) / (math.pi * safe * divisor),
        0.0,
    )


def dft_tables(length):
    points = jnp.arange(length, dtype=jnp.int32)
    phases = points[:, None] * points[None, :] % length
    angles = phases.astype(jnp.float32) * (2.0 * math.pi / length)
    return (jnp.cos(angles), jnp.sin(angles))


def combine_blocks(block_grid, block_rows, border):
    owned = block_grid[:, :, :block_rows]
    overflow = jnp.roll(block_grid[:, :, block_rows:], 1, axis=0)
    owned = owned.at[:, :, :border].add(overflow)
    moved = jnp.moveaxis(owned, 0, 1)
    return moved.reshape((moved.shape[0], moved.shape[1] * moved.shape[2]) + moved.shape[3:])


def contract(data, x_weights, y_weights):
    return jnp.einsum("pycs,ps,ys->cs", data, x_weights, y_weights, precision=highest)


def turn(real_part, imag_part, cosines, sines, orient, pattern):

    def project(data, table):
        return jnp.einsum(pattern, data, table, precision=highest)

    real_out = project(real_part, cosines) - orient * project(imag_part, sines)
    imag_out = project(imag_part, cosines) + orient * project(real_part, sines)
    return jnp.stack([real_out, imag_out])


def slab_shards(charges, cell_offset, base_cell, counts, widths):
    wide_size = lax.axis_size("wide")
    device = lax.axis_index("wide")
    channels, slot_count = charges.shape
    blocks = counts.shape[0]
    capacity = slot_count // blocks
    planes = MESH_X // wide_size
    border = ORDER - 1
    extent = planes + border
    block_rows = MESH_Y // blocks
    y_extent = block_rows + border
    rounds = (border + planes - 1) // planes
    y_local = MESH_Y // wide_size
    live_mask = jnp.arange(capacity, dtype=jnp.int32)[None, :] < counts[:, None]
    charge_blocks = jnp.where(
        live_mask[:, None, :],
        jnp.moveaxis(charges.reshape(channels, blocks, capacity), 0, 1),
        jnp.zeros((), jnp.bfloat16),
    )
    offsets = cell_offset.reshape(3, blocks, capacity)
    bases = base_cell.reshape(3, blocks, capacity)
    x_weights, x_slopes = spline_table(offsets[0], ORDER)
    y_weights, y_slopes = spline_table(offsets[1], ORDER)
    z_weights, z_slopes = spline_table(offsets[2], ORDER)
    row_start = jnp.arange(blocks, dtype=jnp.int32)[:, None] * block_rows
    x_rows, x_drows = stencil_rows(x_weights, x_slopes, bases[0] - device * planes, extent, extent)
    y_rows, y_drows = stencil_rows(y_weights, y_slopes, bases[1] - row_start, y_extent, y_extent)
    z_plain, z_slope = stencil_rows(z_weights, z_slopes, bases[2], MESH_Z, MESH_Z)
    z_table = jnp.stack([z_plain, z_slope], axis=2).astype(jnp.bfloat16)

    def spread_block(inputs):
        x_block, y_block, charge_block, table_block = inputs
        products = (
            x_block[:, None, None, :]
            * y_block[None, :, None, :]
            * charge_block.astype(jnp.float32)[None, None]
        ).astype(jnp.bfloat16)
        spread = jnp.einsum(
            "rs,zs->rz",
            products.reshape(-1, capacity),
            table_block[:, 0],
            preferred_element_type=jnp.float32,
        )
        return spread.reshape(extent, y_extent, channels, MESH_Z)

    block_grid = lax.map(spread_block, (x_rows, y_rows, charge_blocks, z_table))
    grid_ext = combine_blocks(block_grid, block_rows, border)
    z_cos, z_sin = dft_tables(MESH_Z)
    y_cos, y_sin = dft_tables(MESH_Y)
    x_cos, x_sin = dft_tables(MESH_X)
    x_points = jnp.arange(MESH_X, dtype=jnp.int32)
    y_points = device * y_local + jnp.arange(y_local, dtype=jnp.int32)
    z_points = jnp.arange(MESH_Z, dtype=jnp.int32)
    kernel = kernel_table(
        widths,
        folded(x_points, MESH_X),
        folded(y_points, MESH_Y),
        folded(z_points, MESH_Z),
        moduli(x_points, MESH_X),
        moduli(y_points, MESH_Y),
        moduli(z_points, MESH_Z),
    )
    kernel = kernel / float(MESH_X * MESH_Y * MESH_Z)
    owned = grid_ext[:planes]
    for hop_index in range(1, rounds + 1):
        outgoing = grid_ext[hop_index * planes : (hop_index + 1) * planes]
        outgoing = jnp.pad(outgoing, ((0, planes - outgoing.shape[0]), (0, 0), (0, 0), (0, 0)))
        owned = owned + shifted(outgoing, "wide", hop_index)
    real_z = jnp.dot(owned, z_cos, precision=highest)
    imag_z = -jnp.dot(owned, z_sin, precision=highest)
    columns = lax.all_to_all(
        turn(real_z, imag_z, y_cos, y_sin, -1.0, "pycz,yk->pkcz"),
        "wide",
        split_axis=2,
        concat_axis=1,
        tiled=True,
    )
    spectrum = turn(columns[0], columns[1], x_cos, x_sin, -1.0, "xycz,xk->kycz")
    filtered = turn(spectrum[0] * kernel, spectrum[1] * kernel, x_cos, x_sin, 1.0, "xycz,xk->kycz")
    returned = lax.all_to_all(filtered, "wide", split_axis=1, concat_axis=2, tiled=True)
    along_y = turn(returned[0], returned[1], y_cos, y_sin, 1.0, "pycz,yk->pkcz")
    potential_own = (
        jnp.dot(along_y[0], z_cos, precision=highest)
        - jnp.dot(along_y[1], z_sin, precision=highest)
    ).astype(jnp.bfloat16)
    pieces = [potential_own]
    for hop_index in range(1, rounds + 1):
        pieces.append(shifted(potential_own, "wide", -hop_index))
    potential_ext = jnp.concatenate(pieces, axis=0)[:extent]
    blocked = potential_ext.reshape(extent, blocks, block_rows, channels, MESH_Z)
    following = jnp.roll(blocked[:, :, :border], -1, axis=1)
    windows = jnp.moveaxis(jnp.concatenate([blocked, following], axis=2), 1, 0)

    def gather_block(inputs):
        window, x_block, x_dblock, y_block, y_dblock, table_block, charge_block, live_block = inputs
        values = jnp.dot(
            window.reshape(-1, MESH_Z),
            table_block.reshape(MESH_Z, -1),
            preferred_element_type=jnp.float32,
        )
        values = values.reshape(extent, y_extent, channels, 2, capacity)
        direct = values[:, :, :, 0]
        sloped = values[:, :, :, 1]
        potential = jnp.where(live_block[None], contract(direct, x_block, y_block), 0.0)
        gradient = jnp.stack(
            [
                contract(direct, x_dblock, y_block),
                contract(direct, x_block, y_dblock),
                contract(sloped, x_block, y_block),
            ]
        )
        forces = -jnp.sum(gradient * charge_block.astype(jnp.float32)[None], axis=1)
        return (potential, forces)

    potentials, forces = lax.map(
        gather_block, (windows, x_rows, x_drows, y_rows, y_drows, z_table, charge_blocks, live_mask)
    )
    atom_potential = jnp.moveaxis(potentials, 0, 1).reshape(channels, slot_count)
    atom_forces = jnp.moveaxis(forces, 0, 1).reshape(3, slot_count)
    return (atom_potential, atom_forces)


def cas_terms(length):
    points = np.arange(length)
    angles = (points[:, None] * points[None, :] % length) * (2.0 * math.pi / length)
    left = (np.cos(angles) + np.sin(angles)).astype(np.float32)
    terms = []
    for _ in range(2):
        term = left.astype(jnp.bfloat16)
        terms.append(term)
        left = left - term.astype(np.float32)
    return terms


def split(values):
    first = values.astype(jnp.bfloat16)
    return first, (values - first.astype(jnp.float32)).astype(jnp.bfloat16)


def dot32(a, b, contract_b=0):
    return lax.dot_general(a, b, (((1,), (contract_b,)), ((), ())), preferred_element_type=jnp.float32)


def cas_lanes(values, right):
    sums = dot32(jnp.concatenate(split(values), axis=1), right)
    length = values.shape[1]
    return sums[:, :length] + sums[:, length:]


def cas_rows(values, left):
    sums = dot32(left, jnp.concatenate(split(values), axis=0))
    length = values.shape[0]
    return sums[:length] + sums[length:]


def level_of(largest):
    logarithm = jnp.log(jnp.maximum(largest, 1e-36)) * (1.0 / math.log(2.0))
    level = jnp.floor(logarithm + 1e-3).astype(jnp.int32) + 1 - 15 + 126
    return jnp.clip(level, 0, 250)


def power_of_two(level, sign):
    value = jnp.full(level.shape, 2.0 ** (-126 * sign), jnp.float32)
    for bit in range(7):
        value = value * jnp.where((level >> bit) & 1 > 0, 2.0 ** (sign * 2**bit), 1.0)
    return value * jnp.where((level >> 7) & 1 > 0, 2.0 ** (sign * 64), 1.0) * jnp.where((level >> 7) & 1 > 0, 2.0 ** (sign * 64), 1.0)


def channel_kernel(
    offset_ref, base_ref, charge_ref, far_offset_ref, far_ref, inverse_hbm, order_ref, widths_ref,
    right_hbm, left_hbm, out_ref,
    grid_ref, turned_ref, window_ref, spline_ref, place_ref, pair_ref, gain_ref, value_ref, charged_ref,
    inverse_ref, right_ref, left_ref, inverse_done, right_done, left_done,
):
    near, _, blocks, capacity = offset_ref.shape
    slabs = 2 * near
    planes = MESH_X // slabs
    rows = MESH_Y // blocks
    border = ORDER - 1
    frame = 16
    extent = planes + border
    far = MESH_X + border

    loads = [
        pltpu.make_async_copy(inverse_hbm, inverse_ref, inverse_done),
        pltpu.make_async_copy(right_hbm, right_ref, right_done),
        pltpu.make_async_copy(left_hbm, left_ref, left_done),
    ]
    for load in loads:
        load.start()

    def prepare(slab, offset_at, base_at, charge):
        span = pl.ds(pl.multiple_of(slab * blocks, blocks), blocks)
        charged_ref[slab] = charge.astype(jnp.float32)
        bases = [base_at(dimension).astype(jnp.float32).astype(jnp.int32) for dimension in range(3)]
        place_ref[0, span, :] = bases[0] & 7
        place_ref[1, span, :] = bases[1] & 7
        place_ref[2, span, :] = bases[2] & 7
        place_ref[3, span, :] = bases[2] >> 3
        for dimension in range(3):
            weights, slopes = spline_lists(offset_at(dimension), ORDER)
            for kind, values in enumerate((weights, slopes)):
                for position in range(8):
                    value = values[position] if position < ORDER else jnp.zeros_like(values[0])
                    for half in range(capacity // 128):
                        spline_ref[
                            2 * dimension + kind, half, pl.ds(slab * blocks * 8 + position, blocks, stride=8), :
                        ] = value[:, half * 128 : (half + 1) * 128]

    def prepare_both(index, carry):
        prepare(
            index,
            lambda dimension: offset_ref[index, dimension],
            lambda dimension: base_ref[index, dimension],
            charge_ref[index],
        )
        prepare(
            near + index,
            lambda dimension: far_offset_ref[index, dimension],
            lambda dimension: far_ref[3 * index + dimension],
            far_ref[3 * near + index],
        )
        return carry

    lax.fori_loop(0, near, prepare_both, 0, unroll=2)

    def clear(plane, carry):
        grid_ref[plane] = jnp.zeros(grid_ref.shape[1:], jnp.float32)
        return carry

    lax.fori_loop(0, far, clear, 0, unroll=19)
    points = lax.broadcasted_iota(jnp.int32, (8, capacity), 0)

    def row_of(dimension, block):
        return jnp.broadcast_to(place_ref[dimension, pl.ds(block, 1), :], (8, capacity))

    def cyclic_tables(dimension, block, kinds):
        base = row_of(dimension, block)
        index = (points - base) & 7
        span = pl.ds(pl.multiple_of(block * 8, 8), 8)
        tables = []
        for kind in kinds:
            values = jnp.concatenate(
                [spline_ref[2 * dimension + kind, half, span, :] for half in range(capacity // 128)], axis=1
            )
            tables.append(jnp.take_along_axis(values, index, axis=0, mode="promise_in_bounds"))
        return base, points >= base, tables

    def z_tables(block, kinds):
        unused, own, tables = cyclic_tables(2, block, kinds)
        tile = row_of(3, block)
        tile = jnp.where(own, tile, (tile + 1) & (MESH_Z // 8 - 1)).astype(jnp.float32)
        tile = jnp.concatenate([tile, tile - 1.0], axis=0).astype(jnp.bfloat16)
        here = [tile == jnp.bfloat16(2 * index) for index in range(MESH_Z // 16)]
        results = []
        for table in tables:
            twice = jnp.concatenate([table, table], axis=0).astype(jnp.bfloat16)
            results.append(
                jnp.concatenate([jnp.where(mask, twice, jnp.zeros_like(twice)) for mask in here], axis=0)
            )
        return results

    def spread(turn_index, block):
        place = turn_index * blocks + block
        slab = order_ref[turn_index]
        x_base, unused, (x_table,) = cyclic_tables(0, place, (0,))
        unused, y_own, (y_table,) = cyclic_tables(1, place, (0,))
        (z_table,) = z_tables(place, (0,))
        charge = jnp.broadcast_to(charged_ref[turn_index, pl.ds(block, 1), :], (8, capacity))
        x_place = jnp.concatenate([x_base, x_base], axis=0).astype(jnp.float32).astype(jnp.bfloat16)
        low, high = [], []
        for index in range(planes):
            product = (x_table[index : index + 1] * y_table) * charge
            pair = jnp.concatenate(
                [jnp.where(y_own, product, 0.0), jnp.where(y_own, 0.0, product)], axis=0
            ).astype(jnp.bfloat16)
            if index < border:
                own = x_place <= jnp.bfloat16(index)
                low.append(jnp.where(own, pair, jnp.zeros_like(pair)))
                high.append(jnp.where(own, jnp.zeros_like(pair), pair))
            else:
                low.append(pair)
        sums = dot32(jnp.concatenate(low + high, axis=0), z_table, 1)
        row_span = pl.ds(pl.multiple_of(block * rows, rows), frame)
        for index in range(extent):
            grid_ref[slab * planes + index, row_span, :] += sums[index * frame : (index + 1) * frame]

    def spread_step(step, carry):
        spread(step // blocks, step % blocks)
        return carry

    lax.fori_loop(0, slabs * blocks, spread_step, 0, unroll=64)

    for index in range(border):
        grid_ref[index] += grid_ref[MESH_X + index]

    for load in loads:
        load.wait()
    right, left = right_ref[...], left_ref[...]
    width = widths_ref[order_ref[0]]

    def squares(dimension):
        index = lax.broadcasted_iota(jnp.int32, (MESH_X, MESH_Z), dimension)
        index = jnp.where(index * 2 > MESH_X, index - MESH_X, index).astype(jnp.float32) / MESH_X
        return index * index

    across, along = squares(0), squares(1)
    decay = -(math.pi**2) / (width * width)
    gain_ref[...] = jnp.exp(decay * across) * inverse_ref[0]
    scale = 2.0 / (math.pi * MESH_X * MESH_Y * MESH_Z)
    pair_ref[0] = gain_ref[...] * (jnp.exp(decay * along) * (inverse_ref[1] * scale))
    pair_ref[1] = across + along

    def forward(step, carry):
        both = []
        for index in range(2):
            plane = 2 * step + index
            both.append(grid_ref[plane, 0:8, :] + grid_ref[plane, MESH_Y : MESH_Y + 8, :])
            both.append(grid_ref[plane, 8:MESH_Y, :])
        along_z = cas_lanes(jnp.concatenate(both, axis=0), right)
        along_y = cas_rows(
            jnp.concatenate([along_z[:MESH_Y], along_z[MESH_Y:]], axis=1), left
        )
        for index in range(2):
            turned_ref[pl.ds(2 * step + index, MESH_Y, stride=MESH_X), :] = along_y[
                :, index * MESH_Z : (index + 1) * MESH_Z
            ]
        return carry

    lax.fori_loop(0, MESH_X // 2, forward, 0, unroll=64)

    def filtering(step, carry):
        spans = [pl.ds(pl.multiple_of((2 * step + index) * MESH_X, MESH_X), MESH_X) for index in range(2)]
        lines = jnp.concatenate([turned_ref[span, :] for span in spans], axis=1)
        spectrum = cas_rows(lines, left)
        filters = []
        for index in range(2):
            row = 2 * step + index
            frequency = jnp.where(row * 2 > MESH_Y, row - MESH_Y, row).astype(jnp.float32) / MESH_Y
            total = pair_ref[1] + frequency * frequency
            positive = total > 0
            safe = jnp.where(positive, total, 1.0)
            filters.append(jnp.where(positive, pair_ref[0] * gain_ref[pl.ds(row, 1), :] / safe, 0.0))
        lines = cas_rows(spectrum * jnp.concatenate(filters, axis=1), left)
        for index, span in enumerate(spans):
            turned_ref[span, :] = lines[:, index * MESH_Z : (index + 1) * MESH_Z]
        return carry

    lax.fori_loop(0, MESH_Y // 2, filtering, 0, unroll=64)

    def backward(step, carry):
        both = jnp.concatenate(
            [turned_ref[pl.ds(2 * step + index, MESH_Y, stride=MESH_X), :] for index in range(2)], axis=1
        )
        along_y = cas_rows(both, left)
        field = cas_lanes(
            jnp.concatenate([along_y[:, :MESH_Z], along_y[:, MESH_Z:]], axis=0), right
        )
        for index in range(2):
            plane = field[index * MESH_Y : (index + 1) * MESH_Y]
            plane = jnp.concatenate([plane, plane[:8]], axis=0)
            for block in range(blocks):
                window_ref[2 * step + index, block] = plane[block * rows : block * rows + frame].astype(jnp.bfloat16)
        return carry

    lax.fori_loop(0, MESH_X // 2, backward, 0, unroll=64)

    for index in range(border):
        window_ref[MESH_X + index] = window_ref[index]

    def gather(turn_index, block):
        place = turn_index * blocks + block
        slab = order_ref[turn_index]
        x_base, unused, (x_table, x_slope) = cyclic_tables(0, place, (0, 1))
        unused, y_own, (y_table, y_slope) = cyclic_tables(1, place, (0, 1))
        z_table, z_slope = z_tables(place, (0, 1))
        charge = charged_ref[turn_index, pl.ds(block, 1), :]
        window = jnp.concatenate(
            [window_ref[slab * planes + index, block] for index in range(extent)], axis=0
        )

        def chosen(near, index, own):
            def rows_of(plane):
                return jnp.where(
                    y_own, near[plane * frame : plane * frame + 8], near[plane * frame + 8 : plane * frame + 16]
                )

            if index < border:
                return jnp.where(own, rows_of(index), rows_of(planes + index))
            return rows_of(index)

        both = dot32(window, jnp.concatenate([z_table, z_slope], axis=1))
        near, near_z = both[:, :capacity], both[:, capacity:]
        plain = sloped = plain_z = 0.0
        for index in range(planes):
            own = x_base <= index
            part = chosen(near, index, own)
            plain += x_table[index : index + 1] * part
            sloped += x_slope[index : index + 1] * part
            plain_z += x_table[index : index + 1] * chosen(near_z, index, own)
        row = pl.ds(block, 1)
        value_ref[slab, 0, row, :] = jnp.sum(y_table * plain, axis=0, keepdims=True)
        value_ref[slab, 1, row, :] = -charge * jnp.sum(y_table * sloped, axis=0, keepdims=True)
        value_ref[slab, 2, row, :] = -charge * jnp.sum(y_slope * plain, axis=0, keepdims=True)
        value_ref[slab, 3, row, :] = -charge * jnp.sum(y_table * plain_z, axis=0, keepdims=True)

    def gather_step(step, carry):
        gather(step // blocks, step % blocks)
        return carry

    lax.fori_loop(0, slabs * blocks, gather_step, 0, unroll=64)
    halves = capacity // 128
    lines = lax.broadcasted_iota(jnp.int32, (4 * halves, 128), 0)
    shift = 1.5 * 2.0**23

    def encode(slab, carry):
        pieces = [
            value_ref[slab, kind, :, half * 128 : (half + 1) * 128] for kind in range(4) for half in range(halves)
        ]
        largest = jnp.zeros((4 * halves, 128), jnp.float32)
        for line, piece in enumerate(pieces):
            largest = jnp.where(lines == line, jnp.max(jnp.abs(piece), axis=0, keepdims=True), largest)
        level = level_of(largest)
        inverse_scale = power_of_two(level, -1)
        for line, piece in enumerate(pieces):
            codes = (piece * inverse_scale[line : line + 1] + shift) - shift
            out_ref[slab, pl.ds(line * blocks, blocks), :] = codes.astype(jnp.int32).astype(jnp.int16)
        rest = jnp.zeros((blocks - 4 * halves, 128), jnp.int32)
        out_ref[slab, pl.ds(4 * halves * blocks, blocks), :] = jnp.concatenate([level, rest], axis=0).astype(jnp.int16)
        return carry

    lax.fori_loop(0, slabs, encode, 0, unroll=16)


def channel_shards(charges, cell_offset, base_cell, counts, widths):
    device = lax.axis_index("wide")
    channels, slot_count = charges.shape
    blocks = counts.shape[0]
    capacity = slot_count // blocks
    slabs = lax.axis_size("wide")
    live_mask = jnp.arange(capacity, dtype=jnp.int32)[None, :] < counts[:, None]
    charge_blocks = jnp.where(
        live_mask[None], charges.reshape(channels, blocks, capacity), jnp.zeros((), jnp.bfloat16)
    )
    cells = base_cell.astype(jnp.bfloat16).reshape(1, 3, blocks, capacity)
    offsets = cell_offset.reshape(1, 3, blocks, capacity)
    parts = charge_blocks[None]
    order = jnp.zeros((1,), jnp.int32)
    distance = slabs // 2
    ahead = 2
    ahead_route = [(index, index ^ ahead) for index in range(slabs)]
    early_offsets = lax.ppermute(offsets, "wide", ahead_route)
    early_cells = lax.ppermute(cells, "wide", ahead_route)
    while distance > 0:
        route = [(index, index ^ distance) for index in range(slabs)]
        known = 1 if distance == ahead else 0
        upper = (device & distance) > 0
        first, second = parts[:, :distance], parts[:, distance:]
        kept, sent = jnp.where(upper, second, first), jnp.where(upper, first, second)
        count = cells.shape[0]
        bundle = jnp.concatenate([cells[known:].reshape((-1,) + cells.shape[2:]), sent.reshape((-1,) + sent.shape[2:])], axis=0)
        arrived = lax.ppermute(offsets[known:], "wide", route)
        bundle = lax.ppermute(bundle, "wide", route)
        order = jnp.concatenate([order, order ^ distance])
        if distance > 1:
            offsets = jnp.concatenate([offsets, early_offsets, arrived] if known else [offsets, arrived], axis=0)
            fresh = bundle[: 3 * (count - known)].reshape((-1,) + cells.shape[1:])
            cells = jnp.concatenate([cells, early_cells, fresh] if known else [cells, fresh], axis=0)
            parts = jnp.concatenate([kept, bundle[3 * (count - known) :].reshape(kept.shape)], axis=0)
        distance //= 2
    order = order ^ device

    points = np.arange(MESH_X)
    first = np.array([1.0, 26.0, 66.0, 26.0, 1.0, 0.0]) / 120.0
    angles = 2.0 * math.pi * points[:, None] * np.arange(ORDER)[None, :] / MESH_X
    inverse = (1.0 / ((np.cos(angles) @ first) ** 2 + (np.sin(angles) @ first) ** 2)).astype(np.float32)
    inverse = np.stack([np.repeat(inverse[:, None], MESH_Z, axis=1), np.repeat(inverse[None], MESH_X, axis=0)])
    one, two = cas_terms(MESH_X)
    right = np.concatenate([np.concatenate([one, two], axis=1)] * 2, axis=0)
    left = np.concatenate([np.concatenate([one, one], axis=1), np.concatenate([two, two], axis=1)], axis=0)

    halves = capacity // 128
    whole = pl.BlockSpec(memory_space=pltpu.VMEM)
    away = pl.BlockSpec(memory_space=pltpu.HBM)
    scalars = pl.BlockSpec(memory_space=pltpu.SMEM)
    result = pl.pallas_call(
        channel_kernel,
        out_shape=jax.ShapeDtypeStruct((slabs, (4 * halves + 1) * blocks, 128), jnp.int16),
        in_specs=[whole] * 5 + [away] + [scalars] * 2 + [away] * 2,
        out_specs=whole,
        scratch_shapes=[
            pltpu.VMEM((MESH_X + ORDER - 1, MESH_Y + 8, MESH_Z), jnp.float32),
            pltpu.VMEM((MESH_X * MESH_Y + MESH_X, MESH_Z), jnp.float32),
            pltpu.VMEM((MESH_X + ORDER - 1, blocks, 16, MESH_Z), jnp.bfloat16),
            pltpu.VMEM((6, capacity // 128, slabs * blocks * 8 + 8, 128), jnp.float32),
            pltpu.VMEM((4, slabs * blocks, capacity), jnp.int32),
            pltpu.VMEM((2, MESH_X, MESH_Z), jnp.float32),
            pltpu.VMEM((MESH_Y, MESH_Z), jnp.float32),
            pltpu.VMEM((slabs, 4, blocks, capacity), jnp.float32),
            pltpu.VMEM((slabs, blocks, capacity), jnp.float32),
            pltpu.VMEM(inverse.shape, jnp.float32),
            pltpu.VMEM(right.shape, jnp.bfloat16),
            pltpu.VMEM(left.shape, jnp.bfloat16),
            pltpu.SemaphoreType.DMA,
            pltpu.SemaphoreType.DMA,
            pltpu.SemaphoreType.DMA,
        ],
        compiler_params=pltpu.CompilerParams(vmem_limit_bytes=52 * 1024 * 1024),
        name="channel",
    )(
        offsets, cells, kept[:, 0], arrived, bundle, jnp.asarray(inverse), order, widths,
        jnp.asarray(right), jnp.asarray(left),
    )
    returned = lax.all_to_all(result, "wide", split_axis=0, concat_axis=0, tiled=True)
    codes = returned[:, : 4 * halves * blocks].reshape(channels, 4, halves, blocks, 128)
    levels = returned[:, 4 * halves * blocks : 4 * halves * blocks + 4 * halves].astype(jnp.int32)
    scales = power_of_two(levels, 1).reshape(channels, 4, halves, 1, 128)
    values = codes.astype(jnp.float32) * scales
    potential = jnp.moveaxis(values[:, 0], 1, 2).reshape(channels, blocks, capacity)
    atom_potential = jnp.where(live_mask[None], potential, 0.0).reshape(channels, slot_count)
    forces = jnp.moveaxis(jnp.sum(values[:, 1:], axis=0), 1, 2).reshape(3, slot_count)
    return (atom_potential, forces)


def shards(charges, cell_offset, base_cell, counts, widths):
    if lax.axis_size("wide") == charges.shape[0] and MESH_X == 8 * lax.axis_size("wide"):
        return channel_shards(charges, cell_offset, base_cell, counts, widths)
    return slab_shards(charges, cell_offset, base_cell, counts, widths)


def solution(mesh):
    in_specs = (
        P(None, ("groups", "wide")),
        P(None, ("groups", "wide")),
        P(None, ("groups", "wide")),
        P(("groups", "wide")),
        P(),
    )
    out_specs = (P(None, ("groups", "wide")), P(None, ("groups", "wide")))
    return jax.shard_map(shards, mesh=mesh, in_specs=in_specs, out_specs=out_specs, check_vma=False)
```
